32 devices in a mesh: dp: 8 (over z, x), row: 4 (over y, core).
Axes of the slice: x: 2, y: 2, z: 4, core: 2. Of those that a mesh axis runs over, the one named last changes fastest.
Arguments:
- image: bfloat16 [2, 64, 28, 28, 256], P(None, 'dp', 'row'), may hold values from -6 to 6
- tags: bfloat16 [2, 64, 128, 512], P(None, ('dp', 'row')), may hold values from -6 to 6
- tag_lengths: int32 [2, 64], P(None, ('dp', 'row')), may hold values from 40 to 128, as said below
- cotangent: bfloat16 [2, 64, 128, 512], P(None, ('dp', 'row')), may hold values from -6 to 6
- conv_weight: bfloat16 [2, 3, 3, 256, 256], replicated, may hold values from -0.125 to 0.125
- bn_mean: float32 [2, 256], replicated, may hold values from -3 to 3
- bn_var: float32 [2, 256], replicated, may hold values from 0.25 to 4
- bn_scale: float32 [2, 256], replicated, may hold values from 0.25 to 1.75
- bn_shift: float32 [2, 256], replicated, may hold values from -3 to 3
- proj_weight: bfloat16 [256, 512], replicated, may hold values from -0.375 to 0.375
- proj_bias: float32 [512], replicated, may hold values from -3 to 3
- attn_in: bfloat16 [6, 512, 512], replicated, may hold values from -0.25 to 0.25
- attn_out: bfloat16 [2, 512, 512], replicated, may hold values from -1 to 1
- ln_gain: float32 [3, 512], replicated, may hold values from 0.25 to 1.75
- ln_bias: float32 [3, 512], replicated, may hold values from -3 to 3
- ffn_in: bfloat16 [512, 1024], replicated, may hold values from -0.25 to 0.25
- ffn_in_bias: float32 [1024], replicated, may hold values from -3 to 3
- ffn_out: bfloat16 [1024, 512], replicated, may hold values from -0.1875 to 0.1875
- ffn_out_bias: float32 [512], replicated, may hold values from -3 to 3
Outputs:
- decoded: bfloat16 [2, 64, 128, 512], P(None, ('dp', 'row'))
- image_grad: float32 [2, 64, 28, 28, 256], P(None, 'dp', 'row')
- tags_grad: float32 [2, 64, 128, 512], P(None, ('dp', 'row'))
- conv_grad: float32 [2, 3, 3, 256, 256], replicated
- bn_scale_grad: float32 [2, 256], replicated
- bn_shift_grad: float32 [2, 256], replicated
- proj_grad: float32 [256, 512], replicated
- proj_bias_grad: float32 [512], replicated
- attn_in_grad: float32 [6, 512, 512], replicated
- attn_out_grad: float32 [2, 512, 512], replicated
- ln_gain_grad: float32 [3, 512], replicated
- ln_bias_grad: float32 [3, 512], replicated
- ffn_in_grad: float32 [512, 1024], replicated
- ffn_in_bias_grad: float32 [1024], replicated
- ffn_out_grad: float32 [1024, 512], replicated
- ffn_out_bias_grad: float32 [512], replicated
The draws below stay inside these ranges and needn't reach their ends.
Inputs may be any that keep to these rules, and one draw needn't show every extreme that they name: `tag_lengths`: slot j of a table holds a tag when j is below its count; in every micro-batch some table has exactly 128.
All inputs are finite; a program needn't handle non-finite values.
Results may differ from the reference program's by a relative error of at most 0.023.
Values may be sent and summed in bfloat16 or wider, within the bound.
A program may use at most 256 MiB of HBM per device.

```python
import math
import jax
import jax.numpy as jnp
from jax import lax

C = 256
D = 512
HEADS = 8
FF = 1024
HIMG = 28
WIMG = 28
L = 128
MB = 2
GRP = 8
TABLES = 64


def draw_tag_lengths(key, part):
    key = jax.random.fold_in(key, 7)
    first_key, second_key = jax.random.split(key)
    counts = jax.random.randint(first_key, (MB, TABLES), L * 5 // 16, L + 1)
    chosen = jax.random.randint(second_key, (MB, 1), 0, TABLES)
    return jnp.where(jnp.arange(TABLES)[None, :] == chosen, L, counts).astype(jnp.int32)


def shard_levels(stream_key, shape, cuts, low, high):
    def one(dim, blocks):
        steps = jax.random.uniform(jax.random.fold_in(jax.random.fold_in(stream_key, 6), dim), (blocks,), jnp.float32, low / len(cuts), high / len(cuts))
        return jnp.repeat(jnp.exp(steps), shape[dim] // blocks).reshape((-1,) + (1,) * (len(shape) - dim - 1))

    loudness = one(*cuts[0])
    for cut in cuts[1:]:
        loudness = loudness * one(*cut)
    return loudness


def centred(own_key, extent, width, bound, cuts=(), held_as=jnp.bfloat16):
    entries = jax.random.normal(own_key, extent, jnp.float32) * width
    if len(cuts) > 0:
        entries = shard_levels(own_key, extent, cuts, -0.22, 0.18) * entries
    return jnp.clip(entries, min=-bound, max=bound).astype(held_as)


def setup_inputs(seed: int = 0) -> dict:
    key_list = jax.random.split(jax.random.key(seed), 20)
    return {
        "image": centred(key_list[0], (MB, TABLES, HIMG, WIMG, C), 1.0, 6.0, ((1, 8), (2, 4))),
        "tags": centred(key_list[1], (MB, TABLES, L, D), 1.0, 6.0, ((1, 32),)),
        "tag_lengths": draw_tag_lengths(jax.random.fold_in(key_list[19], 71), 0),
        "cotangent": centred(key_list[3], (MB, TABLES, L, D), 1.0, 6.0, ((1, 32),)),
        "conv_weight": centred(key_list[4], (2, 3, 3, C, C), (9 * C) ** -0.5, 0.125),
        "bn_mean": centred(key_list[5], (2, C), 0.5, 3.0, (), jnp.float32),
        "bn_var": jnp.clip(jnp.exp(jax.random.uniform(key_list[6], (2, C), jnp.float32, math.log(0.25), math.log(4.0))), 0.25, 4.0),
        "bn_scale": jnp.clip(1.0 + 0.15 * jax.random.normal(key_list[7], (2, C), jnp.float32), 0.25, 1.75),
        "bn_shift": centred(key_list[8], (2, C), 0.5, 3.0, (), jnp.float32),
        "proj_weight": centred(key_list[9], (C, D), C ** -0.5, 0.375),
        "proj_bias": centred(key_list[10], (D,), 0.5, 3.0, (), jnp.float32),
        "attn_in": centred(key_list[11], (6, D, D), D ** -0.5, 0.25),
        "attn_out": centred(key_list[12], (2, D, D), (D // 16) ** -0.5, 1.0),
        "ln_gain": jnp.clip(1.0 + 0.15 * jax.random.normal(key_list[13], (3, D), jnp.float32), 0.25, 1.75),
        "ln_bias": centred(key_list[14], (3, D), 0.5, 3.0, (), jnp.float32),
        "ffn_in": centred(key_list[15], (D, FF), D ** -0.5, 0.25),
        "ffn_in_bias": centred(key_list[16], (FF,), 0.5, 3.0, (), jnp.float32),
        "ffn_out": centred(key_list[17], (FF, D), FF ** -0.5, 0.1875),
        "ffn_out_bias": centred(key_list[18], (D,), 0.5, 3.0, (), jnp.float32),
    }


EPS = 1e-05
MASKED = -1e+30
PRECISE = lax.Precision.HIGHEST

@jax.custom_vjp
def low(v):
    return lax.optimization_barrier(v.astype(jnp.bfloat16)).astype(jnp.float32)

@jax.custom_vjp
def low_back(v):
    return v

def low_keep(v):
    return (low(v), None)

def low_pass(kept, grad):
    return (grad,)

def back_keep(v):
    return (v, None)

def back_low(kept, grad):
    return (low(grad),)
low.defvjp(low_keep, low_pass)
low_back.defvjp(back_keep, back_low)

def product(form, left, right):
    return jnp.einsum(form, left, right, precision=PRECISE)

def layer_norm(inputs, scaling, offset):
    center = inputs - lax.optimization_barrier(jnp.mean(inputs, -1, keepdims=True))
    spread = lax.optimization_barrier(jnp.mean(center * center, -1, keepdims=True))
    return center * lax.rsqrt(spread + EPS) * scaling + offset

def smooth(inputs):
    return jax.nn.gelu(inputs, approximate=False)

def softmax_rows(scores):
    highest = lax.optimization_barrier(jnp.max(scores, -1, keepdims=True))
    raised = jnp.exp(scores - highest)
    return raised / lax.optimization_barrier(jnp.sum(raised, -1, keepdims=True))

def conv_same(inputs, kernel):
    height = inputs.shape[1]
    breadth = inputs.shape[2]
    padded = jnp.pad(inputs, ((0, 0), (1, 1), (1, 1), (0, 0)))
    summed = jnp.zeros(inputs.shape[:3] + (kernel.shape[-1],), jnp.float32)
    for step_a in range(3):
        for step_b in range(3):
            window = padded[:, step_a:step_a + height, step_b:step_b + breadth, :]
            summed = summed + product('bhwc,cd->bhwd', window, kernel[step_a, step_b])
    return summed

def head_view(matrix):
    return matrix.reshape(matrix.shape[0], matrix.shape[1], HEADS, matrix.shape[2] // HEADS)

def attend(queries, keys_in, values_in, allowed, scale):
    scores = low_back(product('bqhe,bkhe->bhqk', head_view(queries), head_view(keys_in)) * scale)
    if allowed is not None:
        scores = jnp.where(allowed, scores, MASKED)
    shares = low(softmax_rows(scores))
    mixed = product('bhqk,bkhe->bqhe', shares, head_view(values_in))
    return low(low_back(mixed.reshape(queries.shape)))

def block_forward(params, stat_mean, stat_var, images, tag_block, lengths):
    conv_w, scale_bn, shift_bn, proj_w, proj_b, attn_i, attn_o, gains, shifts, ffn_i, ffn_ib, ffn_o, ffn_ob = params
    factor = lax.rsqrt(stat_var + EPS)
    pre_one = low_back(conv_same(images, conv_w[0]))
    hidden = low(smooth((pre_one - stat_mean[0]) * factor[0] * scale_bn[0] + shift_bn[0]))
    pre_two = low_back(conv_same(hidden, conv_w[1]))
    block_out = low(smooth((pre_two - stat_mean[1]) * factor[1] * scale_bn[1] + shift_bn[1] + images))
    tokens = low(low_back(product('bhwc,cd->bhwd', block_out, proj_w) + proj_b))
    memory = tokens.reshape(tokens.shape[0], -1, tokens.shape[-1])
    slots = tag_block.shape[1]
    position = jnp.arange(slots)
    causal = (position[None, :] <= position[:, None])[None, None]
    allowed = causal & (position[None, :] < lengths[:, None])[:, None, None, :]
    scale = 1.0 / math.sqrt(tag_block.shape[-1] // HEADS)
    projected = low(low_back(product('bld,jde->jble', tag_block, attn_i[:3])))
    self_mix = attend(projected[0], projected[1], projected[2], allowed, scale)
    first_in = tag_block + low_back(product('bld,de->ble', self_mix, attn_o[0]))
    first = layer_norm(first_in, gains[0], shifts[0])
    cross_q = low(low_back(product('bld,de->ble', low(first), attn_i[3])))
    cross_kv = low(low_back(product('bid,jde->jbie', memory, attn_i[4:6])))
    cross_mix = attend(cross_q, cross_kv[0], cross_kv[1], None, scale)
    second_in = first + low_back(product('bld,de->ble', cross_mix, attn_o[1]))
    second = layer_norm(second_in, gains[1], shifts[1])
    inner = low_back(product('bld,df->blf', low(second), ffn_i) + ffn_ib)
    outer = low_back(product('blf,fd->bld', low(smooth(inner)), ffn_o) + ffn_ob)
    return layer_norm(second + outer, gains[2], shifts[2])

def reference(image, tags, tag_lengths, cotangent, conv_weight, bn_mean, bn_var, bn_scale, bn_shift, proj_weight, proj_bias, attn_in, attn_out, ln_gain, ln_bias, ffn_in, ffn_in_bias, ffn_out, ffn_out_bias):
    blocks = MB * TABLES // GRP
    images = image.astype(jnp.float32).reshape(blocks, GRP, HIMG, WIMG, C)
    tag_blocks = tags.astype(jnp.float32).reshape(blocks, GRP, L, D)
    length_blocks = tag_lengths.reshape(blocks, GRP)
    stat_mean = bn_mean.astype(jnp.float32)
    stat_var = bn_var.astype(jnp.float32)
    params = (conv_weight.astype(jnp.float32), bn_scale.astype(jnp.float32), bn_shift.astype(jnp.float32), proj_weight.astype(jnp.float32), proj_bias.astype(jnp.float32), attn_in.astype(jnp.float32), attn_out.astype(jnp.float32), ln_gain.astype(jnp.float32), ln_bias.astype(jnp.float32), ffn_in.astype(jnp.float32), ffn_in_bias.astype(jnp.float32), ffn_out.astype(jnp.float32), ffn_out_bias.astype(jnp.float32))

    def forward(weights, image_all, tag_all):

        def one_block(pieces):
            return block_forward(weights, stat_mean, stat_var, pieces[0], pieces[1], pieces[2])
        return lax.map(jax.checkpoint(one_block), (image_all, tag_all, length_blocks))
    result, pullback = jax.vjp(forward, params, images, tag_blocks)
    grad_params, grad_images, grad_tags = pullback(cotangent.astype(jnp.float32).reshape(blocks, GRP, L, D))
    decoded = result.reshape(MB, TABLES, L, D).astype(jnp.bfloat16)
    return (decoded, grad_images.reshape(MB, TABLES, HIMG, WIMG, C), grad_tags.reshape(MB, TABLES, L, D), grad_params[0], grad_params[1], grad_params[2], grad_params[3], grad_params[4], grad_params[5], grad_params[6], grad_params[7], grad_params[8], grad_params[9], grad_params[10], grad_params[11], grad_params[12])
```

```python
import math

import jax
import jax.numpy as jnp
from jax import lax
from jax.sharding import PartitionSpec as P

HEADS = 8


EPS = 1e-05
MASKED = -1e30


def layer_norm(inputs, scaling, offset):
    center = inputs - jnp.mean(inputs, -1, keepdims=True)
    spread = jnp.mean(center * center, -1, keepdims=True)
    return center * lax.rsqrt(spread + EPS) * scaling + offset


def smooth(inputs):
    return jax.nn.gelu(inputs, approximate=False)


def smooth_grad(inputs, upstream):
    return jax.vjp(smooth, inputs)[1](upstream)[0]


def norm_grad(inputs, scaling, offset, upstream):
    pullback = jax.vjp(layer_norm, inputs, scaling, offset)[1]
    return pullback(upstream)


def conv_fwd(inputs, kernel):
    return lax.conv_general_dilated(
        inputs, kernel, (1, 1), ((1, 1), (1, 1)),
        dimension_numbers=("NHWC", "HWIO", "NHWC"), preferred_element_type=jnp.float32,
    )


def conv_back(upstream, kernel):
    return lax.conv_general_dilated(
        upstream, kernel[::-1, ::-1], (1, 1), ((1, 1), (1, 1)),
        dimension_numbers=("NHWC", "HWOI", "NHWC"), preferred_element_type=jnp.float32,
    )


def kernel_grad(inputs, upstream):
    return lax.conv_general_dilated(
        inputs, upstream, (1, 1), ((1, 1), (1, 1)),
        dimension_numbers=("CHWN", "IHWO", "HWNC"), preferred_element_type=jnp.float32,
    )

def head_view(matrix):
    return matrix.reshape(matrix.shape[0], matrix.shape[1], HEADS, matrix.shape[2] // HEADS)


def scores_of(queries, keys_in, allowed, scale):
    scores = (
        jnp.einsum(
            "oqhe,okhe->ohqk",
            head_view(queries),
            head_view(keys_in),
            preferred_element_type=jnp.float32,
        )
        * scale
    )
    if allowed is None:
        return scores
    return jnp.where(allowed, scores, MASKED)


def attend(queries, keys_in, values_in, allowed, scale):
    scores = scores_of(queries, keys_in, allowed, scale)
    highest = jnp.max(scores, -1, keepdims=True)
    raised = jnp.exp(scores - highest)
    totals = jnp.sum(raised, -1, keepdims=True)
    shares = raised / totals
    logsum = highest + jnp.log(totals)
    mixed = jnp.einsum(
        "ohqk,okhe->oqhe",
        shares.astype(jnp.bfloat16),
        head_view(values_in),
        preferred_element_type=jnp.float32,
    )
    return (mixed.reshape(queries.shape).astype(jnp.bfloat16), logsum)


def attend_back(queries, keys_in, values_in, allowed, scale, logsum, upstream):
    scores = scores_of(queries, keys_in, allowed, scale)
    shares = jnp.exp(scores - logsum)
    up_heads = head_view(upstream)
    grad_shares = jnp.einsum(
        "oqhe,okhe->ohqk", up_heads, head_view(values_in), preferred_element_type=jnp.float32
    )
    grad_scores = (
        shares * (grad_shares - jnp.sum(grad_shares * shares, -1, keepdims=True))
    ).astype(jnp.bfloat16)
    grad_query = (
        jnp.einsum(
            "ohqk,okhe->oqhe", grad_scores, head_view(keys_in), preferred_element_type=jnp.float32
        )
        * scale
    )
    grad_key = (
        jnp.einsum(
            "ohqk,oqhe->okhe", grad_scores, head_view(queries), preferred_element_type=jnp.float32
        )
        * scale
    )
    grad_value = jnp.einsum(
        "ohqk,oqhe->okhe", shares.astype(jnp.bfloat16), up_heads, preferred_element_type=jnp.float32
    )
    return (
        grad_query.reshape(queries.shape),
        grad_key.reshape(keys_in.shape),
        grad_value.reshape(values_in.shape),
    )


def body(
    image,
    tags,
    tag_lengths,
    cotangent,
    conv_weight,
    bn_mean,
    bn_var,
    bn_scale,
    bn_shift,
    proj_weight,
    proj_bias,
    attn_in,
    attn_out,
    ln_gain,
    ln_bias,
    ffn_in,
    ffn_in_bias,
    ffn_out,
    ffn_out_bias,
):
    batches = image.shape[0]
    owned = tags.shape[1]
    slots = tags.shape[2]
    scale = 1.0 / math.sqrt(tags.shape[3] // HEADS)
    factor = lax.rsqrt(bn_var + EPS)
    position = jnp.arange(slots)
    causal = (position[None, :] <= position[:, None])[None, None]
    tables = batches * owned
    moved = lax.all_to_all(image, "row", 1, 2, tiled=True)
    inputs = moved.reshape((tables,) + moved.shape[2:])
    pre_one = conv_fwd(inputs, conv_weight[0])
    norm_one = (pre_one - bn_mean[0]) * factor[0]
    act_one = norm_one * bn_scale[0] + bn_shift[0]
    hidden = smooth(act_one).astype(jnp.bfloat16)
    pre_two = conv_fwd(hidden, conv_weight[1])
    norm_two = (pre_two - bn_mean[1]) * factor[1]
    act_two = norm_two * bn_scale[1] + bn_shift[1] + inputs.astype(jnp.float32)
    block_out = smooth(act_two).astype(jnp.bfloat16)
    tokens = (
        jnp.einsum("grwc,cd->grwd", block_out, proj_weight, preferred_element_type=jnp.float32)
        + proj_bias
    ).astype(jnp.bfloat16)
    memory = tokens.reshape(tables, -1, tokens.shape[-1])
    start = tags.reshape((tables,) + tags.shape[2:])
    lengths = tag_lengths.reshape(-1)
    allowed = causal & (position[None, :] < lengths[:, None])[:, None, None, :]
    projected = jnp.einsum(
        "old,jde->jole", start, attn_in[:3], preferred_element_type=jnp.float32
    ).astype(jnp.bfloat16)
    self_mix, self_log = attend(projected[0], projected[1], projected[2], allowed, scale)
    first_in = start.astype(jnp.float32) + jnp.einsum(
        "old,de->ole", self_mix, attn_out[0], preferred_element_type=jnp.float32
    )
    first = layer_norm(first_in, ln_gain[0], ln_bias[0])
    first_b = first.astype(jnp.bfloat16)
    cross_q = jnp.einsum(
        "old,de->ole", first_b, attn_in[3], preferred_element_type=jnp.float32
    ).astype(jnp.bfloat16)
    cross_kv = jnp.einsum(
        "oid,jde->joie", memory, attn_in[4:6], preferred_element_type=jnp.float32
    ).astype(jnp.bfloat16)
    cross_mix, cross_log = attend(cross_q, cross_kv[0], cross_kv[1], None, scale)
    second_in = first + jnp.einsum(
        "old,de->ole", cross_mix, attn_out[1], preferred_element_type=jnp.float32
    )
    second = layer_norm(second_in, ln_gain[1], ln_bias[1])
    second_b = second.astype(jnp.bfloat16)
    inner = (
        jnp.einsum("old,df->olf", second_b, ffn_in, preferred_element_type=jnp.float32)
        + ffn_in_bias
    )
    inner_act = smooth(inner).astype(jnp.bfloat16)
    third_in = (
        second
        + jnp.einsum("olf,fd->old", inner_act, ffn_out, preferred_element_type=jnp.float32)
        + ffn_out_bias
    )
    decoded = layer_norm(third_in, ln_gain[2], ln_bias[2]).astype(jnp.bfloat16)
    grad_third, gain_three, shift_three = norm_grad(
        third_in, ln_gain[2], ln_bias[2], cotangent.reshape(start.shape).astype(jnp.float32)
    )
    grad_outer = grad_third.astype(jnp.bfloat16)
    ffn_out_g = jnp.einsum(
        "olf,old->fd", inner_act, grad_outer, preferred_element_type=jnp.float32
    )
    ffn_out_bias_g = jnp.sum(grad_outer.astype(jnp.float32), axis=(0, 1))
    grad_act = jnp.einsum(
        "old,fd->olf", grad_outer, ffn_out, preferred_element_type=jnp.float32
    )
    grad_inner = smooth_grad(inner, grad_act).astype(jnp.bfloat16)
    ffn_in_g = jnp.einsum(
        "old,olf->df", second_b, grad_inner, preferred_element_type=jnp.float32
    )
    ffn_in_bias_g = jnp.sum(grad_inner.astype(jnp.float32), axis=(0, 1))
    grad_second = grad_third + jnp.einsum(
        "olf,df->old", grad_inner, ffn_in, preferred_element_type=jnp.float32
    )
    grad_second_in, gain_two, shift_two = norm_grad(
        second_in, ln_gain[1], ln_bias[1], grad_second
    )
    grad_cross_out = grad_second_in.astype(jnp.bfloat16)
    out_two_g = jnp.einsum(
        "old,ole->de", cross_mix, grad_cross_out, preferred_element_type=jnp.float32
    )
    grad_cross_mix = jnp.einsum(
        "ole,de->old", grad_cross_out, attn_out[1], preferred_element_type=jnp.float32
    ).astype(jnp.bfloat16)
    cross_grads = attend_back(
        cross_q, cross_kv[0], cross_kv[1], None, scale, cross_log, grad_cross_mix
    )
    grad_cross_q = cross_grads[0].astype(jnp.bfloat16)
    grad_cross_kv = jnp.stack([cross_grads[1], cross_grads[2]]).astype(jnp.bfloat16)
    in_three_g = jnp.einsum(
        "old,ole->de", first_b, grad_cross_q, preferred_element_type=jnp.float32
    )
    in_pair_g = jnp.einsum(
        "oid,joie->jde", memory, grad_cross_kv, preferred_element_type=jnp.float32
    )
    grad_memory = jnp.einsum(
        "joie,jde->oid", grad_cross_kv, attn_in[4:6], preferred_element_type=jnp.float32
    )
    grad_first = grad_second_in + jnp.einsum(
        "ole,de->old", grad_cross_q, attn_in[3], preferred_element_type=jnp.float32
    )
    grad_first_in, gain_one, shift_one = norm_grad(first_in, ln_gain[0], ln_bias[0], grad_first)
    grad_self_out = grad_first_in.astype(jnp.bfloat16)
    out_one_g = jnp.einsum(
        "old,ole->de", self_mix, grad_self_out, preferred_element_type=jnp.float32
    )
    grad_self_mix = jnp.einsum(
        "ole,de->old", grad_self_out, attn_out[0], preferred_element_type=jnp.float32
    ).astype(jnp.bfloat16)
    self_grads = attend_back(
        projected[0], projected[1], projected[2], allowed, scale, self_log, grad_self_mix
    )
    grad_projected = jnp.stack([self_grads[0], self_grads[1], self_grads[2]]).astype(
        jnp.bfloat16
    )
    in_self_g = jnp.einsum(
        "old,jole->jde", start, grad_projected, preferred_element_type=jnp.float32
    )
    tags_grad = (
        grad_first_in
        + jnp.einsum(
            "jole,jde->old", grad_projected, attn_in[:3], preferred_element_type=jnp.float32
        )
    )
    grad_tokens = grad_memory.reshape(tokens.shape).astype(jnp.bfloat16)
    proj_g = jnp.einsum(
        "grwc,grwd->cd", block_out, grad_tokens, preferred_element_type=jnp.float32
    )
    proj_bias_g = jnp.sum(grad_tokens.astype(jnp.float32), axis=(0, 1, 2))
    grad_block = jnp.einsum(
        "grwd,cd->grwc", grad_tokens, proj_weight, preferred_element_type=jnp.float32
    )
    grad_act_two = smooth_grad(act_two, grad_block)
    scale_two_g = jnp.sum(grad_act_two * norm_two, axis=(0, 1, 2))
    shift_two_g = jnp.sum(grad_act_two, axis=(0, 1, 2))
    grad_pre_two = (grad_act_two * bn_scale[1] * factor[1]).astype(jnp.bfloat16)
    conv_two_g = kernel_grad(hidden, grad_pre_two)
    grad_hidden = conv_back(grad_pre_two, conv_weight[1])
    grad_act_one = smooth_grad(act_one, grad_hidden)
    scale_one_g = jnp.sum(grad_act_one * norm_one, axis=(0, 1, 2))
    shift_one_g = jnp.sum(grad_act_one, axis=(0, 1, 2))
    grad_pre_one = (grad_act_one * bn_scale[0] * factor[0]).astype(jnp.bfloat16)
    conv_one_g = kernel_grad(inputs, grad_pre_one)
    image_grad = conv_back(grad_pre_one, conv_weight[0]) + grad_act_two
    local = (
        jnp.stack([conv_one_g, conv_two_g]),
        jnp.stack([scale_one_g, scale_two_g]),
        jnp.stack([shift_one_g, shift_two_g]),
        proj_g,
        proj_bias_g,
        jnp.concatenate([in_self_g, in_three_g[None], in_pair_g]),
        jnp.stack([out_one_g, out_two_g]),
        jnp.stack([gain_one, gain_two, gain_three]),
        jnp.stack([shift_one, shift_two, shift_three]),
        ffn_in_g,
        ffn_in_bias_g,
        ffn_out_g,
        ffn_out_bias_g,
    )
    wide = [0, 3, 5, 6, 9, 11]
    sent = [g.astype(jnp.bfloat16) if i in wide else g for i, g in enumerate(local)]
    big = lax.psum(tuple(sent[i] for i in wide), ("dp", "row"))
    rest = [i for i in range(len(sent)) if i not in wide]
    small = lax.psum(jnp.concatenate([sent[i].reshape(-1) for i in rest]), ("dp", "row"))
    summed = list(local)
    for i, g in zip(wide, big):
        summed[i] = g.astype(jnp.float32)
    at = 0
    for i in rest:
        summed[i] = small[at : at + local[i].size].reshape(local[i].shape)
        at += local[i].size
    back = image_grad.astype(jnp.bfloat16).reshape((batches, owned) + image_grad.shape[1:])
    back = lax.all_to_all(back, "row", 2, 1, tiled=True)
    return (
        decoded.reshape(tags.shape),
        back.astype(jnp.float32),
        tags_grad.reshape(tags.shape),
        *summed,
    )


def solution(mesh):
    placed = (
        P(None, "dp", "row", None, None),
        P(None, ("dp", "row"), None, None),
        P(None, ("dp", "row")),
        P(None, ("dp", "row"), None, None),
        P(),
        P(),
        P(),
        P(),
        P(),
        P(),
        P(),
        P(),
        P(),
        P(),
        P(),
        P(),
        P(),
        P(),
        P(),
    )
    return jax.shard_map(
        body,
        mesh=mesh,
        in_specs=placed,
        out_specs=(
            P(None, ("dp", "row"), None, None),
            P(None, "dp", "row", None, None),
            P(None, ("dp", "row"), None, None),
            P(),
            P(),
            P(),
            P(),
            P(),
            P(),
            P(),
            P(),
            P(),
            P(),
            P(),
            P(),
            P(),
        ),
        check_vma=False,
    )
```

```python
import jax
import jax.numpy as jnp
from jax import lax
from jax.experimental import pallas as pl
from jax.experimental.pallas import tpu as pltpu
from jax.sharding import PartitionSpec as P

HEADS = 8
GROUP = 4
EPS = 1e-05
MASKED = -1e30
BF = jnp.bfloat16
F32 = jnp.float32
WIDE = 32
LEAD = 40
MIB = 1024 * 1024


def dot(left, right):
    return jnp.dot(left, right, preferred_element_type=F32)


def dot_nt(left, right):
    return lax.dot_general(left, right, (((1,), (1,)), ((), ())), preferred_element_type=F32)


def dot_tn(left, right):
    return lax.dot_general(left, right, (((0,), (0,)), ((), ())), preferred_element_type=F32)


def gelu_pair(value):
    cdf = 0.5 + 0.5 * lax.erf(value * 0.7071067811865476)
    density = jnp.exp(value * value * -0.5) * 0.3989422804014327
    return value * cdf, cdf + value * density


def real_columns(rows):
    at = lax.broadcasted_iota(jnp.int32, (rows, 1), 0)
    return lax.rem(at, WIDE) < 28


def spread(shifted, held, cells):
    for b in range(3):
        shifted[WIDE : WIDE + cells, b * 256 : (b + 1) * 256] = held[
            LEAD - 1 + b : LEAD - 1 + b + cells, :
        ].astype(BF)


def three_rows(shifted, start, rows):
    return jnp.concatenate(
        [shifted[start + a * WIDE : start + a * WIDE + rows, :] for a in range(3)], axis=1
    )


def clear_edges(shifted, helds, cells):
    shifted[0:WIDE, :] = jnp.zeros((WIDE, shifted.shape[1]), BF)
    shifted[WIDE + cells :, :] = jnp.zeros((WIDE, shifted.shape[1]), BF)
    for held in helds:
        held[0:LEAD, :] = jnp.zeros((LEAD, held.shape[1]), F32)
        held[LEAD + cells :, :] = jnp.zeros((held.shape[0] - LEAD - cells, held.shape[1]), F32)


def block_forward_kernel(
    image, weight, mean, var, scale, shift, proj, proj_bias, key_value,
    padded, hidden, block_out, slope_one, slope_two, norm_one, norm_two, memory, cross_kv,
    shifted, held_in, held_mid,
):
    cells = padded.shape[1]
    half = cells // 2
    height = image.shape[1]
    factor = lax.rsqrt(var[...] + EPS)

    @pl.when(pl.program_id(0) == 0)
    def _():
        clear_edges(shifted, (held_in, held_mid), cells)
        held_in[LEAD : LEAD + cells, :] = jnp.zeros((cells, 256), F32)

    for r in range(height):
        held_in[LEAD + r * WIDE : LEAD + r * WIDE + 28, :] = image[0, r].astype(F32)
    padded[0] = held_in[LEAD : LEAD + cells, :].astype(BF)
    spread(shifted, held_in, cells)
    real = real_columns(half)
    for start in (0, half):
        pre = dot(three_rows(shifted, start, half), weight[0])
        norm = (pre - mean[0:1]) * factor[0:1]
        act, slope = gelu_pair(norm * scale[0:1] + shift[0:1])
        act = jnp.where(real, act, 0.0)
        held_mid[LEAD + start : LEAD + start + half, :] = act
        hidden[0, start : start + half, :] = act.astype(BF)
        slope_one[0, start : start + half, :] = jnp.where(real, slope, 0.0).astype(BF)
        norm_one[0, start : start + half, :] = norm.astype(BF)
    spread(shifted, held_mid, cells)
    for start in (0, half):
        pre = dot(three_rows(shifted, start, half), weight[1])
        norm = (pre - mean[1:2]) * factor[1:2]
        total = norm * scale[1:2] + shift[1:2] + held_in[LEAD + start : LEAD + start + half, :]
        act, slope = gelu_pair(total)
        block = act.astype(BF)
        block_out[0, start : start + half, :] = block
        slope_two[0, start : start + half, :] = slope.astype(BF)
        norm_two[0, start : start + half, :] = norm.astype(BF)
        tokens = (dot(block, proj[...]) + proj_bias[...]).astype(BF)
        memory[0, start : start + half, :] = tokens
        for k in range(2):
            cross_kv[0, start : start + half, k * 512 : (k + 1) * 512] = dot(
                tokens, key_value[k]
            ).astype(BF)


def whole(*shape):
    zeros = (0,) * len(shape)
    return pl.BlockSpec(shape, lambda t: zeros)


def per_table(*shape):
    zeros = (0,) * len(shape)
    return pl.BlockSpec((1,) + shape, lambda t: (t,) + zeros)


def block_forward(image, weight, mean, var, scale, shift, proj, proj_bias, key_value):
    tables, height, breadth, width = image.shape
    cells = height * WIDE
    model = proj.shape[1]
    small = jax.ShapeDtypeStruct((tables, cells, width), BF)
    stats = [whole(2, width)] * 4
    return pl.pallas_call(
        block_forward_kernel,
        grid=(tables,),
        in_specs=[per_table(height, breadth, width), whole(*weight.shape)] + stats
        + [whole(*proj.shape), whole(1, model), whole(*key_value.shape)],
        out_specs=[per_table(cells, width)] * 7 + [per_table(cells, model), per_table(cells, 2 * model)],
        out_shape=[small] * 7 + [
            jax.ShapeDtypeStruct((tables, cells, model), BF),
            jax.ShapeDtypeStruct((tables, cells, 2 * model), BF),
        ],
        scratch_shapes=[
            pltpu.VMEM((cells + 2 * WIDE, 3 * width), BF),
            pltpu.VMEM((cells + 80, width), F32),
            pltpu.VMEM((cells + 80, width), F32),
        ],
        compiler_params=pltpu.CompilerParams(vmem_limit_bytes=56 * MIB),
        name="block_forward",
    )(image, weight, mean, var, scale, shift, proj, proj_bias, key_value)


def block_backward_kernel(
    grad_tokens, padded, hidden, block_out, slope_one, slope_two, norm_one, norm_two,
    weight_back, mean, var, scale, proj,
    image_grad, conv_grad, bn_sums, proj_grad, proj_bias_grad,
    shifted, held, kept, conv_sum, proj_sum, bn_sum, bias_sum,
):
    step = pl.program_id(0)
    cells = padded.shape[1]
    half = cells // 2
    height = image_grad.shape[1]
    gain = lax.rsqrt(var[...] + EPS) * scale[...]

    @pl.when(step == 0)
    def _():
        clear_edges(shifted, (held,), cells)
        conv_sum[...] = jnp.zeros_like(conv_sum)
        proj_sum[...] = jnp.zeros_like(proj_sum)
        bn_sum[...] = jnp.zeros_like(bn_sum)
        bias_sum[...] = jnp.zeros_like(bias_sum)

    def add_stats(layer, grad, norm):
        bn_sum[layer : layer + 1, :] += jnp.sum(grad * norm.astype(F32), axis=0, keepdims=True)
        bn_sum[2 + layer : 3 + layer, :] += jnp.sum(grad, axis=0, keepdims=True)

    def add_conv(layer, inputs):
        turned = inputs.T
        for a in range(3):
            start = (2 - a) * WIDE
            found = dot(turned, shifted[start : start + cells, :])
            for b in range(3):
                conv_sum[layer, a, b] += found[:, (2 - b) * 256 : (3 - b) * 256]

    proj_sum[...] += dot_tn(block_out[0], grad_tokens[0])
    bias_sum[...] += jnp.sum(grad_tokens[0].astype(F32), axis=0, keepdims=True)
    for start in (0, half):
        part = slice(start, start + half)
        grad = slope_two[0, part, :].astype(F32) * dot_nt(grad_tokens[0, part, :], proj[...])
        kept[part, :] = grad
        add_stats(1, grad, norm_two[0, part, :])
        held[LEAD + start : LEAD + start + half, :] = grad * gain[1:2]
    spread(shifted, held, cells)
    for start in (0, half):
        part = slice(start, start + half)
        back = dot(three_rows(shifted, start, half), weight_back[1])
        grad = slope_one[0, part, :].astype(F32) * back
        add_stats(0, grad, norm_one[0, part, :])
        held[LEAD + start : LEAD + start + half, :] = grad * gain[0:1]
    add_conv(1, hidden[0])
    spread(shifted, held, cells)
    for start in (0, half):
        back = dot(three_rows(shifted, start, half), weight_back[0]) + kept[start : start + half, :]
        back = back.astype(BF)
        for r in range(half // WIDE):
            image_grad[0, start // WIDE + r] = back[r * WIDE : r * WIDE + 28, :]
    add_conv(0, padded[0])

    @pl.when(step == pl.num_programs(0) - 1)
    def _():
        conv_grad[...] = conv_sum[...].astype(BF)
        proj_grad[...] = proj_sum[...].astype(BF)
        bn_sums[...] = bn_sum[...]
        proj_bias_grad[...] = bias_sum[...]


def block_backward(
    grad_tokens, padded, hidden, block_out, slope_one, slope_two, norm_one, norm_two,
    weight_back, mean, var, scale, proj, height, breadth,
):
    tables, cells, model = grad_tokens.shape
    width = proj.shape[0]
    per = per_table(cells, width)
    conv_shape = (2, 3, 3, width, width)
    return pl.pallas_call(
        block_backward_kernel,
        grid=(tables,),
        in_specs=[per_table(cells, model)] + [per] * 7
        + [whole(*weight_back.shape)] + [whole(2, width)] * 3 + [whole(*proj.shape)],
        out_specs=[
            per_table(height, breadth, width), whole(*conv_shape), whole(4, width),
            whole(*proj.shape), whole(1, model),
        ],
        out_shape=[
            jax.ShapeDtypeStruct((tables, height, breadth, width), BF),
            jax.ShapeDtypeStruct(conv_shape, BF),
            jax.ShapeDtypeStruct((4, width), F32),
            jax.ShapeDtypeStruct(proj.shape, BF),
            jax.ShapeDtypeStruct((1, model), F32),
        ],
        scratch_shapes=[
            pltpu.VMEM((cells + 2 * WIDE, 3 * width), BF),
            pltpu.VMEM((cells + 80, width), F32),
            pltpu.VMEM((cells, width), F32),
            pltpu.VMEM(conv_shape, F32),
            pltpu.VMEM(proj.shape, F32),
            pltpu.VMEM((4, width), F32),
            pltpu.VMEM((1, model), F32),
        ],
        compiler_params=pltpu.CompilerParams(vmem_limit_bytes=56 * MIB),
        name="block_backward",
    )(
        grad_tokens, padded, hidden, block_out, slope_one, slope_two, norm_one, norm_two,
        weight_back, mean, var, scale, proj,
    )


def lane_masks(rows, lanes):
    at = lax.broadcasted_iota(jnp.int32, (rows, lanes), 1) // 64
    return [at == h for h in range(GROUP)]


def by_head(value, masks):
    zero = jnp.zeros_like(value)
    return jnp.concatenate([jnp.where(m, value, zero) for m in masks], axis=0)


def own_lanes(stacked, masks):
    rows = stacked.shape[0] // GROUP
    total = stacked[0:rows]
    for h in range(1, GROUP):
        total = jnp.where(masks[h], stacked[h * rows : (h + 1) * rows], total)
    return total


def softmax_rows(scores):
    raised = jnp.exp(scores - jnp.max(scores, axis=-1, keepdims=True))
    return raised / jnp.sum(raised, axis=-1, keepdims=True)


def normalise(value):
    center = value - jnp.mean(value, axis=-1, keepdims=True)
    inverse = lax.rsqrt(jnp.mean(center * center, axis=-1, keepdims=True) + EPS)
    return center * inverse, inverse


def norm_back(upstream, gain, unit, inverse):
    scaled = upstream * gain
    mean = jnp.mean(scaled, axis=-1, keepdims=True)
    along = jnp.mean(scaled * unit, axis=-1, keepdims=True)
    return inverse * (scaled - mean - unit * along)


def column_sum(value):
    return jnp.sum(value, axis=0, keepdims=True)


def decoder_kernel(
    lengths, ln_gain, ln_bias, ffn_in_bias, ffn_out_bias,
    tags_far, cotangent_far, memory_far, cross_kv_far, attn_in_far, attn_out_far, ffn_in_far, ffn_out_far,
    decoded, tags_grad, grad_tokens, attn_in_grad, attn_out_grad, ffn_in_grad, ffn_out_grad,
    ln_gain_grad, ln_bias_grad, ffn_in_bias_grad, ffn_out_bias_grad,
    tags, cotangent, memory, cross_kv, attn_in, attn_out, ffn_in, ffn_out,
    qkv, mix, self_shares, cross_shares, cross_q, up, grad_qkv, grad_q, grad_kv, pair_sum,
    staged, weight_sem, kv_sem, memory_sem, staged_sem,
    held_attn_in, held_attn_out, held_ffn_in, held_ffn_out, grad_sem,
):
    tables, cells = memory_far.shape[0], memory_far.shape[1]
    slots = tags.shape[0] // tables

    def fetch_kv(t):
        return pltpu.make_async_copy(cross_kv_far.at[t], cross_kv.at[t], kv_sem.at[t])

    def fetch_memory(t):
        slot = lax.rem(t, 2)
        return pltpu.make_async_copy(memory_far.at[t], memory.at[slot], memory_sem.at[slot])

    def put_tokens(t):
        slot = lax.rem(t, 2)
        return pltpu.make_async_copy(staged.at[slot], grad_tokens.at[t], staged_sem.at[slot])

    fetches = [
        pltpu.make_async_copy(far, near, weight_sem.at[i])
        for i, (far, near) in enumerate(
            [(tags_far, tags)]
            + [(attn_in_far.at[k], attn_in.at[k]) for k in range(4)]
            + [(attn_out_far, attn_out), (cotangent_far, cotangent)]
            + [(ffn_in_far, ffn_in), (ffn_out_far, ffn_out)]
            + [(attn_in_far.at[k], attn_in.at[k]) for k in (4, 5)]
        )
    ]
    for copy in fetches[:6]:
        copy.start()
    for t in range(tables):
        fetch_kv(t).start()
    for copy in fetches[6:]:
        copy.start()
    fetch_memory(0).start()
    half = 256
    wide_f32 = lane_masks(slots, half)
    real_key = lax.rem(lax.broadcasted_iota(jnp.int32, (GROUP * slots, cells), 1), WIDE) < 28

    def allowed_of(t):
        row = lax.broadcasted_iota(jnp.int32, (slots, slots), 0)
        col = lax.broadcasted_iota(jnp.int32, (slots, slots), 1)
        once = (col <= row) & (col < lengths[t])
        return jnp.concatenate([once] * GROUP, axis=0)

    puts = [
        pltpu.make_async_copy(held_ffn_out, ffn_out_grad, grad_sem.at[0]),
        pltpu.make_async_copy(held_ffn_in, ffn_in_grad, grad_sem.at[1]),
        pltpu.make_async_copy(held_attn_out, attn_out_grad, grad_sem.at[2]),
    ] + [
        pltpu.make_async_copy(held_attn_in.at[k], attn_in_grad.at[k], grad_sem.at[3 + k])
        for k in range(6)
    ]
    fetches[0].wait()
    for k in range(3):
        fetches[1 + k].wait()
        qkv[k] = dot(tags[...], attn_in[k]).astype(BF)

    def self_forward(t, carry):
        rows = pl.ds(pl.multiple_of(t * slots, slots), slots)
        allowed = allowed_of(t)
        for g in range(2):
            lanes = slice(g * half, (g + 1) * half)
            query = by_head(qkv[0, rows, lanes], wide_f32)
            scores = dot_nt(query, qkv[1, rows, lanes]) * 0.125
            shares = softmax_rows(jnp.where(allowed, scores, MASKED)).astype(BF)
            self_shares[t, g] = shares
            mix[0, rows, lanes] = own_lanes(dot(shares, qkv[2, rows, lanes]), wide_f32).astype(BF)
        return carry

    lax.fori_loop(0, tables, self_forward, 0)
    fetches[5].wait()
    first_unit, first_inv = normalise(tags[...].astype(F32) + dot(mix[0], attn_out[0]))
    first = first_unit * ln_gain[0:1] + ln_bias[0:1]
    first_low = first.astype(BF)
    fetches[4].wait()
    cross_q[...] = dot(first_low, attn_in[3]).astype(BF)

    def cross_forward(t, carry):
        fetch_kv(t).wait()
        rows = pl.ds(pl.multiple_of(t * slots, slots), slots)
        for g in range(2):
            lanes = slice(g * half, (g + 1) * half)
            query = by_head(cross_q[rows, lanes], wide_f32)
            scores = dot_nt(query, cross_kv[t, :, lanes]) * 0.125
            shares = softmax_rows(jnp.where(real_key, scores, MASKED)).astype(BF)
            cross_shares[t, g] = shares
            value = cross_kv[t, :, 512 + g * half : 512 + (g + 1) * half]
            mix[1, rows, lanes] = own_lanes(dot(shares, value), wide_f32).astype(BF)
        return carry

    lax.fori_loop(0, tables, cross_forward, 0)
    second_unit, second_inv = normalise(first + dot(mix[1], attn_out[1]))
    second = second_unit * ln_gain[1:2] + ln_bias[1:2]
    second_low = second.astype(BF)
    for copy in fetches[6:]:
        copy.wait()
    act, slope = gelu_pair(dot(second_low, ffn_in[...]) + ffn_in_bias[...])
    inner_act = act.astype(BF)
    third_unit, third_inv = normalise(second + dot(inner_act, ffn_out[...]) + ffn_out_bias[...])
    decoded[...] = (third_unit * ln_gain[2:3] + ln_bias[2:3]).astype(BF)

    up_three = cotangent[...].astype(F32)
    ln_gain_grad[2:3, :] = column_sum(up_three * third_unit)
    ln_bias_grad[2:3, :] = column_sum(up_three)
    grad_third = norm_back(up_three, ln_gain[2:3], third_unit, third_inv)
    grad_outer = grad_third.astype(BF)
    held_ffn_out[...] = dot_tn(inner_act, grad_outer).astype(BF)
    puts[0].start()
    ffn_out_bias_grad[...] = column_sum(grad_outer.astype(F32))
    grad_inner = (slope * dot_nt(grad_outer, ffn_out[...])).astype(BF)
    held_ffn_in[...] = dot_tn(second_low, grad_inner).astype(BF)
    puts[1].start()
    ffn_in_bias_grad[...] = column_sum(grad_inner.astype(F32))
    up_two = grad_third + dot_nt(grad_inner, ffn_in[...])
    ln_gain_grad[1:2, :] = column_sum(up_two * second_unit)
    ln_bias_grad[1:2, :] = column_sum(up_two)
    grad_second = norm_back(up_two, ln_gain[1:2], second_unit, second_inv)
    grad_cross_out = grad_second.astype(BF)
    held_attn_out[1] = dot_tn(mix[1], grad_cross_out).astype(BF)
    up[...] = dot_nt(grad_cross_out, attn_out[1]).astype(BF)
    pair_sum[...] = jnp.zeros_like(pair_sum)

    def cross_back(t, carry):
        @pl.when(t + 1 < tables)
        def _():
            fetch_memory(t + 1).start()

        rows = pl.ds(pl.multiple_of(t * slots, slots), slots)
        for g in range(2):
            lanes = slice(g * half, (g + 1) * half)
            value_lanes = slice(512 + g * half, 512 + (g + 1) * half)
            query = by_head(cross_q[rows, lanes], wide_f32)
            upstream = by_head(up[rows, lanes], wide_f32)
            low = cross_shares[t, g]
            shares = low.astype(F32)
            grad_shares = dot_nt(upstream, cross_kv[t, :, value_lanes])
            mean = jnp.sum(grad_shares * shares, axis=-1, keepdims=True)
            grad_scores = (shares * (grad_shares - mean)).astype(BF)
            grad_q[rows, lanes] = (
                own_lanes(dot(grad_scores, cross_kv[t, :, lanes]), wide_f32) * 0.125
            ).astype(BF)
            grad_kv[:, lanes] = (dot_tn(grad_scores, query) * 0.125).astype(BF)
            grad_kv[:, value_lanes] = dot_tn(low, upstream).astype(BF)
        @pl.when(t >= 2)
        def _():
            put_tokens(t - 2).wait()

        slot = lax.rem(t, 2)
        staged[slot] = (
            dot_nt(grad_kv[:, 0:512], attn_in[4]) + dot_nt(grad_kv[:, 512:1024], attn_in[5])
        ).astype(BF)
        put_tokens(t).start()
        fetch_memory(t).wait()
        pair_sum[...] += dot_tn(memory[slot], grad_kv[...])
        return carry

    lax.fori_loop(0, tables, cross_back, 0)
    for t in range(max(tables - 2, 0), tables):
        put_tokens(t).wait()
    for k in range(2):
        held_attn_in[4 + k] = pair_sum[:, k * 512 : (k + 1) * 512].astype(BF)
        puts[7 + k].start()
    held_attn_in[3] = dot_tn(first_low, grad_q[...]).astype(BF)
    puts[6].start()
    up_one = grad_second + dot_nt(grad_q[...], attn_in[3])
    ln_gain_grad[0:1, :] = column_sum(up_one * first_unit)
    ln_bias_grad[0:1, :] = column_sum(up_one)
    grad_first = norm_back(up_one, ln_gain[0:1], first_unit, first_inv)
    grad_self_out = grad_first.astype(BF)
    held_attn_out[0] = dot_tn(mix[0], grad_self_out).astype(BF)
    puts[2].start()
    up[...] = dot_nt(grad_self_out, attn_out[0]).astype(BF)

    def self_back(t, carry):
        rows = pl.ds(pl.multiple_of(t * slots, slots), slots)
        for g in range(2):
            lanes = slice(g * half, (g + 1) * half)
            query = by_head(qkv[0, rows, lanes], wide_f32)
            upstream = by_head(up[rows, lanes], wide_f32)
            low = self_shares[t, g]
            shares = low.astype(F32)
            grad_shares = dot_nt(upstream, qkv[2, rows, lanes])
            mean = jnp.sum(grad_shares * shares, axis=-1, keepdims=True)
            grad_scores = (shares * (grad_shares - mean)).astype(BF)
            grad_qkv[0, rows, lanes] = (
                own_lanes(dot(grad_scores, qkv[1, rows, lanes]), wide_f32) * 0.125
            ).astype(BF)
            grad_qkv[1, rows, lanes] = (dot_tn(grad_scores, query) * 0.125).astype(BF)
            grad_qkv[2, rows, lanes] = dot_tn(low, upstream).astype(BF)
        return carry

    lax.fori_loop(0, tables, self_back, 0)
    total = grad_first
    for k in range(3):
        held_attn_in[k] = dot_tn(tags[...], grad_qkv[k]).astype(BF)
        puts[3 + k].start()
        total = total + dot_nt(grad_qkv[k], attn_in[k])
    tags_grad[...] = total
    for copy in puts:
        copy.wait()


def decoder(
    lengths, tags, cotangent, memory, cross_kv, attn_in, attn_out, ln_gain, ln_bias,
    ffn_in, ffn_in_bias, ffn_out, ffn_out_bias,
):
    tables, cells, model = memory.shape
    rows = tags.shape[0]
    slots = rows // tables
    inner = ffn_in.shape[1]
    here = pl.BlockSpec(memory_space=pltpu.VMEM)
    far = pl.BlockSpec(memory_space=pl.ANY)
    shape = jax.ShapeDtypeStruct
    stacked = GROUP * slots
    return pl.pallas_call(
        decoder_kernel,
        in_specs=[pl.BlockSpec(memory_space=pltpu.SMEM)] + [here] * 4 + [far] * 8,
        out_specs=[here] * 2 + [far] * 5 + [here] * 4,
        out_shape=[
            shape((rows, model), BF), shape((rows, model), F32), shape((tables, cells, model), BF),
            shape(attn_in.shape, BF), shape(attn_out.shape, BF), shape(ffn_in.shape, BF),
            shape(ffn_out.shape, BF), shape((3, model), F32), shape((3, model), F32),
            shape((1, inner), F32), shape((1, model), F32),
        ],
        scratch_shapes=[
            pltpu.VMEM((rows, model), BF),
            pltpu.VMEM((rows, model), BF),
            pltpu.VMEM((2, cells, model), BF),
            pltpu.VMEM((tables, cells, 2 * model), BF),
            pltpu.VMEM(attn_in.shape, BF),
            pltpu.VMEM(attn_out.shape, BF),
            pltpu.VMEM(ffn_in.shape, BF),
            pltpu.VMEM(ffn_out.shape, BF),
            pltpu.VMEM((3, rows, model), BF),
            pltpu.VMEM((2, rows, model), BF),
            pltpu.VMEM((tables, 2, stacked, slots), BF),
            pltpu.VMEM((tables, 2, stacked, cells), BF),
            pltpu.VMEM((rows, model), BF),
            pltpu.VMEM((rows, model), BF),
            pltpu.VMEM((3, rows, model), BF),
            pltpu.VMEM((rows, model), BF),
            pltpu.VMEM((cells, 2 * model), BF),
            pltpu.VMEM((model, 2 * model), F32),
            pltpu.VMEM((2, cells, model), BF),
            pltpu.SemaphoreType.DMA((11,)),
            pltpu.SemaphoreType.DMA((tables,)),
            pltpu.SemaphoreType.DMA((2,)),
            pltpu.SemaphoreType.DMA((2,)),
            pltpu.VMEM(attn_in.shape, BF),
            pltpu.VMEM(attn_out.shape, BF),
            pltpu.VMEM(ffn_in.shape, BF),
            pltpu.VMEM(ffn_out.shape, BF),
            pltpu.SemaphoreType.DMA((9,)),
        ],
        compiler_params=pltpu.CompilerParams(vmem_limit_bytes=60 * MIB),
        name="decoder",
    )(
        lengths, ln_gain, ln_bias, ffn_in_bias, ffn_out_bias,
        tags, cotangent, memory, cross_kv, attn_in, attn_out, ffn_in, ffn_out,
    )


def body(
    image, tags, tag_lengths, cotangent, conv_weight, bn_mean, bn_var, bn_scale, bn_shift,
    proj_weight, proj_bias, attn_in, attn_out, ln_gain, ln_bias,
    ffn_in, ffn_in_bias, ffn_out, ffn_out_bias,
):
    batches, owned, slots, model = tags.shape
    width = image.shape[-1]
    tables = batches * owned
    moved = lax.all_to_all(image, "row", 1, 2, tiled=True)
    whole_images = moved.reshape((tables,) + moved.shape[2:])
    weight = conv_weight.reshape(2, 9 * width, width)
    weight_back = conv_weight[:, ::-1, ::-1].transpose(0, 1, 2, 4, 3).reshape(2, 9 * width, width)
    forward = block_forward(
        whole_images, weight, bn_mean, bn_var, bn_scale, bn_shift,
        proj_weight, proj_bias.reshape(1, -1), attn_in[4:6],
    )
    padded, hidden, block_out, slope_one, slope_two, norm_one, norm_two, memory, cross_kv = forward
    (
        decoded, tags_grad, grad_tokens, attn_in_g, attn_out_g, ffn_in_g, ffn_out_g,
        gain_g, bias_g, ffn_in_bias_g, ffn_out_bias_g,
    ) = decoder(
        tag_lengths.reshape(-1), tags.reshape(-1, model), cotangent.reshape(-1, model),
        memory, cross_kv, attn_in, attn_out, ln_gain, ln_bias,
        ffn_in, ffn_in_bias.reshape(1, -1), ffn_out, ffn_out_bias.reshape(1, -1),
    )
    image_grad, conv_g, bn_g, proj_g, proj_bias_g = block_backward(
        grad_tokens, padded, hidden, block_out, slope_one, slope_two, norm_one, norm_two,
        weight_back, bn_mean, bn_var, bn_scale, proj_weight, moved.shape[2], moved.shape[3],
    )
    back = image_grad.reshape(moved.shape)
    back = lax.all_to_all(back, "row", 2, 1, tiled=True)
    big = lax.psum((conv_g, proj_g, attn_in_g, attn_out_g, ffn_in_g, ffn_out_g), ("dp", "row"))
    conv_g, proj_g, attn_in_g, attn_out_g, ffn_in_g, ffn_out_g = [g.astype(F32) for g in big]
    small = [bn_g, proj_bias_g, gain_g, bias_g, ffn_in_bias_g, ffn_out_bias_g]
    flat = lax.psum(jnp.concatenate([g.reshape(-1) for g in small]), ("dp", "row"))
    found, at = [], 0
    for g in small:
        found.append(flat[at : at + g.size].reshape(g.shape))
        at += g.size
    bn_g, proj_bias_g, gain_g, bias_g, ffn_in_bias_g, ffn_out_bias_g = found
    return (
        decoded.reshape(tags.shape), back.astype(F32), tags_grad.reshape(tags.shape),
        conv_g, bn_g[0:2], bn_g[2:4], proj_g, proj_bias_g.reshape(-1),
        attn_in_g, attn_out_g, gain_g, bias_g,
        ffn_in_g, ffn_in_bias_g.reshape(-1), ffn_out_g, ffn_out_bias_g.reshape(-1),
    )


def solution(mesh):
    by_rows = P(None, "dp", "row", None, None)
    by_table = P(None, ("dp", "row"), None, None)
    return jax.shard_map(
        body,
        mesh=mesh,
        in_specs=(by_rows, by_table, P(None, ("dp", "row")), by_table) + (P(),) * 15,
        out_specs=(by_table, by_rows, by_table) + (P(),) * 13,
        check_vma=False,
    )
```

```python
import functools

import jax
import jax.numpy as jnp
from jax import lax
from jax.experimental import pallas as pl
from jax.experimental.pallas import tpu as pltpu
from jax.sharding import PartitionSpec as P

HEADS = 8
GROUP = 4
EPS = 1e-05
MASKED = -1e30
BF = jnp.bfloat16
F32 = jnp.float32
WIDE = 32
LEAD = 40
MIB = 1024 * 1024
MESH = pl.DeviceIdType.MESH


def dot(left, right):
    return jnp.dot(left, right, preferred_element_type=F32)


def dot_nt(left, right):
    return lax.dot_general(left, right, (((1,), (1,)), ((), ())), preferred_element_type=F32)


def dot_tn(left, right):
    return lax.dot_general(left, right, (((0,), (0,)), ((), ())), preferred_element_type=F32)


def gelu_pair(value):
    cdf = 0.5 + 0.5 * lax.erf(value * 0.7071067811865476)
    density = jnp.exp(value * value * -0.5) * 0.3989422804014327
    return value * cdf, cdf + value * density


def real_columns(rows):
    at = lax.broadcasted_iota(jnp.int32, (rows, 1), 0)
    return lax.rem(at, WIDE) < 28


def spread(shifted, held, cells):
    for b in range(3):
        shifted[WIDE : WIDE + cells, b * 256 : (b + 1) * 256] = held[
            LEAD - 1 + b : LEAD - 1 + b + cells, :
        ].astype(BF)


def three_rows(shifted, start, rows):
    return jnp.concatenate(
        [shifted[start + a * WIDE : start + a * WIDE + rows, :] for a in range(3)], axis=1
    )


def clear_edges(shifted, helds, cells):
    shifted[0:WIDE, :] = jnp.zeros((WIDE, shifted.shape[1]), BF)
    shifted[WIDE + cells :, :] = jnp.zeros((WIDE, shifted.shape[1]), BF)
    for held in helds:
        held[0:LEAD, :] = jnp.zeros((LEAD, held.shape[1]), F32)
        held[LEAD + cells :, :] = jnp.zeros((held.shape[0] - LEAD - cells, held.shape[1]), F32)


def block_forward_kernel(
    image, weight, mean, var, scale, shift, proj, proj_bias, key_value,
    padded, hidden, block_out, slope_one, slope_two, norm_one, norm_two, memory, cross_kv,
    shifted, held_in, held_mid,
):
    cells = padded.shape[1]
    half = cells // 2
    height = image.shape[1]
    factor = lax.rsqrt(var[...] + EPS)

    @pl.when(pl.program_id(0) == 0)
    def _():
        clear_edges(shifted, (held_in, held_mid), cells)
        held_in[LEAD : LEAD + cells, :] = jnp.zeros((cells, 256), F32)

    for r in range(height):
        held_in[LEAD + r * WIDE : LEAD + r * WIDE + 28, :] = image[0, r].astype(F32)
    padded[0] = held_in[LEAD : LEAD + cells, :].astype(BF)
    spread(shifted, held_in, cells)
    real = real_columns(half)
    for start in (0, half):
        pre = dot(three_rows(shifted, start, half), weight[0])
        norm = (pre - mean[0:1]) * factor[0:1]
        act, slope = gelu_pair(norm * scale[0:1] + shift[0:1])
        act = jnp.where(real, act, 0.0)
        held_mid[LEAD + start : LEAD + start + half, :] = act
        hidden[0, start : start + half, :] = act.astype(BF)
        slope_one[0, start : start + half, :] = jnp.where(real, slope, 0.0).astype(BF)
        norm_one[0, start : start + half, :] = norm.astype(BF)
    spread(shifted, held_mid, cells)
    for start in (0, half):
        pre = dot(three_rows(shifted, start, half), weight[1])
        norm = (pre - mean[1:2]) * factor[1:2]
        total = norm * scale[1:2] + shift[1:2] + held_in[LEAD + start : LEAD + start + half, :]
        act, slope = gelu_pair(total)
        block = act.astype(BF)
        block_out[0, start : start + half, :] = block
        slope_two[0, start : start + half, :] = slope.astype(BF)
        norm_two[0, start : start + half, :] = norm.astype(BF)
        tokens = (dot(block, proj[...]) + proj_bias[...]).astype(BF)
        memory[0, start : start + half, :] = tokens
        for k in range(2):
            cross_kv[0, start : start + half, k * 512 : (k + 1) * 512] = dot(
                tokens, key_value[k]
            ).astype(BF)


def whole(*shape):
    zeros = (0,) * len(shape)
    return pl.BlockSpec(shape, lambda t: zeros)


def per_table(*shape):
    zeros = (0,) * len(shape)
    return pl.BlockSpec((1,) + shape, lambda t: (t,) + zeros)


def block_forward(image, weight, mean, var, scale, shift, proj, proj_bias, key_value):
    tables, height, breadth, width = image.shape
    cells = height * WIDE
    model = proj.shape[1]
    small = jax.ShapeDtypeStruct((tables, cells, width), BF)
    stats = [whole(2, width)] * 4
    return pl.pallas_call(
        block_forward_kernel,
        grid=(tables,),
        in_specs=[per_table(height, breadth, width), whole(*weight.shape)] + stats
        + [whole(*proj.shape), whole(1, model), whole(*key_value.shape)],
        out_specs=[per_table(cells, width)] * 7 + [per_table(cells, model), per_table(cells, 2 * model)],
        out_shape=[small] * 7 + [
            jax.ShapeDtypeStruct((tables, cells, model), BF),
            jax.ShapeDtypeStruct((tables, cells, 2 * model), BF),
        ],
        scratch_shapes=[
            pltpu.VMEM((cells + 2 * WIDE, 3 * width), BF),
            pltpu.VMEM((cells + 80, width), F32),
            pltpu.VMEM((cells + 80, width), F32),
        ],
        compiler_params=pltpu.CompilerParams(vmem_limit_bytes=56 * MIB),
        name="block_forward",
    )(image, weight, mean, var, scale, shift, proj, proj_bias, key_value)


def block_backward_kernel(
    grad_tokens, padded, hidden, block_out, slope_one, slope_two, norm_one, norm_two,
    weight_back, mean, var, scale, proj,
    image_grad, grads, bn_sums, proj_bias_grad,
    shifted, held, kept, conv_sum, proj_sum, bn_sum, bias_sum,
):
    step = pl.program_id(0)
    cells = padded.shape[1]
    half = cells // 2
    height = image_grad.shape[1]
    gain = lax.rsqrt(var[...] + EPS) * scale[...]

    @pl.when(step == 0)
    def _():
        clear_edges(shifted, (held,), cells)
        conv_sum[...] = jnp.zeros_like(conv_sum)
        proj_sum[...] = jnp.zeros_like(proj_sum)
        bn_sum[...] = jnp.zeros_like(bn_sum)
        bias_sum[...] = jnp.zeros_like(bias_sum)

    def add_stats(layer, grad, norm):
        bn_sum[layer : layer + 1, :] += jnp.sum(grad * norm.astype(F32), axis=0, keepdims=True)
        bn_sum[2 + layer : 3 + layer, :] += jnp.sum(grad, axis=0, keepdims=True)

    def add_conv(layer, inputs):
        turned = inputs.T
        for a in range(3):
            start = (2 - a) * WIDE
            found = dot(turned, shifted[start : start + cells, :])
            for b in range(3):
                conv_sum[layer, a, b] += found[:, (2 - b) * 256 : (3 - b) * 256]

    proj_sum[...] += dot_tn(block_out[0], grad_tokens[0])
    bias_sum[...] += jnp.sum(grad_tokens[0].astype(F32), axis=0, keepdims=True)
    for start in (0, half):
        part = slice(start, start + half)
        grad = slope_two[0, part, :].astype(F32) * dot_nt(grad_tokens[0, part, :], proj[...])
        kept[part, :] = grad
        add_stats(1, grad, norm_two[0, part, :])
        held[LEAD + start : LEAD + start + half, :] = grad * gain[1:2]
    spread(shifted, held, cells)
    for start in (0, half):
        part = slice(start, start + half)
        back = dot(three_rows(shifted, start, half), weight_back[1])
        grad = slope_one[0, part, :].astype(F32) * back
        add_stats(0, grad, norm_one[0, part, :])
        held[LEAD + start : LEAD + start + half, :] = grad * gain[0:1]
    add_conv(1, hidden[0])
    spread(shifted, held, cells)
    for start in (0, half):
        back = dot(three_rows(shifted, start, half), weight_back[0]) + kept[start : start + half, :]
        back = back.astype(BF)
        for r in range(half // WIDE):
            image_grad[0, start // WIDE + r] = back[r * WIDE : r * WIDE + 28, :]
    add_conv(0, padded[0])

    @pl.when(step == pl.num_programs(0) - 1)
    def _():
        for a in range(3):
            for b in range(3):
                rows = slice((3 * a + b) * 256, (3 * a + b + 1) * 256)
                for layer in range(2):
                    grads[rows, layer * 256 : (layer + 1) * 256] = conv_sum[layer, a, b].astype(BF)
        grads[9 * 256 :, :] = proj_sum[...].astype(BF)
        bn_sums[...] = bn_sum[...]
        proj_bias_grad[...] = bias_sum[...]


def block_backward(
    grad_tokens, padded, hidden, block_out, slope_one, slope_two, norm_one, norm_two,
    weight_back, mean, var, scale, proj, height, breadth,
):
    tables, cells, model = grad_tokens.shape
    width = proj.shape[0]
    per = per_table(cells, width)
    conv_shape = (2, 3, 3, width, width)
    return pl.pallas_call(
        block_backward_kernel,
        grid=(tables,),
        in_specs=[per_table(cells, model)] + [per] * 7
        + [whole(*weight_back.shape)] + [whole(2, width)] * 3 + [whole(*proj.shape)],
        out_specs=[
            per_table(height, breadth, width), whole(10 * width, model), whole(4, width), whole(1, model),
        ],
        out_shape=[
            jax.ShapeDtypeStruct((tables, height, breadth, width), BF),
            jax.ShapeDtypeStruct((10 * width, model), BF),
            jax.ShapeDtypeStruct((4, width), F32),
            jax.ShapeDtypeStruct((1, model), F32),
        ],
        scratch_shapes=[
            pltpu.VMEM((cells + 2 * WIDE, 3 * width), BF),
            pltpu.VMEM((cells + 80, width), F32),
            pltpu.VMEM((cells, width), F32),
            pltpu.VMEM(conv_shape, F32),
            pltpu.VMEM(proj.shape, F32),
            pltpu.VMEM((4, width), F32),
            pltpu.VMEM((1, model), F32),
        ],
        compiler_params=pltpu.CompilerParams(vmem_limit_bytes=56 * MIB),
        name="block_backward",
    )(
        grad_tokens, padded, hidden, block_out, slope_one, slope_two, norm_one, norm_two,
        weight_back, mean, var, scale, proj,
    )


def lane_masks(rows, lanes):
    at = lax.broadcasted_iota(jnp.int32, (rows, lanes), 1) // 64
    return [at == h for h in range(GROUP)]


def by_head(value, masks):
    zero = jnp.zeros_like(value)
    return jnp.concatenate([jnp.where(m, value, zero) for m in masks], axis=0)


def own_lanes(stacked, masks):
    rows = stacked.shape[0] // GROUP
    total = stacked[0:rows]
    for h in range(1, GROUP):
        total = jnp.where(masks[h], stacked[h * rows : (h + 1) * rows], total)
    return total


def softmax_rows(scores):
    raised = jnp.exp(scores - jnp.max(scores, axis=-1, keepdims=True))
    return raised / jnp.sum(raised, axis=-1, keepdims=True)


def normalise(value):
    center = value - jnp.mean(value, axis=-1, keepdims=True)
    inverse = lax.rsqrt(jnp.mean(center * center, axis=-1, keepdims=True) + EPS)
    return center * inverse, inverse


def norm_back(upstream, gain, unit, inverse):
    scaled = upstream * gain
    mean = jnp.mean(scaled, axis=-1, keepdims=True)
    along = jnp.mean(scaled * unit, axis=-1, keepdims=True)
    return inverse * (scaled - mean - unit * along)


def column_sum(value):
    return jnp.sum(value, axis=0, keepdims=True)


def decoder_kernel(
    lengths, ln_gain, ln_bias, ffn_in_bias, ffn_out_bias,
    tags_far, cotangent_far, memory_far, cross_kv_far, attn_in_far, attn_out_far, ffn_in_far, ffn_out_far,
    decoded, tags_grad, grad_tokens, grads_far,
    ln_gain_grad, ln_bias_grad, ffn_in_bias_grad, ffn_out_bias_grad,
    tags, cotangent, memory, cross_kv, attn_in, attn_out, ffn_in, ffn_out,
    qkv, mix, self_shares, cross_shares, cross_q, up, grad_qkv, grad_q, grad_kv, pair_sum,
    staged, weight_sem, kv_sem, memory_sem, staged_sem,
    grads, grad_sem,
):
    tables, cells = memory_far.shape[0], memory_far.shape[1]
    slots = tags.shape[0] // tables

    def fetch_kv(t):
        return pltpu.make_async_copy(cross_kv_far.at[t], cross_kv.at[t], kv_sem.at[t])

    def fetch_memory(t):
        slot = lax.rem(t, 2)
        return pltpu.make_async_copy(memory_far.at[t], memory.at[slot], memory_sem.at[slot])

    def put_tokens(t):
        slot = lax.rem(t, 2)
        return pltpu.make_async_copy(staged.at[slot], grad_tokens.at[t], staged_sem.at[slot])

    fetches = [
        pltpu.make_async_copy(far, near, weight_sem.at[i])
        for i, (far, near) in enumerate(
            [(tags_far, tags)]
            + [(attn_in_far.at[k], attn_in.at[k]) for k in range(4)]
            + [(attn_out_far, attn_out), (cotangent_far, cotangent)]
            + [(ffn_in_far, ffn_in), (ffn_out_far, ffn_out)]
            + [(attn_in_far.at[k], attn_in.at[k]) for k in (4, 5)]
        )
    ]
    for copy in fetches[:6]:
        copy.start()
    for t in range(tables):
        fetch_kv(t).start()
    for copy in fetches[6:]:
        copy.start()
    fetch_memory(0).start()
    half = 256
    wide_f32 = lane_masks(slots, half)
    real_key = lax.rem(lax.broadcasted_iota(jnp.int32, (GROUP * slots, cells), 1), WIDE) < 28

    def allowed_of(t):
        row = lax.broadcasted_iota(jnp.int32, (slots, slots), 0)
        col = lax.broadcasted_iota(jnp.int32, (slots, slots), 1)
        once = (col <= row) & (col < lengths[t])
        return jnp.concatenate([once] * GROUP, axis=0)

    def put_grad(i, value):
        grads[i] = value.astype(BF)
        copy = pltpu.make_async_copy(grads.at[i], grads_far.at[i], grad_sem.at[i])
        copy.start()
        puts.append(copy)

    puts = []
    fetches[0].wait()
    for k in range(3):
        fetches[1 + k].wait()
        qkv[k] = dot(tags[...], attn_in[k]).astype(BF)

    def self_forward(t, carry):
        rows = pl.ds(pl.multiple_of(t * slots, slots), slots)
        allowed = allowed_of(t)
        for g in range(2):
            lanes = slice(g * half, (g + 1) * half)
            query = by_head(qkv[0, rows, lanes], wide_f32)
            scores = dot_nt(query, qkv[1, rows, lanes]) * 0.125
            shares = softmax_rows(jnp.where(allowed, scores, MASKED)).astype(BF)
            self_shares[t, g] = shares
            mix[0, rows, lanes] = own_lanes(dot(shares, qkv[2, rows, lanes]), wide_f32).astype(BF)
        return carry

    lax.fori_loop(0, tables, self_forward, 0)
    fetches[5].wait()
    first_unit, first_inv = normalise(tags[...].astype(F32) + dot(mix[0], attn_out[0]))
    first = first_unit * ln_gain[0:1] + ln_bias[0:1]
    first_low = first.astype(BF)
    fetches[4].wait()
    cross_q[...] = dot(first_low, attn_in[3]).astype(BF)

    def cross_forward(t, carry):
        fetch_kv(t).wait()
        rows = pl.ds(pl.multiple_of(t * slots, slots), slots)
        for g in range(2):
            lanes = slice(g * half, (g + 1) * half)
            query = by_head(cross_q[rows, lanes], wide_f32)
            scores = dot_nt(query, cross_kv[t, :, lanes]) * 0.125
            shares = softmax_rows(jnp.where(real_key, scores, MASKED)).astype(BF)
            cross_shares[t, g] = shares
            value = cross_kv[t, :, 512 + g * half : 512 + (g + 1) * half]
            mix[1, rows, lanes] = own_lanes(dot(shares, value), wide_f32).astype(BF)
        return carry

    lax.fori_loop(0, tables, cross_forward, 0)
    second_unit, second_inv = normalise(first + dot(mix[1], attn_out[1]))
    second = second_unit * ln_gain[1:2] + ln_bias[1:2]
    second_low = second.astype(BF)
    for copy in fetches[6:]:
        copy.wait()
    act, slope = gelu_pair(dot(second_low, ffn_in[...]) + ffn_in_bias[...])
    inner_act = act.astype(BF)
    third_unit, third_inv = normalise(second + dot(inner_act, ffn_out[...]) + ffn_out_bias[...])
    decoded[...] = (third_unit * ln_gain[2:3] + ln_bias[2:3]).astype(BF)

    up_three = cotangent[...].astype(F32)
    ln_gain_grad[2:3, :] = column_sum(up_three * third_unit)
    ln_bias_grad[2:3, :] = column_sum(up_three)
    grad_third = norm_back(up_three, ln_gain[2:3], third_unit, third_inv)
    grad_outer = grad_third.astype(BF)
    ffn_out_total = dot_tn(inner_act, grad_outer)
    for k in range(2):
        put_grad(8 + k, ffn_out_total[k * 512 : (k + 1) * 512])
    ffn_out_bias_grad[...] = column_sum(grad_outer.astype(F32))
    grad_inner = (slope * dot_nt(grad_outer, ffn_out[...])).astype(BF)
    ffn_in_total = dot_tn(second_low, grad_inner)
    for k in range(2):
        put_grad(10 + k, ffn_in_total[:, k * 512 : (k + 1) * 512])
    ffn_in_bias_grad[...] = column_sum(grad_inner.astype(F32))
    up_two = grad_third + dot_nt(grad_inner, ffn_in[...])
    ln_gain_grad[1:2, :] = column_sum(up_two * second_unit)
    ln_bias_grad[1:2, :] = column_sum(up_two)
    grad_second = norm_back(up_two, ln_gain[1:2], second_unit, second_inv)
    grad_cross_out = grad_second.astype(BF)
    put_grad(7, dot_tn(mix[1], grad_cross_out))
    up[...] = dot_nt(grad_cross_out, attn_out[1]).astype(BF)
    pair_sum[...] = jnp.zeros_like(pair_sum)

    def cross_back(t, carry):
        @pl.when(t + 1 < tables)
        def _():
            fetch_memory(t + 1).start()

        rows = pl.ds(pl.multiple_of(t * slots, slots), slots)
        for g in range(2):
            lanes = slice(g * half, (g + 1) * half)
            value_lanes = slice(512 + g * half, 512 + (g + 1) * half)
            query = by_head(cross_q[rows, lanes], wide_f32)
            upstream = by_head(up[rows, lanes], wide_f32)
            low = cross_shares[t, g]
            shares = low.astype(F32)
            grad_shares = dot_nt(upstream, cross_kv[t, :, value_lanes])
            mean = jnp.sum(grad_shares * shares, axis=-1, keepdims=True)
            grad_scores = (shares * (grad_shares - mean)).astype(BF)
            grad_q[rows, lanes] = (
                own_lanes(dot(grad_scores, cross_kv[t, :, lanes]), wide_f32) * 0.125
            ).astype(BF)
            grad_kv[:, lanes] = (dot_tn(grad_scores, query) * 0.125).astype(BF)
            grad_kv[:, value_lanes] = dot_tn(low, upstream).astype(BF)
        @pl.when(t >= 2)
        def _():
            put_tokens(t - 2).wait()

        slot = lax.rem(t, 2)
        staged[slot] = (
            dot_nt(grad_kv[:, 0:512], attn_in[4]) + dot_nt(grad_kv[:, 512:1024], attn_in[5])
        ).astype(BF)
        put_tokens(t).start()
        fetch_memory(t).wait()
        pair_sum[...] += dot_tn(memory[slot], grad_kv[...])
        return carry

    lax.fori_loop(0, tables, cross_back, 0)
    for t in range(max(tables - 2, 0), tables):
        put_tokens(t).wait()
    for k in range(2):
        put_grad(4 + k, pair_sum[:, k * 512 : (k + 1) * 512])
    put_grad(3, dot_tn(first_low, grad_q[...]))
    up_one = grad_second + dot_nt(grad_q[...], attn_in[3])
    ln_gain_grad[0:1, :] = column_sum(up_one * first_unit)
    ln_bias_grad[0:1, :] = column_sum(up_one)
    grad_first = norm_back(up_one, ln_gain[0:1], first_unit, first_inv)
    grad_self_out = grad_first.astype(BF)
    put_grad(6, dot_tn(mix[0], grad_self_out))
    up[...] = dot_nt(grad_self_out, attn_out[0]).astype(BF)

    def self_back(t, carry):
        rows = pl.ds(pl.multiple_of(t * slots, slots), slots)
        for g in range(2):
            lanes = slice(g * half, (g + 1) * half)
            query = by_head(qkv[0, rows, lanes], wide_f32)
            upstream = by_head(up[rows, lanes], wide_f32)
            low = self_shares[t, g]
            shares = low.astype(F32)
            grad_shares = dot_nt(upstream, qkv[2, rows, lanes])
            mean = jnp.sum(grad_shares * shares, axis=-1, keepdims=True)
            grad_scores = (shares * (grad_shares - mean)).astype(BF)
            grad_qkv[0, rows, lanes] = (
                own_lanes(dot(grad_scores, qkv[1, rows, lanes]), wide_f32) * 0.125
            ).astype(BF)
            grad_qkv[1, rows, lanes] = (dot_tn(grad_scores, query) * 0.125).astype(BF)
            grad_qkv[2, rows, lanes] = dot_tn(low, upstream).astype(BF)
        return carry

    lax.fori_loop(0, tables, self_back, 0)
    total = grad_first
    for k in range(3):
        put_grad(k, dot_tn(tags[...], grad_qkv[k]))
        total = total + dot_nt(grad_qkv[k], attn_in[k])
    tags_grad[...] = total
    for copy in puts:
        copy.wait()


def decoder(
    lengths, tags, cotangent, memory, cross_kv, attn_in, attn_out, ln_gain, ln_bias,
    ffn_in, ffn_in_bias, ffn_out, ffn_out_bias,
):
    tables, cells, model = memory.shape
    rows = tags.shape[0]
    slots = rows // tables
    inner = ffn_in.shape[1]
    here = pl.BlockSpec(memory_space=pltpu.VMEM)
    far = pl.BlockSpec(memory_space=pl.ANY)
    shape = jax.ShapeDtypeStruct
    stacked = GROUP * slots
    return pl.pallas_call(
        decoder_kernel,
        in_specs=[pl.BlockSpec(memory_space=pltpu.SMEM)] + [here] * 4 + [far] * 8,
        out_specs=[here] * 2 + [far] * 2 + [here] * 4,
        out_shape=[
            shape((rows, model), BF), shape((rows, model), F32), shape((tables, cells, model), BF),
            shape((12, 512, model), BF), shape((3, model), F32), shape((3, model), F32),
            shape((1, inner), F32), shape((1, model), F32),
        ],
        scratch_shapes=[
            pltpu.VMEM((rows, model), BF),
            pltpu.VMEM((rows, model), BF),
            pltpu.VMEM((2, cells, model), BF),
            pltpu.VMEM((tables, cells, 2 * model), BF),
            pltpu.VMEM(attn_in.shape, BF),
            pltpu.VMEM(attn_out.shape, BF),
            pltpu.VMEM(ffn_in.shape, BF),
            pltpu.VMEM(ffn_out.shape, BF),
            pltpu.VMEM((3, rows, model), BF),
            pltpu.VMEM((2, rows, model), BF),
            pltpu.VMEM((tables, 2, stacked, slots), BF),
            pltpu.VMEM((tables, 2, stacked, cells), BF),
            pltpu.VMEM((rows, model), BF),
            pltpu.VMEM((rows, model), BF),
            pltpu.VMEM((3, rows, model), BF),
            pltpu.VMEM((rows, model), BF),
            pltpu.VMEM((cells, 2 * model), BF),
            pltpu.VMEM((model, 2 * model), F32),
            pltpu.VMEM((2, cells, model), BF),
            pltpu.SemaphoreType.DMA((11,)),
            pltpu.SemaphoreType.DMA((tables,)),
            pltpu.SemaphoreType.DMA((2,)),
            pltpu.SemaphoreType.DMA((2,)),
            pltpu.VMEM((12, 512, model), BF),
            pltpu.SemaphoreType.DMA((12,)),
        ],
        compiler_params=pltpu.CompilerParams(vmem_limit_bytes=60 * MIB),
        name="decoder",
    )(
        lengths, ln_gain, ln_bias, ffn_in_bias, ffn_out_bias,
        tags, cotangent, memory, cross_kv, attn_in, attn_out, ffn_in, ffn_out,
    )


def orders(dp, row):
    row_bits = [("row", 1 << i) for i in range(row.bit_length() - 1)]
    dp_bits = [("dp", 1 << i) for i in range(dp.bit_length() - 1)]
    pair, others = row_bits[:1], row_bits[1:]
    near, far = dp_bits[:1], dp_bits[1:]
    return [pair + near + others + far, pair + others + near + far, pair + far + near + others]


def plan_of(units):
    turn = (0, 1, 2) * 4 + (0, 1, 0, 1, 0)
    return [(turn[i % len(turn)], i, 1) for i in range(units)]


def side_of(axis, bit):
    return lax.rem(lax.axis_index(axis) // bit, 2)


def partner_of(axis, bit):
    return {axis: lax.axis_index(axis) + bit * (1 - 2 * side_of(axis, bit))}


def add_rows(target, held, start, landed, at, rows):
    step = 128
    while rows % step:
        step //= 2

    def one(i, carry):
        here = pl.ds(pl.multiple_of(start + i * step, 16), step)
        there = pl.ds(pl.multiple_of(at + i * step, 16), step)
        target[here, :] = held[here, :] + landed[there, :]
        return carry

    lax.fori_loop(0, rows // step, one, 0)


def reduce_kernel(plan, streams, unit, sizes, row, *refs):
    count = len(sizes)
    parts, small, image_grad = refs[:count], refs[count], refs[count + 1]
    total, small_total, image_back = refs[count + 2 : count + 5]
    held, landed, done, small_held, small_landed = refs[count + 5 : count + 10]
    load_sem, send_sem, land_sem, back_sem, home_sem = refs[count + 10 : count + 15]
    small_send, small_land, out_sem, image_send, image_land, image_sem = refs[count + 15 :]
    stages = len(streams[0])
    rows_all = sum(sizes)
    bounds = [sum(sizes[:i]) for i in range(count + 1)]
    loads = [
        pltpu.make_async_copy(part, held.at[pl.ds(bounds[i], sizes[i]), :], load_sem.at[i])
        for i, part in enumerate(parts)
    ]
    for copy in loads:
        copy.start()
    barrier = pltpu.get_barrier_semaphore()
    me = lax.axis_index("row")
    peers = [{"row": lax.rem(me + d, row)} for d in range(1, row)]
    across = [partner_of(axis, bit) for axis, bit in streams[0] if axis == "dp"]
    for device in peers + across:
        pl.semaphore_signal(barrier, inc=1, device_id=device, device_id_type=MESH)
    pl.semaphore_wait(barrier, len(peers) + len(across))
    batches, owned, height = image_back.shape[0], image_back.shape[1] // row, image_back.shape[2]
    mine = pl.ds(me * owned, owned)
    images = []
    for b in range(batches):
        for d in range(1, row):
            device = {"row": lax.rem(me + d, row)}
            images.append(pltpu.make_async_remote_copy(
                src_ref=image_grad.at[b, :, pl.ds(device["row"] * height, height)],
                dst_ref=image_back.at[b, mine],
                send_sem=image_send.at[b, d - 1], recv_sem=image_land.at[b, d - 1],
                device_id=device, device_id_type=MESH,
            ))
        images.append(pltpu.make_async_copy(
            image_grad.at[b, :, pl.ds(me * height, height)], image_back.at[b, mine], image_sem.at[b],
        ))
    for copy in images:
        copy.start()
    small_held[0] = small[...]
    loaded = [False] * count

    def need(first, last):
        for i in range(count):
            if bounds[i] < last and bounds[i + 1] > first and not loaded[i]:
                loads[i].wait()
                loaded[i] = True

    state = [dict(start=first * unit, rows=n * unit, at=0) for _, first, n in plan]
    flights, backs, outs = {}, {}, []

    def small_step(s):
        if s > 0:
            flights["small", s - 1].wait()
            both = small_held[s - 1] + small_landed[s - 1]
            if s == stages:
                small_total[...] = both
                return
            small_held[s] = both
        axis, bit = streams[0][s]
        copy = pltpu.make_async_remote_copy(
            src_ref=small_held.at[s], dst_ref=small_landed.at[s],
            send_sem=small_send.at[s], recv_sem=small_land.at[s],
            device_id=partner_of(axis, bit), device_id_type=MESH,
        )
        copy.start()
        flights["small", s] = copy

    def collect(c, s, target):
        _, first, n = plan[c]
        now = state[c]
        flights[c, s].wait_recv()
        add_rows(target, held, now["start"], landed, first * unit + now["at"], now["rows"])
        now["at"] += now["rows"]

    def split(c, s):
        stream, first, n = plan[c]
        now = state[c]
        axis, bit = streams[stream][s]
        if s == 0:
            need(first * unit, (first + n) * unit)
        else:
            collect(c, s - 1, held)
        half = now["rows"] // 2
        side = side_of(axis, bit)
        base = now["start"]
        copy = pltpu.make_async_remote_copy(
            src_ref=held.at[pl.ds(pl.multiple_of(base + (1 - side) * half, 16), half), :],
            dst_ref=landed.at[pl.ds(first * unit + now["at"], half), :],
            send_sem=send_sem.at[c, s], recv_sem=land_sem.at[c, s],
            device_id=partner_of(axis, bit), device_id_type=MESH,
        )
        copy.start()
        flights[c, s] = copy
        now["start"] = base + side * half
        now["rows"] = half

    def merge(c, s):
        stream, first, n = plan[c]
        now = state[c]
        axis, bit = streams[stream][s]
        if s == stages - 1:
            collect(c, s, done)
        else:
            backs[c, s + 1].wait_recv()
            now["rows"] *= 2
            now["start"] = now["start"] - side_of(*streams[stream][s + 1]) * (now["rows"] // 2)
        region = done.at[pl.ds(pl.multiple_of(now["start"], 16), now["rows"]), :]
        copy = pltpu.make_async_remote_copy(
            src_ref=region, dst_ref=region,
            send_sem=back_sem.at[c, s], recv_sem=home_sem.at[c, s],
            device_id=partner_of(axis, bit), device_id_type=MESH,
        )
        copy.start()
        backs[c, s] = copy

    def finish(c):
        _, first, n = plan[c]
        backs[c, 0].wait_recv()
        last = min((first + n) * unit, rows_all)
        if last > first * unit:
            region = pl.ds(first * unit, last - first * unit)
            copy = pltpu.make_async_copy(done.at[region, :], total.at[region, :], out_sem.at[c])
            copy.start()
            outs.append(copy)

    lags, seen = [], {}
    for stream, _, _ in plan:
        lags.append(seen.get(stream, 0))
        seen[stream] = lags[-1] + 1
    for turn in range(2 * stages + 1 + max(lags)):
        if turn <= stages:
            small_step(turn)
        for c, lag in reversed(list(enumerate(lags))):
            k = turn - lag
            if 0 <= k < stages:
                split(c, k)
            elif stages <= k < 2 * stages:
                merge(c, 2 * stages - 1 - k)
            elif k == 2 * stages:
                finish(c)
    for c in range(len(plan)):
        for s in range(stages):
            flights[c, s].wait_send()
            backs[c, s].wait_send()
    for copy in outs + images:
        copy.wait()


def reduce_all(parts, small, image_grad, dp, row):
    streams = orders(dp, row)
    stages = len(streams[0])
    sizes = [p.shape[0] for p in parts]
    rows, width = sum(sizes), parts[0].shape[1]
    unit = 16 * dp * row
    plan = plan_of(-(-rows // unit))
    chunks = len(plan)
    batches, owned, height, breadth, channels = image_grad.shape
    back = (batches, owned * row, height // row, breadth, channels)
    far = pl.BlockSpec(memory_space=pl.ANY)
    near = pl.BlockSpec(memory_space=pltpu.VMEM)
    sem = pltpu.SemaphoreType.DMA
    return pl.pallas_call(
        functools.partial(reduce_kernel, plan, streams, unit, sizes, row),
        in_specs=[far] * len(parts) + [near, far],
        out_specs=[far, near, far],
        out_shape=[
            jax.ShapeDtypeStruct((rows, width), BF),
            jax.ShapeDtypeStruct(small.shape, F32),
            jax.ShapeDtypeStruct(back, BF),
        ],
        scratch_shapes=[
            pltpu.VMEM((chunks * unit, width), BF),
            pltpu.VMEM((chunks * unit, width), BF),
            pltpu.VMEM((chunks * unit, width), BF),
            pltpu.VMEM((stages,) + small.shape, F32),
            pltpu.VMEM((stages,) + small.shape, F32),
            sem((len(parts),)), sem((chunks, stages)), sem((chunks, stages)),
            sem((chunks, stages)), sem((chunks, stages)),
            sem((stages,)), sem((stages,)), sem((chunks,)),
            sem((batches, row - 1)), sem((batches, row - 1)), sem((batches,)),
        ],
        compiler_params=pltpu.CompilerParams(
            vmem_limit_bytes=40 * MIB, collective_id=0, has_side_effects=True
        ),
        name="reduce_all",
    )(*parts, small, image_grad)


def body(
    image, tags, tag_lengths, cotangent, conv_weight, bn_mean, bn_var, bn_scale, bn_shift,
    proj_weight, proj_bias, attn_in, attn_out, ln_gain, ln_bias,
    ffn_in, ffn_in_bias, ffn_out, ffn_out_bias,
):
    batches, owned, slots, model = tags.shape
    width = image.shape[-1]
    tables = batches * owned
    moved = lax.all_to_all(image, "row", 1, 2, tiled=True)
    whole_images = moved.reshape((tables,) + moved.shape[2:])
    weight = conv_weight.reshape(2, 9 * width, width)
    weight_back = conv_weight[:, ::-1, ::-1].transpose(0, 1, 2, 4, 3).reshape(2, 9 * width, width)
    forward = block_forward(
        whole_images, weight, bn_mean, bn_var, bn_scale, bn_shift,
        proj_weight, proj_bias.reshape(1, -1), attn_in[4:6],
    )
    padded, hidden, block_out, slope_one, slope_two, norm_one, norm_two, memory, cross_kv = forward
    decoded, tags_grad, grad_tokens, decoder_g, gain_g, bias_g, ffn_in_bias_g, ffn_out_bias_g = decoder(
        tag_lengths.reshape(-1), tags.reshape(-1, model), cotangent.reshape(-1, model),
        memory, cross_kv, attn_in, attn_out, ln_gain, ln_bias,
        ffn_in, ffn_in_bias.reshape(1, -1), ffn_out, ffn_out_bias.reshape(1, -1),
    )
    image_grad, block_g, bn_g, proj_bias_g = block_backward(
        grad_tokens, padded, hidden, block_out, slope_one, slope_two, norm_one, norm_two,
        weight_back, bn_mean, bn_var, bn_scale, proj_weight, moved.shape[2], moved.shape[3],
    )
    small = [bn_g, proj_bias_g, gain_g, bias_g, ffn_in_bias_g, ffn_out_bias_g]
    flat = jnp.concatenate([g.reshape(-1, model) for g in small])
    spare = -flat.shape[0] % 8
    total, flat, back = reduce_all(
        (decoder_g.reshape(-1, model), block_g), jnp.pad(flat, ((0, spare), (0, 0))),
        image_grad.reshape(moved.shape), lax.axis_size("dp"), lax.axis_size("row"),
    )
    found, at = [], 0
    for g in small:
        rows = g.size // model
        found.append(flat[at : at + rows].reshape(g.shape))
        at += rows
    bn_g, proj_bias_g, gain_g, bias_g, ffn_in_bias_g, ffn_out_bias_g = found
    units = total[: 12 * 512].reshape(12, 512, model).astype(F32)
    conv_g = total[12 * 512 : 12 * 512 + 9 * width].reshape(3, 3, width, 2, width)
    proj_g = total[12 * 512 + 9 * width :]
    return (
        decoded.reshape(tags.shape), back.astype(F32), tags_grad.reshape(tags.shape),
        conv_g.transpose(3, 0, 1, 2, 4).astype(F32), bn_g[0:2], bn_g[2:4],
        proj_g.astype(F32), proj_bias_g.reshape(-1),
        units[0:6], units[6:8], gain_g, bias_g,
        jnp.concatenate([units[10], units[11]], axis=1), ffn_in_bias_g.reshape(-1),
        units[8:10].reshape(ffn_out.shape), ffn_out_bias_g.reshape(-1),
    )


def solution(mesh):
    by_rows = P(None, "dp", "row", None, None)
    by_table = P(None, ("dp", "row"), None, None)
    return jax.shard_map(
        body,
        mesh=mesh,
        in_specs=(by_rows, by_table, P(None, ("dp", "row")), by_table) + (P(),) * 15,
        out_specs=(by_table, by_rows, by_table) + (P(),) * 13,
        check_vma=False,
    )
```

```python
import functools

import jax
import jax.numpy as jnp
from jax import lax
from jax.experimental import pallas as pl
from jax.experimental.pallas import tpu as pltpu
from jax.sharding import PartitionSpec as P

HEADS = 8
GROUP = 4
EPS = 1e-05
MASKED = -1e30
BF = jnp.bfloat16
F32 = jnp.float32
WIDE = 32
LEAD = 40
MIB = 1024 * 1024
MESH = pl.DeviceIdType.MESH


def dot(left, right):
    return jnp.dot(left, right, preferred_element_type=F32)


def dot_nt(left, right):
    return lax.dot_general(left, right, (((1,), (1,)), ((), ())), preferred_element_type=F32)


def dot_tn(left, right):
    return lax.dot_general(left, right, (((0,), (0,)), ((), ())), preferred_element_type=F32)


def gelu_pair(value):
    cdf = 0.5 + 0.5 * lax.erf(value * 0.7071067811865476)
    density = jnp.exp(value * value * -0.5) * 0.3989422804014327
    return value * cdf, cdf + value * density


def real_columns(rows):
    at = lax.broadcasted_iota(jnp.int32, (rows, 1), 0)
    return lax.rem(at, WIDE) < 28


def spread(shifted, held, cells):
    for b in range(3):
        shifted[WIDE : WIDE + cells, b * 256 : (b + 1) * 256] = held[
            LEAD - 1 + b : LEAD - 1 + b + cells, :
        ].astype(BF)


def three_rows(shifted, start, rows):
    return jnp.concatenate(
        [shifted[start + a * WIDE : start + a * WIDE + rows, :] for a in range(3)], axis=1
    )


def clear_edges(shifted, helds, cells):
    shifted[0:WIDE, :] = jnp.zeros((WIDE, shifted.shape[1]), BF)
    shifted[WIDE + cells :, :] = jnp.zeros((WIDE, shifted.shape[1]), BF)
    for held in helds:
        held[0:LEAD, :] = jnp.zeros((LEAD, held.shape[1]), F32)
        held[LEAD + cells :, :] = jnp.zeros((held.shape[0] - LEAD - cells, held.shape[1]), F32)


def block_forward_kernel(
    row, image, weight, mean, var, scale, shift, proj, proj_bias, key_value,
    padded, hidden, block_out, slope_one, slope_two, norm_one, norm_two, memory, cross_kv,
    shifted, held_in, held_mid, raw, loose, sent, landed, load_sem, send_sem, land_sem, home_sem,
):
    table = pl.program_id(0)
    cells = padded.shape[1]
    half = cells // 2
    tables, batches, rows = landed.shape[0], image.shape[0], sent.shape[2]
    owned = tables // batches
    group = owned * row
    me = lax.axis_index("row")
    factor = lax.rsqrt(var[...] + EPS)
    mine = pl.ds(pl.multiple_of(me * rows, WIDE), rows)

    def exchange(t, d):
        peer = lax.rem(me + d, row)
        return pltpu.make_async_remote_copy(
            src_ref=sent.at[t, peer], dst_ref=landed.at[t, mine],
            send_sem=send_sem.at[t, d - 1], recv_sem=land_sem.at[t, d - 1],
            device_id={"row": peer}, device_id_type=MESH,
        )

    def keep(t):
        return pltpu.make_async_copy(sent.at[t, me], landed.at[t, mine], home_sem.at[t])

    def take_apart(b):
        gap = jnp.zeros((WIDE - 28, 128), F32)
        for h in range(2):
            lanes = slice(h * 128, (h + 1) * 128)
            loose[h] = raw[b, :, lanes].astype(F32)
            for g in range(group):
                for r in range(rows // WIDE):
                    line = loose[h, pl.ds(r * 28 * group + g, 28, stride=group), :]
                    line = jnp.concatenate([line, gap], axis=0).astype(BF)
                    sent[b * owned + g % owned, g // owned, r * WIDE : (r + 1) * WIDE, lanes] = line

    @pl.when(table == 0)
    def _():
        loads = [pltpu.make_async_copy(image.at[b], raw.at[b], load_sem.at[b]) for b in range(batches)]
        for copy in loads:
            copy.start()
        barrier = pltpu.get_barrier_semaphore()
        for d in range(1, row):
            pl.semaphore_signal(
                barrier, inc=1, device_id={"row": lax.rem(me + d, row)}, device_id_type=MESH
            )
        for b in range(batches):
            loads[b].wait()
            take_apart(b)
            if b == 0:
                pl.semaphore_wait(barrier, row - 1)
            for t in range(b * owned, (b + 1) * owned):
                for d in range(1, row):
                    exchange(t, d).start()
                keep(t).start()
        clear_edges(shifted, (held_in, held_mid), cells)

    for d in range(1, row):
        exchange(table, d).wait_recv()
    keep(table).wait()
    padded[0] = landed[table]
    held_in[LEAD : LEAD + cells, :] = landed[table].astype(F32)
    spread(shifted, held_in, cells)
    real = real_columns(half)
    for start in (0, half):
        pre = dot(three_rows(shifted, start, half), weight[0])
        norm = (pre - mean[0:1]) * factor[0:1]
        act, slope = gelu_pair(norm * scale[0:1] + shift[0:1])
        act = jnp.where(real, act, 0.0)
        held_mid[LEAD + start : LEAD + start + half, :] = act
        hidden[0, start : start + half, :] = act.astype(BF)
        slope_one[0, start : start + half, :] = jnp.where(real, slope, 0.0).astype(BF)
        norm_one[0, start : start + half, :] = norm.astype(BF)
    spread(shifted, held_mid, cells)
    for start in (0, half):
        pre = dot(three_rows(shifted, start, half), weight[1])
        norm = (pre - mean[1:2]) * factor[1:2]
        total = norm * scale[1:2] + shift[1:2] + held_in[LEAD + start : LEAD + start + half, :]
        act, slope = gelu_pair(total)
        block = act.astype(BF)
        block_out[0, start : start + half, :] = block
        slope_two[0, start : start + half, :] = slope.astype(BF)
        norm_two[0, start : start + half, :] = norm.astype(BF)
        tokens = (dot(block, proj[...]) + proj_bias[...]).astype(BF)
        memory[0, start : start + half, :] = tokens
        for k in range(2):
            cross_kv[0, start : start + half, k * 512 : (k + 1) * 512] = dot(
                tokens, key_value[k]
            ).astype(BF)

    @pl.when(table == tables - 1)
    def _():
        for t in range(tables):
            for d in range(1, row):
                exchange(t, d).wait_send()


def whole(*shape):
    zeros = (0,) * len(shape)
    return pl.BlockSpec(shape, lambda t: zeros)


def per_table(*shape):
    zeros = (0,) * len(shape)
    return pl.BlockSpec((1,) + shape, lambda t: (t,) + zeros)


def block_forward(image, weight, mean, var, scale, shift, proj, proj_bias, attn_in, row, group, part):
    batches, width = image.shape[0], image.shape[2]
    tables, cells = batches * (group // row), part * row * WIDE
    model = proj.shape[1]
    small = jax.ShapeDtypeStruct((tables, cells, width), BF)
    stats = [whole(2, width)] * 4
    return pl.pallas_call(
        functools.partial(block_forward_kernel, row),
        grid=(tables,),
        in_specs=[pl.BlockSpec(memory_space=pl.ANY), whole(*weight.shape)] + stats
        + [whole(*proj.shape), whole(1, model), pl.BlockSpec((2,) + attn_in.shape[1:], lambda t: (2, 0, 0))],
        out_specs=[per_table(cells, width)] * 7 + [per_table(cells, model), per_table(cells, 2 * model)],
        out_shape=[small] * 7 + [
            jax.ShapeDtypeStruct((tables, cells, model), BF),
            jax.ShapeDtypeStruct((tables, cells, 2 * model), BF),
        ],
        scratch_shapes=[
            pltpu.VMEM((cells + 2 * WIDE, 3 * width), BF),
            pltpu.VMEM((cells + 80, width), F32),
            pltpu.VMEM((cells + 80, width), F32),
            pltpu.VMEM(image.shape, BF),
            pltpu.VMEM((2, image.shape[1], 128), F32),
            pltpu.VMEM((tables, row, part * WIDE, width), BF),
            pltpu.VMEM((tables, cells, width), BF),
            pltpu.SemaphoreType.DMA((batches,)),
            pltpu.SemaphoreType.DMA((tables, row - 1)),
            pltpu.SemaphoreType.DMA((tables, row - 1)),
            pltpu.SemaphoreType.DMA((tables,)),
        ],
        compiler_params=pltpu.CompilerParams(
            vmem_limit_bytes=56 * MIB, collective_id=1, has_side_effects=True
        ),
        name="block_forward",
    )(image, weight, mean, var, scale, shift, proj, proj_bias, attn_in)


def block_backward_kernel(
    grad_tokens, padded, hidden, block_out, slope_one, slope_two, norm_one, norm_two,
    weight, var, scale, proj,
    image_grad, grads, bn_sums, proj_bias_grad,
    shifted, held, kept, weight_back, conv_sum, proj_sum, bn_sum, bias_sum,
):
    step = pl.program_id(0)
    cells = padded.shape[1]
    half = cells // 2
    gain = lax.rsqrt(var[...] + EPS) * scale[...]

    @pl.when(step == 0)
    def _():
        clear_edges(shifted, (held,), cells)
        conv_sum[...] = jnp.zeros_like(conv_sum)
        proj_sum[...] = jnp.zeros_like(proj_sum)
        bn_sum[...] = jnp.zeros_like(bn_sum)
        bias_sum[...] = jnp.zeros_like(bias_sum)
        for layer in range(2):
            for tap in range(9):
                turned = weight[layer, tap * 256 : (tap + 1) * 256, :].T
                weight_back[layer, (8 - tap) * 256 : (9 - tap) * 256, :] = turned

    def add_stats(layer, grad, norm):
        bn_sum[layer : layer + 1, :] += jnp.sum(grad * norm.astype(F32), axis=0, keepdims=True)
        bn_sum[2 + layer : 3 + layer, :] += jnp.sum(grad, axis=0, keepdims=True)

    def add_conv(layer, inputs):
        turned = inputs.T
        for a in range(3):
            start = (2 - a) * WIDE
            found = dot(turned, shifted[start : start + cells, :])
            for b in range(3):
                conv_sum[layer, a, b] += found[:, (2 - b) * 256 : (3 - b) * 256]

    proj_sum[...] += dot_tn(block_out[0], grad_tokens[0])
    bias_sum[...] += jnp.sum(grad_tokens[0].astype(F32), axis=0, keepdims=True)
    for start in (0, half):
        part = slice(start, start + half)
        grad = slope_two[0, part, :].astype(F32) * dot_nt(grad_tokens[0, part, :], proj[...])
        kept[part, :] = grad
        add_stats(1, grad, norm_two[0, part, :])
        held[LEAD + start : LEAD + start + half, :] = grad * gain[1:2]
    spread(shifted, held, cells)
    for start in (0, half):
        part = slice(start, start + half)
        back = dot(three_rows(shifted, start, half), weight_back[1])
        grad = slope_one[0, part, :].astype(F32) * back
        add_stats(0, grad, norm_one[0, part, :])
        held[LEAD + start : LEAD + start + half, :] = grad * gain[0:1]
    add_conv(1, hidden[0])
    spread(shifted, held, cells)
    for start in (0, half):
        back = dot(three_rows(shifted, start, half), weight_back[0]) + kept[start : start + half, :]
        image_grad[0, start : start + half, :] = back.astype(BF)
    add_conv(0, padded[0])

    @pl.when(step == pl.num_programs(0) - 1)
    def _():
        for a in range(3):
            for b in range(3):
                rows = slice((3 * a + b) * 256, (3 * a + b + 1) * 256)
                for layer in range(2):
                    grads[rows, layer * 256 : (layer + 1) * 256] = conv_sum[layer, a, b].astype(BF)
        grads[9 * 256 :, :] = proj_sum[...].astype(BF)
        bn_sums[...] = bn_sum[...]
        proj_bias_grad[...] = bias_sum[...]


def block_backward(
    grad_tokens, padded, hidden, block_out, slope_one, slope_two, norm_one, norm_two,
    weight, var, scale, proj,
):
    tables, cells, model = grad_tokens.shape
    width = proj.shape[0]
    per = per_table(cells, width)
    conv_shape = (2, 3, 3, width, width)
    return pl.pallas_call(
        block_backward_kernel,
        grid=(tables,),
        in_specs=[per_table(cells, model)] + [per] * 7
        + [whole(*weight.shape)] + [whole(2, width)] * 2 + [whole(*proj.shape)],
        out_specs=[
            per, whole(10 * width, model), whole(4, width), whole(1, model),
        ],
        out_shape=[
            jax.ShapeDtypeStruct((tables, cells, width), BF),
            jax.ShapeDtypeStruct((10 * width, model), BF),
            jax.ShapeDtypeStruct((4, width), F32),
            jax.ShapeDtypeStruct((1, model), F32),
        ],
        scratch_shapes=[
            pltpu.VMEM((cells + 2 * WIDE, 3 * width), BF),
            pltpu.VMEM((cells + 80, width), F32),
            pltpu.VMEM((cells, width), F32),
            pltpu.VMEM(weight.shape, BF),
            pltpu.VMEM(conv_shape, F32),
            pltpu.VMEM(proj.shape, F32),
            pltpu.VMEM((4, width), F32),
            pltpu.VMEM((1, model), F32),
        ],
        compiler_params=pltpu.CompilerParams(vmem_limit_bytes=56 * MIB),
        name="block_backward",
    )(
        grad_tokens, padded, hidden, block_out, slope_one, slope_two, norm_one, norm_two,
        weight, var, scale, proj,
    )


def lane_masks(rows, lanes):
    at = lax.broadcasted_iota(jnp.int32, (rows, lanes), 1) // 64
    return [at == h for h in range(GROUP)]


def by_head(value, masks):
    zero = jnp.zeros_like(value)
    return jnp.concatenate([jnp.where(m, value, zero) for m in masks], axis=0)


def own_lanes(stacked, masks):
    rows = stacked.shape[0] // GROUP
    total = stacked[0:rows]
    for h in range(1, GROUP):
        total = jnp.where(masks[h], stacked[h * rows : (h + 1) * rows], total)
    return total


def softmax_rows(scores):
    raised = jnp.exp(scores - jnp.max(scores, axis=-1, keepdims=True))
    return raised * (1.0 / jnp.sum(raised, axis=-1, keepdims=True))


def normalise(value):
    center = value - jnp.mean(value, axis=-1, keepdims=True)
    inverse = lax.rsqrt(jnp.mean(center * center, axis=-1, keepdims=True) + EPS)
    return center * inverse, inverse


def norm_back(upstream, gain, unit, inverse):
    scaled = upstream * gain
    mean = jnp.mean(scaled, axis=-1, keepdims=True)
    along = jnp.mean(scaled * unit, axis=-1, keepdims=True)
    return inverse * (scaled - mean - unit * along)


def column_sum(value):
    return jnp.sum(value, axis=0, keepdims=True)


def decoder_kernel(
    lengths, ln_gain, ln_bias, ffn_in_bias, ffn_out_bias,
    tags_far, cotangent_far, memory_far, cross_kv_far, attn_in_far, attn_out_far, ffn_in_far, ffn_out_far,
    decoded, tags_grad, grad_tokens, grads_far,
    ln_gain_grad, ln_bias_grad, ffn_in_bias_grad, ffn_out_bias_grad,
    tags, cotangent, memory, cross_kv, attn_in, attn_out, ffn_in, ffn_out,
    qkv, mix, self_shares, cross_shares, cross_q, up, grad_qkv, grad_q, grad_kv, pair_sum,
    staged, weight_sem, kv_sem, memory_sem, staged_sem,
    grads, grad_sem,
):
    tables, cells = memory_far.shape[0], memory_far.shape[1]
    slots = tags.shape[0] // tables

    def fetch_kv(t):
        return pltpu.make_async_copy(cross_kv_far.at[t], cross_kv.at[t], kv_sem.at[t])

    def fetch_memory(t):
        slot = lax.rem(t, 2)
        return pltpu.make_async_copy(memory_far.at[t], memory.at[slot], memory_sem.at[slot])

    def put_tokens(t):
        slot = lax.rem(t, 2)
        return pltpu.make_async_copy(staged.at[slot], grad_tokens.at[t], staged_sem.at[slot])

    fetches = [
        pltpu.make_async_copy(far, near, weight_sem.at[i])
        for i, (far, near) in enumerate(
            [(tags_far, tags)]
            + [(attn_in_far.at[k], attn_in.at[k]) for k in range(4)]
            + [(attn_out_far, attn_out), (cotangent_far, cotangent)]
            + [(ffn_in_far, ffn_in), (ffn_out_far, ffn_out)]
            + [(attn_in_far.at[k], attn_in.at[k]) for k in (4, 5)]
        )
    ]
    for copy in fetches[:6]:
        copy.start()
    for t in range(tables):
        fetch_kv(t).start()
    for copy in fetches[6:]:
        copy.start()
    fetch_memory(0).start()
    half = 256
    wide_f32 = lane_masks(slots, half)
    real_key = lax.rem(lax.broadcasted_iota(jnp.int32, (GROUP * slots, cells), 1), WIDE) < 28

    def allowed_of(t):
        row = lax.broadcasted_iota(jnp.int32, (slots, slots), 0)
        col = lax.broadcasted_iota(jnp.int32, (slots, slots), 1)
        once = (col <= row) & (col < lengths[t])
        return jnp.concatenate([once] * GROUP, axis=0)

    def put_grad(i, value):
        grads[i] = value.astype(BF)
        copy = pltpu.make_async_copy(grads.at[i], grads_far.at[i], grad_sem.at[i])
        copy.start()
        puts.append(copy)

    puts = []
    fetches[0].wait()
    for k in range(3):
        fetches[1 + k].wait()
        qkv[k] = dot(tags[...], attn_in[k]).astype(BF)

    def self_forward(t, carry):
        rows = pl.ds(pl.multiple_of(t * slots, slots), slots)
        allowed = allowed_of(t)
        for g in range(2):
            lanes = slice(g * half, (g + 1) * half)
            query = by_head(qkv[0, rows, lanes], wide_f32)
            scores = dot_nt(query, qkv[1, rows, lanes]) * 0.125
            shares = softmax_rows(jnp.where(allowed, scores, MASKED)).astype(BF)
            self_shares[t, g] = shares
            mix[0, rows, lanes] = own_lanes(dot(shares, qkv[2, rows, lanes]), wide_f32).astype(BF)
        return carry

    lax.fori_loop(0, tables, self_forward, 0)
    fetches[5].wait()
    first_unit, first_inv = normalise(tags[...].astype(F32) + dot(mix[0], attn_out[0]))
    first = first_unit * ln_gain[0:1] + ln_bias[0:1]
    first_low = first.astype(BF)
    fetches[4].wait()
    cross_q[...] = dot(first_low, attn_in[3]).astype(BF)

    def cross_forward(t, carry):
        fetch_kv(t).wait()
        rows = pl.ds(pl.multiple_of(t * slots, slots), slots)
        for g in range(2):
            lanes = slice(g * half, (g + 1) * half)
            query = by_head(cross_q[rows, lanes], wide_f32)
            scores = dot_nt(query, cross_kv[t, :, lanes]) * 0.125
            shares = softmax_rows(jnp.where(real_key, scores, MASKED)).astype(BF)
            cross_shares[t, g] = shares
            value = cross_kv[t, :, 512 + g * half : 512 + (g + 1) * half]
            mix[1, rows, lanes] = own_lanes(dot(shares, value), wide_f32).astype(BF)
        return carry

    lax.fori_loop(0, tables, cross_forward, 0)
    second_unit, second_inv = normalise(first + dot(mix[1], attn_out[1]))
    second = second_unit * ln_gain[1:2] + ln_bias[1:2]
    second_low = second.astype(BF)
    for copy in fetches[6:]:
        copy.wait()
    act, slope = gelu_pair(dot(second_low, ffn_in[...]) + ffn_in_bias[...])
    inner_act = act.astype(BF)
    third_unit, third_inv = normalise(second + dot(inner_act, ffn_out[...]) + ffn_out_bias[...])
    decoded[...] = (third_unit * ln_gain[2:3] + ln_bias[2:3]).astype(BF)

    up_three = cotangent[...].astype(F32)
    ln_gain_grad[2:3, :] = column_sum(up_three * third_unit)
    ln_bias_grad[2:3, :] = column_sum(up_three)
    grad_third = norm_back(up_three, ln_gain[2:3], third_unit, third_inv)
    grad_outer = grad_third.astype(BF)
    ffn_out_total = dot_tn(inner_act, grad_outer)
    for k in range(2):
        put_grad(8 + k, ffn_out_total[k * 512 : (k + 1) * 512])
    ffn_out_bias_grad[...] = column_sum(grad_outer.astype(F32))
    grad_inner = (slope * dot_nt(grad_outer, ffn_out[...])).astype(BF)
    ffn_in_total = dot_tn(second_low, grad_inner)
    for k in range(2):
        put_grad(10 + k, ffn_in_total[:, k * 512 : (k + 1) * 512])
    ffn_in_bias_grad[...] = column_sum(grad_inner.astype(F32))
    up_two = grad_third + dot_nt(grad_inner, ffn_in[...])
    ln_gain_grad[1:2, :] = column_sum(up_two * second_unit)
    ln_bias_grad[1:2, :] = column_sum(up_two)
    grad_second = norm_back(up_two, ln_gain[1:2], second_unit, second_inv)
    grad_cross_out = grad_second.astype(BF)
    put_grad(7, dot_tn(mix[1], grad_cross_out))
    up[...] = dot_nt(grad_cross_out, attn_out[1]).astype(BF)
    pair_sum[...] = jnp.zeros_like(pair_sum)

    def cross_back(t, carry):
        @pl.when(t + 1 < tables)
        def _():
            fetch_memory(t + 1).start()

        rows = pl.ds(pl.multiple_of(t * slots, slots), slots)
        for g in range(2):
            lanes = slice(g * half, (g + 1) * half)
            value_lanes = slice(512 + g * half, 512 + (g + 1) * half)
            query = by_head(cross_q[rows, lanes], wide_f32)
            upstream = by_head(up[rows, lanes], wide_f32)
            low = cross_shares[t, g]
            shares = low.astype(F32)
            grad_shares = dot_nt(upstream, cross_kv[t, :, value_lanes])
            mean = jnp.sum(grad_shares * shares, axis=-1, keepdims=True)
            grad_scores = (shares * (grad_shares - mean)).astype(BF)
            grad_q[rows, lanes] = (
                own_lanes(dot(grad_scores, cross_kv[t, :, lanes]), wide_f32) * 0.125
            ).astype(BF)
            grad_kv[:, lanes] = (dot_tn(grad_scores, query) * 0.125).astype(BF)
            grad_kv[:, value_lanes] = dot_tn(low, upstream).astype(BF)
        @pl.when(t >= 2)
        def _():
            put_tokens(t - 2).wait()

        slot = lax.rem(t, 2)
        staged[slot] = (
            dot_nt(grad_kv[:, 0:512], attn_in[4]) + dot_nt(grad_kv[:, 512:1024], attn_in[5])
        ).astype(BF)
        put_tokens(t).start()
        fetch_memory(t).wait()
        pair_sum[...] += dot_tn(memory[slot], grad_kv[...])
        return carry

    lax.fori_loop(0, tables, cross_back, 0)
    for t in range(max(tables - 2, 0), tables):
        put_tokens(t).wait()
    for k in range(2):
        put_grad(4 + k, pair_sum[:, k * 512 : (k + 1) * 512])
    put_grad(3, dot_tn(first_low, grad_q[...]))
    up_one = grad_second + dot_nt(grad_q[...], attn_in[3])
    ln_gain_grad[0:1, :] = column_sum(up_one * first_unit)
    ln_bias_grad[0:1, :] = column_sum(up_one)
    grad_first = norm_back(up_one, ln_gain[0:1], first_unit, first_inv)
    grad_self_out = grad_first.astype(BF)
    put_grad(6, dot_tn(mix[0], grad_self_out))
    up[...] = dot_nt(grad_self_out, attn_out[0]).astype(BF)

    def self_back(t, carry):
        rows = pl.ds(pl.multiple_of(t * slots, slots), slots)
        for g in range(2):
            lanes = slice(g * half, (g + 1) * half)
            query = by_head(qkv[0, rows, lanes], wide_f32)
            upstream = by_head(up[rows, lanes], wide_f32)
            low = self_shares[t, g]
            shares = low.astype(F32)
            grad_shares = dot_nt(upstream, qkv[2, rows, lanes])
            mean = jnp.sum(grad_shares * shares, axis=-1, keepdims=True)
            grad_scores = (shares * (grad_shares - mean)).astype(BF)
            grad_qkv[0, rows, lanes] = (
                own_lanes(dot(grad_scores, qkv[1, rows, lanes]), wide_f32) * 0.125
            ).astype(BF)
            grad_qkv[1, rows, lanes] = (dot_tn(grad_scores, query) * 0.125).astype(BF)
            grad_qkv[2, rows, lanes] = dot_tn(low, upstream).astype(BF)
        return carry

    lax.fori_loop(0, tables, self_back, 0)
    total = grad_first
    for k in range(3):
        put_grad(k, dot_tn(tags[...], grad_qkv[k]))
        total = total + dot_nt(grad_qkv[k], attn_in[k])
    tags_grad[...] = total
    for copy in puts:
        copy.wait()


def decoder(
    lengths, tags, cotangent, memory, cross_kv, attn_in, attn_out, ln_gain, ln_bias,
    ffn_in, ffn_in_bias, ffn_out, ffn_out_bias,
):
    tables, cells, model = memory.shape
    rows = tags.shape[0]
    slots = rows // tables
    inner = ffn_in.shape[1]
    here = pl.BlockSpec(memory_space=pltpu.VMEM)
    far = pl.BlockSpec(memory_space=pl.ANY)
    shape = jax.ShapeDtypeStruct
    stacked = GROUP * slots
    return pl.pallas_call(
        decoder_kernel,
        in_specs=[pl.BlockSpec(memory_space=pltpu.SMEM)] + [here] * 4 + [far] * 8,
        out_specs=[here] * 2 + [far] * 2 + [here] * 4,
        out_shape=[
            shape((rows, model), BF), shape((rows, model), F32), shape((tables, cells, model), BF),
            shape((12, 512, model), BF), shape((3, model), F32), shape((3, model), F32),
            shape((1, inner), F32), shape((1, model), F32),
        ],
        scratch_shapes=[
            pltpu.VMEM((rows, model), BF),
            pltpu.VMEM((rows, model), BF),
            pltpu.VMEM((2, cells, model), BF),
            pltpu.VMEM((tables, cells, 2 * model), BF),
            pltpu.VMEM(attn_in.shape, BF),
            pltpu.VMEM(attn_out.shape, BF),
            pltpu.VMEM(ffn_in.shape, BF),
            pltpu.VMEM(ffn_out.shape, BF),
            pltpu.VMEM((3, rows, model), BF),
            pltpu.VMEM((2, rows, model), BF),
            pltpu.VMEM((tables, 2, stacked, slots), BF),
            pltpu.VMEM((tables, 2, stacked, cells), BF),
            pltpu.VMEM((rows, model), BF),
            pltpu.VMEM((rows, model), BF),
            pltpu.VMEM((3, rows, model), BF),
            pltpu.VMEM((rows, model), BF),
            pltpu.VMEM((cells, 2 * model), BF),
            pltpu.VMEM((model, 2 * model), F32),
            pltpu.VMEM((2, cells, model), BF),
            pltpu.SemaphoreType.DMA((11,)),
            pltpu.SemaphoreType.DMA((tables,)),
            pltpu.SemaphoreType.DMA((2,)),
            pltpu.SemaphoreType.DMA((2,)),
            pltpu.VMEM((12, 512, model), BF),
            pltpu.SemaphoreType.DMA((12,)),
        ],
        compiler_params=pltpu.CompilerParams(vmem_limit_bytes=60 * MIB),
        name="decoder",
    )(
        lengths, ln_gain, ln_bias, ffn_in_bias, ffn_out_bias,
        tags, cotangent, memory, cross_kv, attn_in, attn_out, ffn_in, ffn_out,
    )


def orders(dp, row):
    row_bits = [("row", 1 << i) for i in range(row.bit_length() - 1)]
    dp_bits = [("dp", 1 << i) for i in range(dp.bit_length() - 1)]
    pair, others = row_bits[:1], row_bits[1:]
    near, far = dp_bits[:1], dp_bits[1:]
    return [pair + near + others + far, pair + others + near + far, pair + far + near + others]


def plan_of(units):
    turn = (0, 2, 1) * 4 + (0, 2, 0, 0, 0)
    return [(turn[i % len(turn)], i, 1) for i in range(units)]


def side_of(axis, bit):
    return lax.rem(lax.axis_index(axis) // bit, 2)


def partner_of(axis, bit):
    return {axis: lax.axis_index(axis) + bit * (1 - 2 * side_of(axis, bit))}


def add_rows(target, held, start, landed, at, rows):
    step = 128
    while rows % step:
        step //= 2

    def one(i, carry):
        here = pl.ds(pl.multiple_of(start + i * step, 16), step)
        there = pl.ds(pl.multiple_of(at + i * step, 16), step)
        target[here, :] = held[here, :] + landed[there, :]
        return carry

    lax.fori_loop(0, rows // step, one, 0)


def reduce_kernel(plan, streams, unit, sizes, row, *refs):
    count = len(sizes)
    parts, image_grad, smalls, refs = refs[:count], refs[count], refs[count + 1 : count + 7], refs[count + 7 :]
    total, small_total, image_back = refs[:3]
    held, landed, done, small_held, small_landed = refs[3:8]
    load_sem, send_sem, land_sem, back_sem, home_sem = refs[8:13]
    small_send, small_land, out_sem, image_send, image_land, image_sem = refs[13:]
    stages = len(streams[0])
    rows_all = sum(sizes)
    bounds = [sum(sizes[:i]) for i in range(count + 1)]
    loads = [
        pltpu.make_async_copy(part, held.at[pl.ds(bounds[i], sizes[i]), :], load_sem.at[i])
        for i, part in enumerate(parts)
    ]
    for copy in loads:
        copy.start()
    barrier = pltpu.get_barrier_semaphore()
    me = lax.axis_index("row")
    peers = [{"row": lax.rem(me + d, row)} for d in range(1, row)]
    across = [partner_of(axis, bit) for axis, bit in streams[0] if axis == "dp"]
    for device in peers + across:
        pl.semaphore_signal(barrier, inc=1, device_id=device, device_id_type=MESH)
    pl.semaphore_wait(barrier, len(peers) + len(across))
    owned, rows = image_back.shape[1] // row, image_back.shape[2]
    images = []
    for t in range(image_grad.shape[0]):
        target = image_back.at[t // owned, me * owned + t % owned]
        for d in range(1, row):
            peer = lax.rem(me + d, row)
            images.append(pltpu.make_async_remote_copy(
                src_ref=image_grad.at[t, pl.ds(pl.multiple_of(peer * rows, WIDE), rows)], dst_ref=target,
                send_sem=image_send.at[t, d - 1], recv_sem=image_land.at[t, d - 1],
                device_id={"row": peer}, device_id_type=MESH,
            ))
        images.append(pltpu.make_async_copy(
            image_grad.at[t, pl.ds(pl.multiple_of(me * rows, WIDE), rows)], target, image_sem.at[t],
        ))
    for copy in images:
        copy.start()
    bn, proj_bias, gain, bias, ffn_in_bias, ffn_out_bias = smalls
    small_held[0] = jnp.concatenate([
        jnp.concatenate([bn[0:2, :], bn[2:4, :]], axis=1), proj_bias[...], ffn_out_bias[...],
        ffn_in_bias[:, 0:512], ffn_in_bias[:, 512:1024], jnp.zeros((2, 512), F32),
        gain[...], bias[...], jnp.zeros((2, 512), F32),
    ], axis=0)
    loaded = [False] * count

    def need(first, last):
        for i in range(count):
            if bounds[i] < last and bounds[i + 1] > first and not loaded[i]:
                loads[i].wait()
                loaded[i] = True

    state = [dict(start=first * unit, rows=n * unit, at=0) for _, first, n in plan]
    flights, backs, outs = {}, {}, []

    def small_step(s):
        if s > 0:
            flights["small", s - 1].wait()
            both = small_held[s - 1] + small_landed[s - 1]
            if s == stages:
                small_total[...] = both
                return
            small_held[s] = both
        axis, bit = streams[0][s]
        copy = pltpu.make_async_remote_copy(
            src_ref=small_held.at[s], dst_ref=small_landed.at[s],
            send_sem=small_send.at[s], recv_sem=small_land.at[s],
            device_id=partner_of(axis, bit), device_id_type=MESH,
        )
        copy.start()
        flights["small", s] = copy

    def collect(c, s, target):
        _, first, n = plan[c]
        now = state[c]
        flights[c, s].wait_recv()
        add_rows(target, held, now["start"], landed, first * unit + now["at"], now["rows"])
        now["at"] += now["rows"]

    def split(c, s):
        stream, first, n = plan[c]
        now = state[c]
        axis, bit = streams[stream][s]
        if s == 0:
            need(first * unit, (first + n) * unit)
        else:
            collect(c, s - 1, held)
        half = now["rows"] // 2
        side = side_of(axis, bit)
        base = now["start"]
        copy = pltpu.make_async_remote_copy(
            src_ref=held.at[pl.ds(pl.multiple_of(base + (1 - side) * half, 16), half), :],
            dst_ref=landed.at[pl.ds(first * unit + now["at"], half), :],
            send_sem=send_sem.at[c, s], recv_sem=land_sem.at[c, s],
            device_id=partner_of(axis, bit), device_id_type=MESH,
        )
        copy.start()
        flights[c, s] = copy
        now["start"] = base + side * half
        now["rows"] = half

    def merge(c, s):
        stream, first, n = plan[c]
        now = state[c]
        axis, bit = streams[stream][s]
        if s == stages - 1:
            collect(c, s, done)
        else:
            backs[c, s + 1].wait_recv()
            now["rows"] *= 2
            now["start"] = now["start"] - side_of(*streams[stream][s + 1]) * (now["rows"] // 2)
        region = done.at[pl.ds(pl.multiple_of(now["start"], 16), now["rows"]), :]
        copy = pltpu.make_async_remote_copy(
            src_ref=region, dst_ref=region,
            send_sem=back_sem.at[c, s], recv_sem=home_sem.at[c, s],
            device_id=partner_of(axis, bit), device_id_type=MESH,
        )
        copy.start()
        backs[c, s] = copy

    def finish(c):
        _, first, n = plan[c]
        backs[c, 0].wait_recv()
        last = min((first + n) * unit, rows_all)
        if last > first * unit:
            region = pl.ds(first * unit, last - first * unit)
            copy = pltpu.make_async_copy(done.at[region, :], total.at[region, :], out_sem.at[c])
            copy.start()
            outs.append(copy)

    lags, seen = [], {}
    for stream, _, _ in plan:
        lags.append(seen.get(stream, 0))
        seen[stream] = lags[-1] + 1
    for turn in range(2 * stages + 1 + max(lags)):
        if turn <= stages:
            small_step(turn)
        for c, lag in reversed(list(enumerate(lags))):
            k = turn - lag
            if 0 <= k < stages:
                split(c, k)
            elif stages <= k < 2 * stages:
                merge(c, 2 * stages - 1 - k)
            elif k == 2 * stages:
                finish(c)
    for c in range(len(plan)):
        for s in range(stages):
            flights[c, s].wait_send()
            backs[c, s].wait_send()
    for copy in outs + images:
        copy.wait()


def reduce_all(parts, image_grad, smalls, dp, row, batches):
    streams = orders(dp, row)
    stages = len(streams[0])
    sizes = [p.shape[0] for p in parts]
    rows, width = sum(sizes), parts[0].shape[1]
    unit = 16 * dp * row
    plan = plan_of(-(-rows // unit))
    chunks = len(plan)
    tables, cells, channels = image_grad.shape
    back = (batches, tables // batches * row, cells // row, channels)
    small = (16, width)
    far = pl.BlockSpec(memory_space=pl.ANY)
    near = pl.BlockSpec(memory_space=pltpu.VMEM)
    sem = pltpu.SemaphoreType.DMA
    return pl.pallas_call(
        functools.partial(reduce_kernel, plan, streams, unit, sizes, row),
        in_specs=[far] * (len(parts) + 1) + [near] * len(smalls),
        out_specs=[far, near, far],
        out_shape=[
            jax.ShapeDtypeStruct((rows, width), BF),
            jax.ShapeDtypeStruct(small, F32),
            jax.ShapeDtypeStruct(back, BF),
        ],
        scratch_shapes=[
            pltpu.VMEM((chunks * unit, width), BF),
            pltpu.VMEM((chunks * unit, width), BF),
            pltpu.VMEM((chunks * unit, width), BF),
            pltpu.VMEM((stages,) + small, F32),
            pltpu.VMEM((stages,) + small, F32),
            sem((len(parts),)), sem((chunks, stages)), sem((chunks, stages)),
            sem((chunks, stages)), sem((chunks, stages)),
            sem((stages,)), sem((stages,)), sem((chunks,)),
            sem((tables, row - 1)), sem((tables, row - 1)), sem((tables,)),
        ],
        compiler_params=pltpu.CompilerParams(
            vmem_limit_bytes=60 * MIB, collective_id=0, has_side_effects=True
        ),
        name="reduce_all",
    )(*parts, image_grad, *smalls)


def widen_kernel(
    small, total, back, conv, proj, attn_in, attn_out, ffn_in, ffn_out, image_grad,
    bn_scale, bn_shift, proj_bias, gain, bias, ffn_in_bias, ffn_out_bias,
    narrow, wide, narrow_image, wide_image, in_sem, out_sem, image_in, image_out,
):
    units = in_sem.shape[0]
    batches, group = back.shape[0], back.shape[1]

    def rows(i):
        return pl.ds(i * 512, 512)

    fetches = [
        pltpu.make_async_copy(total.at[rows(i)], narrow.at[rows(i)], in_sem.at[i]) for i in range(units)
    ]
    images = [(b, g) for b in range(batches) for g in range(group)]
    image_fetches = [
        pltpu.make_async_copy(back.at[b, g], narrow_image.at[i], image_in.at[i])
        for i, (b, g) in enumerate(images)
    ]
    for copy in fetches + image_fetches:
        copy.start()
    bn_scale[...] = small[0:2, 0:256]
    bn_shift[...] = small[0:2, 256:512]
    proj_bias[...] = small[2:3, :]
    ffn_out_bias[...] = small[3:4, :]
    ffn_in_bias[:, 0:512] = small[4:5, :]
    ffn_in_bias[:, 512:1024] = small[5:6, :]
    gain[...] = small[8:11, :]
    bias[...] = small[11:14, :]
    slots = wide.shape[0]
    targets = [attn_in.at[i] for i in range(6)] + [attn_out.at[i] for i in range(2)]
    targets += [ffn_out.at[rows(i)] for i in range(2)]
    targets += [ffn_in.at[:, pl.ds(i * 512, 512)] for i in range(2)]
    pending = []

    def put(i, pairs):
        copies = [
            pltpu.make_async_copy(source, target, out_sem.at[i % slots, j])
            for j, (source, target) in enumerate(pairs)
        ]
        for copy in copies:
            copy.start()
        pending.append(copies)

    for i in range(units):
        fetches[i].wait()
        if i >= slots:
            for copy in pending[i - slots]:
                copy.wait()
        slot = wide.at[i % slots]
        slot[...] = narrow[rows(i), :].astype(F32)
        if i < 12:
            put(i, [(slot, targets[i])])
            continue
        pairs = []
        for half in range(2):
            tap = 2 * (i - 12) + half
            here = pl.ds(half * 256, 256)
            if tap < 9:
                for layer in range(2):
                    lanes = pl.ds(layer * 256, 256)
                    pairs.append((slot.at[here, lanes], conv.at[layer, tap // 3, tap % 3]))
            else:
                pairs.append((slot.at[here], proj))
        put(i, pairs)
    waits = []
    for b in range(batches):
        for g in range(group):
            image_fetches[b * group + g].wait()
            for r in range(back.shape[2] // WIDE):
                line = narrow_image[b * group + g, r * WIDE : (r + 1) * WIDE, :].astype(F32)
                for h in range(2):
                    lanes = slice(h * 128, (h + 1) * 128)
                    wide_image[b, h, pl.ds(r * 28 * group + g, 28, stride=group), :] = line[0:28, lanes]
        for h in range(2):
            waits.append(pltpu.make_async_copy(
                wide_image.at[b, h], image_grad.at[b, :, pl.ds(h * 128, 128)], image_out.at[b, h]
            ))
            waits[-1].start()
    for copies in pending[-slots:] + [waits]:
        for copy in copies:
            copy.wait()


def widen(small, total, back, image_shape, width, model, inner):
    rows = total.shape[0]
    units = rows // 512
    batches, group = back.shape[:2]
    far = pl.BlockSpec(memory_space=pl.ANY)
    near = pl.BlockSpec(memory_space=pltpu.VMEM)
    sem = pltpu.SemaphoreType.DMA
    shapes = [
        (2, 3, 3, width, width), (width, model), (6, model, model), (2, model, model),
        (model, inner), (inner, model), image_shape,
    ]
    small_shapes = [(2, width)] * 2 + [(1, model), (3, model), (3, model), (1, inner), (1, model)]
    return pl.pallas_call(
        widen_kernel,
        in_specs=[near] + [far] * 2,
        out_specs=[far] * 7 + [near] * 7,
        out_shape=[jax.ShapeDtypeStruct(s, F32) for s in shapes + small_shapes],
        scratch_shapes=[
            pltpu.VMEM((rows, model), BF),
            pltpu.VMEM((4, 512, model), F32),
            pltpu.VMEM((batches * group,) + back.shape[2:], BF),
            pltpu.VMEM((batches, 2, image_shape[1], 128), F32),
            sem((units,)), sem((4, 4)), sem((batches * group,)), sem((batches, 2)),
        ],
        compiler_params=pltpu.CompilerParams(vmem_limit_bytes=60 * MIB),
        name="widen",
    )(small, total, back)


def body(
    image, tags, tag_lengths, cotangent, conv_weight, bn_mean, bn_var, bn_scale, bn_shift,
    proj_weight, proj_bias, attn_in, attn_out, ln_gain, ln_bias,
    ffn_in, ffn_in_bias, ffn_out, ffn_out_bias,
):
    batches, owned, slots, model = tags.shape
    width = image.shape[-1]
    tables = batches * owned
    row = lax.axis_size("row")
    group, part, breadth = image.shape[1:4]
    flat_image = image.transpose(0, 2, 3, 1, 4).reshape(batches, part * breadth * group, width)
    weight = conv_weight.reshape(2, 9 * width, width)
    forward = block_forward(
        flat_image, weight, bn_mean, bn_var, bn_scale, bn_shift,
        proj_weight, proj_bias.reshape(1, -1), attn_in, row, group, part,
    )
    padded, hidden, block_out, slope_one, slope_two, norm_one, norm_two, memory, cross_kv = forward
    decoded, tags_grad, grad_tokens, decoder_g, gain_g, bias_g, ffn_in_bias_g, ffn_out_bias_g = decoder(
        tag_lengths.reshape(-1), tags.reshape(-1, model), cotangent.reshape(-1, model),
        memory, cross_kv, attn_in, attn_out, ln_gain, ln_bias,
        ffn_in, ffn_in_bias.reshape(1, -1), ffn_out, ffn_out_bias.reshape(1, -1),
    )
    image_grad, block_g, bn_g, proj_bias_g = block_backward(
        grad_tokens, padded, hidden, block_out, slope_one, slope_two, norm_one, norm_two,
        weight, bn_var, bn_scale, proj_weight,
    )
    total, small, back = reduce_all(
        (decoder_g.reshape(-1, model), block_g), image_grad,
        (bn_g, proj_bias_g, gain_g, bias_g, ffn_in_bias_g, ffn_out_bias_g),
        lax.axis_size("dp"), row, batches,
    )
    (
        conv_g, proj_g, attn_in_g, attn_out_g, ffn_in_g, ffn_out_g, image_g,
        bn_scale_g, bn_shift_g, proj_bias_g, gain_g, bias_g, ffn_in_bias_g, ffn_out_bias_g,
    ) = widen(small, total, back, flat_image.shape, width, model, ffn_in.shape[1])
    image_g = image_g.reshape(batches, part, breadth, group, width).transpose(0, 3, 1, 2, 4)
    return (
        decoded.reshape(tags.shape), image_g, tags_grad.reshape(tags.shape),
        conv_g, bn_scale_g, bn_shift_g, proj_g, proj_bias_g.reshape(-1),
        attn_in_g, attn_out_g, gain_g, bias_g,
        ffn_in_g, ffn_in_bias_g.reshape(-1), ffn_out_g, ffn_out_bias_g.reshape(-1),
    )


def solution(mesh):
    by_rows = P(None, "dp", "row", None, None)
    by_table = P(None, ("dp", "row"), None, None)
    return jax.shard_map(
        body,
        mesh=mesh,
        in_specs=(by_rows, by_table, P(None, ("dp", "row")), by_table) + (P(),) * 15,
        out_specs=(by_table, by_rows, by_table) + (P(),) * 13,
        check_vma=False,
    )
```

```python
import functools

import jax
import jax.numpy as jnp
from jax import lax
from jax.experimental import pallas as pl
from jax.experimental.pallas import tpu as pltpu
from jax.sharding import PartitionSpec as P

HEADS = 8
GROUP = 4
EPS = 1e-05
MASKED = -1e30
BF = jnp.bfloat16
F32 = jnp.float32
WIDE = 32
LEAD = 40
SLOTS = 5
PITCH = 3
SIZE = 1
EARLY = (0, 2, 1, 0, 1)
LATE = (0, 2, 1, 0, 1)
MIB = 1024 * 1024
MESH = pl.DeviceIdType.MESH
LOGICAL = pl.DeviceIdType.LOGICAL


def dot(left, right):
    return jnp.dot(left, right, preferred_element_type=F32)


def dot_nt(left, right):
    return lax.dot_general(left, right, (((1,), (1,)), ((), ())), preferred_element_type=F32)


def dot_tn(left, right):
    return lax.dot_general(left, right, (((0,), (0,)), ((), ())), preferred_element_type=F32)


def gelu_pair(value):
    cdf = 0.5 + 0.5 * lax.erf(value * 0.7071067811865476)
    density = jnp.exp(value * value * -0.5) * 0.3989422804014327
    return value * cdf, cdf + value * density


def real_columns(rows):
    at = lax.broadcasted_iota(jnp.int32, (rows, 1), 0)
    return lax.rem(at, WIDE) < 28


def spread(shifted, held, cells):
    for b in range(3):
        shifted[WIDE : WIDE + cells, b * 256 : (b + 1) * 256] = held[
            LEAD - 1 + b : LEAD - 1 + b + cells, :
        ].astype(BF)


def three_rows(shifted, start, rows):
    return jnp.concatenate(
        [shifted[start + a * WIDE : start + a * WIDE + rows, :] for a in range(3)], axis=1
    )


def clear_edges(shifted, helds, cells):
    shifted[0:WIDE, :] = jnp.zeros((WIDE, shifted.shape[1]), BF)
    shifted[WIDE + cells :, :] = jnp.zeros((WIDE, shifted.shape[1]), BF)
    for held in helds:
        held[0:LEAD, :] = jnp.zeros((LEAD, held.shape[1]), F32)
        held[LEAD + cells :, :] = jnp.zeros((held.shape[0] - LEAD - cells, held.shape[1]), F32)


def block_forward_kernel(
    row, image, weight, mean, var, scale, shift, proj, proj_bias, key_value,
    padded, hidden, block_out, slope_one, slope_two, norm_one, norm_two, memory, cross_kv,
    shifted, held_in, held_mid, raw, loose, sent, landed, load_sem, send_sem, land_sem, home_sem,
):
    table = pl.program_id(0)
    cells = padded.shape[1]
    half = cells // 2
    tables, batches, rows = landed.shape[0], image.shape[0], sent.shape[2]
    owned = tables // batches
    group = owned * row
    me = lax.axis_index("row")
    factor = lax.rsqrt(var[...] + EPS)
    mine = pl.ds(pl.multiple_of(me * rows, WIDE), rows)

    def exchange(t, d):
        peer = lax.rem(me + d, row)
        return pltpu.make_async_remote_copy(
            src_ref=sent.at[t, peer], dst_ref=landed.at[t, mine],
            send_sem=send_sem.at[t, d - 1], recv_sem=land_sem.at[t, d - 1],
            device_id={"row": peer}, device_id_type=MESH,
        )

    def keep(t):
        return pltpu.make_async_copy(sent.at[t, me], landed.at[t, mine], home_sem.at[t])

    def take_apart(b):
        gap = jnp.zeros((WIDE - 28, 128), F32)
        for h in range(2):
            lanes = slice(h * 128, (h + 1) * 128)
            loose[h] = raw[b, :, lanes].astype(F32)
            for g in range(group):
                for r in range(rows // WIDE):
                    line = loose[h, pl.ds(r * 28 * group + g, 28, stride=group), :]
                    line = jnp.concatenate([line, gap], axis=0).astype(BF)
                    sent[b * owned + g % owned, g // owned, r * WIDE : (r + 1) * WIDE, lanes] = line

    @pl.when(table == 0)
    def _():
        loads = [pltpu.make_async_copy(image.at[b], raw.at[b], load_sem.at[b]) for b in range(batches)]
        for copy in loads:
            copy.start()
        barrier = pltpu.get_barrier_semaphore()
        for d in range(1, row):
            pl.semaphore_signal(
                barrier, inc=1, device_id={"row": lax.rem(me + d, row)}, device_id_type=MESH
            )
        for b in range(batches):
            loads[b].wait()
            take_apart(b)
            if b == 0:
                pl.semaphore_wait(barrier, row - 1)
            for t in range(b * owned, (b + 1) * owned):
                for d in range(1, row):
                    exchange(t, d).start()
                keep(t).start()
        clear_edges(shifted, (held_in, held_mid), cells)

    for d in range(1, row):
        exchange(table, d).wait_recv()
    keep(table).wait()
    padded[0] = landed[table]
    held_in[LEAD : LEAD + cells, :] = landed[table].astype(F32)
    spread(shifted, held_in, cells)
    real = real_columns(half)
    for start in (0, half):
        pre = dot(three_rows(shifted, start, half), weight[0])
        norm = (pre - mean[0:1]) * factor[0:1]
        act, slope = gelu_pair(norm * scale[0:1] + shift[0:1])
        act = jnp.where(real, act, 0.0)
        held_mid[LEAD + start : LEAD + start + half, :] = act
        hidden[0, start : start + half, :] = act.astype(BF)
        slope_one[0, start : start + half, :] = jnp.where(real, slope, 0.0).astype(BF)
        norm_one[0, start : start + half, :] = norm.astype(BF)
    spread(shifted, held_mid, cells)
    for start in (0, half):
        pre = dot(three_rows(shifted, start, half), weight[1])
        norm = (pre - mean[1:2]) * factor[1:2]
        total = norm * scale[1:2] + shift[1:2] + held_in[LEAD + start : LEAD + start + half, :]
        act, slope = gelu_pair(total)
        block = act.astype(BF)
        block_out[0, start : start + half, :] = block
        slope_two[0, start : start + half, :] = slope.astype(BF)
        norm_two[0, start : start + half, :] = norm.astype(BF)
        tokens = (dot(block, proj[...]) + proj_bias[...]).astype(BF)
        memory[0, start : start + half, :] = tokens
        for k in range(2):
            cross_kv[0, start : start + half, k * 512 : (k + 1) * 512] = dot(
                tokens, key_value[k]
            ).astype(BF)

    @pl.when(table == tables - 1)
    def _():
        for t in range(tables):
            for d in range(1, row):
                exchange(t, d).wait_send()


def whole(*shape):
    zeros = (0,) * len(shape)
    return pl.BlockSpec(shape, lambda t: zeros)


def per_table(*shape):
    zeros = (0,) * len(shape)
    return pl.BlockSpec((1,) + shape, lambda t: (t,) + zeros)


def block_forward(image, weight, mean, var, scale, shift, proj, proj_bias, attn_in, row, group, part):
    batches, width = image.shape[0], image.shape[2]
    tables, cells = batches * (group // row), part * row * WIDE
    model = proj.shape[1]
    small = jax.ShapeDtypeStruct((tables, cells, width), BF)
    stats = [whole(2, width)] * 4
    return pl.pallas_call(
        functools.partial(block_forward_kernel, row),
        grid=(tables,),
        in_specs=[pl.BlockSpec(memory_space=pl.ANY), whole(*weight.shape)] + stats
        + [whole(*proj.shape), whole(1, model), pl.BlockSpec((2,) + attn_in.shape[1:], lambda t: (2, 0, 0))],
        out_specs=[per_table(cells, width)] * 7 + [per_table(cells, model), per_table(cells, 2 * model)],
        out_shape=[small] * 7 + [
            jax.ShapeDtypeStruct((tables, cells, model), BF),
            jax.ShapeDtypeStruct((tables, cells, 2 * model), BF),
        ],
        scratch_shapes=[
            pltpu.VMEM((cells + 2 * WIDE, 3 * width), BF),
            pltpu.VMEM((cells + 80, width), F32),
            pltpu.VMEM((cells + 80, width), F32),
            pltpu.VMEM(image.shape, BF),
            pltpu.VMEM((2, image.shape[1], 128), F32),
            pltpu.VMEM((tables, row, part * WIDE, width), BF),
            pltpu.VMEM((tables, cells, width), BF),
            pltpu.SemaphoreType.DMA((batches,)),
            pltpu.SemaphoreType.DMA((tables, row - 1)),
            pltpu.SemaphoreType.DMA((tables, row - 1)),
            pltpu.SemaphoreType.DMA((tables,)),
        ],
        compiler_params=pltpu.CompilerParams(
            vmem_limit_bytes=56 * MIB, collective_id=1, has_side_effects=True
        ),
        name="block_forward",
    )(image, weight, mean, var, scale, shift, proj, proj_bias, attn_in)


def orders(dp, row):
    row_digits = [("row", 1 << i, 2) for i in range(row.bit_length() - 1)]
    far, stride = [], 2
    while stride < dp:
        radix = 2
        far.append(("dp", stride, radix))
        stride *= radix
    pair, others, near = row_digits[:1], row_digits[1:], [("dp", 1, 2)]
    return [pair + near + others + far, pair + others + near + far, pair + far + near + others]


def places(dp, row, route):
    at = {"dp": lax.axis_index("dp"), "row": lax.axis_index("row")}
    weight = {"dp": row, "row": 1}
    here = at["dp"] * row + at["row"]
    peers = [lax.rem(at["row"] + d, row) for d in range(row)]
    peer_ids = [here - at["row"] + peer for peer in peers]
    own, partners = {}, {}
    for digit in route:
        axis, stride, radix = digit
        own[digit] = [lax.rem(at[axis] // stride + d, radix) for d in range(radix)]
        partners[digit] = [
            here + (other - own[digit][0]) * (stride * weight[axis]) for other in own[digit]
        ]
    return peers, peer_ids, own, partners


def timetable(early, late, stages, slots):
    table, chunks, at_unit = {}, [], 0
    for first, count, pitch, size, turns in ((0, early, PITCH, SIZE, EARLY), (slots, late, 1, 1, LATE)):
        seen, last, i = {}, at_unit + count, 0
        while at_unit < last:
            stream = turns[i % len(turns)]
            lag = seen.get(stream, 0)
            seen[stream] = lag + 1
            units = min(size, last - at_unit)
            chunks.append((stream, at_unit, units))
            at_unit, i = at_unit + units, i + 1
            for k in range(2 * stages + 1):
                at = first + pitch * (lag + k)
                if pitch > 1 and at >= slots:
                    at = slots + (at - slots) // pitch
                table.setdefault(at, []).append((len(chunks) - 1, k))
    return {at: steps[::-1] for at, steps in sorted(table.items())}, chunks


class Summing:
    def __init__(self, chunks, routes, own, partners, unit, held, landed, done, total, rows_all, sems):
        self.chunks, self.routes, self.unit, self.partners = chunks, routes, unit, partners
        self.held, self.landed, self.done, self.total, self.rows_all = held, landed, done, total, rows_all
        self.send_sem, self.land_sem, self.back_sem, self.home_sem, self.out_sem = sems
        self.stages = len(routes[0])
        self.plans = {}
        for stream, units in sorted({(stream, units) for stream, _, units in chunks}):
            start, rows, slot, plan = 0, unit * units, 0, []
            for digit in routes[stream]:
                radix = digit[2]
                part = rows // radix
                targets = [start + other * part for other in own[digit]]
                plan.append((targets, part, unit * units - rows, slot, partners[digit]))
                start, rows, slot = targets[0], part, slot + radix - 1
            self.plans[stream, units] = plan

    def plan(self, c, s):
        stream, _, units = self.chunks[c]
        return self.plans[stream, units][s]

    def base(self, c):
        return self.chunks[c][1] * self.unit

    def rows_at(self, c, offset, rows):
        return pl.ds(pl.multiple_of(self.base(c) + offset, 16), rows)

    def out(self, c, s):
        targets, part, landing, slot, partners = self.plan(c, s)
        return [
            pltpu.make_async_remote_copy(
                src_ref=self.held.at[self.rows_at(c, targets[d], part), :],
                dst_ref=self.landed.at[pl.ds(self.base(c) + landing + (d - 1) * part, part), :],
                send_sem=self.send_sem.at[c, slot + d - 1], recv_sem=self.land_sem.at[c, slot + d - 1],
                device_id=partners[d], device_id_type=LOGICAL,
            )
            for d in range(1, len(partners))
        ]

    def back(self, c, s):
        targets, part, _, slot, partners = self.plan(c, s)
        here = self.done.at[self.rows_at(c, targets[0], part), :]
        return [
            pltpu.make_async_remote_copy(
                src_ref=here, dst_ref=here,
                send_sem=self.back_sem.at[c, slot + d - 1], recv_sem=self.home_sem.at[c, slot + d - 1],
                device_id=partners[d], device_id_type=LOGICAL,
            )
            for d in range(1, len(partners))
        ]

    def collect(self, c, s, target):
        targets, part, landing, _, partners = self.plan(c, s)
        for copy in self.out(c, s):
            copy.wait_recv()
        step = min(part, 256)
        for i in range(0, part, step):
            here = self.rows_at(c, targets[0] + i, step)
            found = self.held[here, :].astype(F32)
            for d in range(len(partners) - 1):
                found += self.landed[pl.ds(self.base(c) + landing + d * part + i, step), :].astype(F32)
            target[here, :] = found.astype(BF)

    def finish(self, c):
        rows = pl.ds(self.base(c), min(self.unit * self.chunks[c][2], self.rows_all - self.base(c)))
        return pltpu.make_async_copy(self.done.at[rows, :], self.total.at[rows, :], self.out_sem.at[c])

    def step(self, c, k):
        last = self.stages
        if 0 < k < last:
            self.collect(c, k - 1, self.held)
        elif k == last:
            self.collect(c, k - 1, self.done)
        elif k > last:
            for copy in self.back(c, 2 * last - k):
                copy.wait_recv()
        if k < last:
            copies = self.out(c, k)
        elif k < 2 * last:
            copies = self.back(c, 2 * last - 1 - k)
        else:
            copies = [self.finish(c)]
        for copy in copies:
            copy.start()

    def settle(self):
        for c in range(len(self.chunks)):
            for s in range(self.stages):
                for copy in self.out(c, s) + self.back(c, s):
                    copy.wait_send()
            self.finish(c).wait()


def block_backward_kernel(
    plan, routes, unit, dp, row,
    grad_tokens, padded, hidden, block_out, slope_one, slope_two, norm_one, norm_two,
    weight, var, scale, proj, early, line_gain, line_bias, line_ffn_in, line_ffn_out,
    total, small_total, image_back,
    shifted_two, shifted_one, held, kept, weight_back, conv_sum, proj_sum, bn_sum, bias_sum, image_grad,
    parts, landed, done, small_held, small_landed,
    load_sem, send_sem, land_sem, back_sem, home_sem, out_sem,
    small_send, small_land, image_send, image_land, image_sem,
):
    step = pl.program_id(0)
    tables, cells = image_grad.shape[0], padded.shape[1]
    half = cells // 2
    owned, rows = image_back.shape[1] // row, image_back.shape[2]
    gain = lax.rsqrt(var[...] + EPS) * scale[...]
    peers, peer_ids, own, partners = places(dp, row, routes[0])
    me = peers[0]
    turns, chunks = plan
    stages = len(routes[0])
    early_rows = early.shape[0]
    summing = Summing(
        chunks, routes, own, partners, unit, parts, landed, done, total, total.shape[0],
        (send_sem, land_sem, back_sem, home_sem, out_sem),
    )
    load = pltpu.make_async_copy(early, parts.at[pl.ds(0, early_rows), :], load_sem)

    def image_copy(t, d):
        return pltpu.make_async_remote_copy(
            src_ref=image_grad.at[t, pl.ds(pl.multiple_of(peers[d] * rows, WIDE), rows)],
            dst_ref=image_back.at[t // owned, me * owned + lax.rem(t, owned)],
            send_sem=image_send.at[t, d - 1], recv_sem=image_land.at[t, d - 1],
            device_id=peer_ids[d], device_id_type=LOGICAL,
        )

    def image_keep(t):
        return pltpu.make_async_copy(
            image_grad.at[t, pl.ds(pl.multiple_of(me * rows, WIDE), rows)],
            image_back.at[t // owned, me * owned + lax.rem(t, owned)], image_sem.at[t],
        )

    def slot(phase):
        for t in range(tables):
            steps = turns.get(t * SLOTS + phase)
            if steps:
                @pl.when(step == t)
                def _():
                    for c, k in steps:
                        summing.step(c, k)

    @pl.when(step == 0)
    def _():
        load.start()
        barrier = pltpu.get_barrier_semaphore()
        greeted = peer_ids[1:]
        for digit in routes[0]:
            if digit[0] == "dp":
                greeted = greeted + partners[digit][1:]
        for device in greeted:
            pl.semaphore_signal(barrier, inc=1, device_id=device, device_id_type=LOGICAL)
        clear_edges(shifted_two, (held,), cells)
        clear_edges(shifted_one, (), cells)
        conv_sum[...] = jnp.zeros_like(conv_sum)
        proj_sum[...] = jnp.zeros_like(proj_sum)
        bn_sum[...] = jnp.zeros_like(bn_sum)
        bias_sum[...] = jnp.zeros_like(bias_sum)
        pl.semaphore_wait(barrier, len(greeted))
        load.wait()

    slot(0)

    @pl.when(step == 0)
    def _():
        for layer in range(2):
            for tap in range(9):
                turned = weight[layer, tap * 256 : (tap + 1) * 256, :].T
                weight_back[layer, (8 - tap) * 256 : (9 - tap) * 256, :] = turned

    def add_stats(layer, grad, norm):
        bn_sum[layer : layer + 1, :] += jnp.sum(grad * norm.astype(F32), axis=0, keepdims=True)
        bn_sum[2 + layer : 3 + layer, :] += jnp.sum(grad, axis=0, keepdims=True)

    def add_conv(layer, inputs, shifted):
        turned = inputs.T
        for a in range(3):
            start = (2 - a) * WIDE
            found = dot(turned, shifted[start : start + cells, :])
            for b in range(3):
                conv_sum[layer, a, b] += found[:, (2 - b) * 256 : (3 - b) * 256]

    proj_sum[...] += dot_tn(block_out[0], grad_tokens[0])
    bias_sum[...] += jnp.sum(grad_tokens[0].astype(F32), axis=0, keepdims=True)
    for start in (0, half):
        part = slice(start, start + half)
        grad = slope_two[0, part, :].astype(F32) * dot_nt(grad_tokens[0, part, :], proj[...])
        kept[part, :] = grad
        add_stats(1, grad, norm_two[0, part, :])
        held[LEAD + start : LEAD + start + half, :] = grad * gain[1:2]
    slot(1)
    spread(shifted_two, held, cells)
    for start in (0, half):
        part = slice(start, start + half)
        back = dot(three_rows(shifted_two, start, half), weight_back[1])
        grad = slope_one[0, part, :].astype(F32) * back
        add_stats(0, grad, norm_one[0, part, :])
        held[LEAD + start : LEAD + start + half, :] = grad * gain[0:1]
    slot(2)
    spread(shifted_one, held, cells)
    for start in (0, half):
        back = dot(three_rows(shifted_one, start, half), weight_back[0]) + kept[start : start + half, :]
        image_grad[step, start : start + half, :] = back.astype(BF)
    for d in range(1, row):
        image_copy(step, d).start()
    image_keep(step).start()
    slot(3)
    add_conv(1, hidden[0], shifted_two)
    slot(4)
    add_conv(0, padded[0], shifted_one)

    @pl.when(step == tables - 1)
    def _():
        for a in range(3):
            for b in range(3):
                at = early_rows + (3 * a + b) * 256
                for layer in range(2):
                    lanes = slice(layer * 256, (layer + 1) * 256)
                    parts[at : at + 256, lanes] = conv_sum[layer, a, b].astype(BF)
        at = early_rows + 9 * 256
        parts[at : at + 256, :] = proj_sum[...].astype(BF)
        small_held[0] = jnp.concatenate([
            jnp.concatenate([bn_sum[0:2, :], bn_sum[2:4, :]], axis=1), bias_sum[...], line_ffn_out[...],
            line_ffn_in[:, 0:512], line_ffn_in[:, 512:1024], jnp.zeros((2, 512), F32),
            line_gain[...], line_bias[...], jnp.zeros((2, 512), F32),
        ], axis=0)

        slots = [sum(digit[2] - 1 for digit in routes[0][:s]) for s in range(stages)]

        def small_copies(s):
            return [
                pltpu.make_async_remote_copy(
                    src_ref=small_held.at[s], dst_ref=small_landed.at[slots[s] + d - 1],
                    send_sem=small_send.at[slots[s] + d - 1], recv_sem=small_land.at[slots[s] + d - 1],
                    device_id=partners[routes[0][s]][d], device_id_type=LOGICAL,
                )
                for d in range(1, routes[0][s][2])
            ]

        for at, steps in turns.items():
            if at < tables * SLOTS:
                continue
            s = at - tables * SLOTS
            if 0 < s <= stages:
                found = small_held[s - 1]
                for d, copy in enumerate(small_copies(s - 1)):
                    copy.wait()
                    found += small_landed[slots[s - 1] + d]
                if s < stages:
                    small_held[s] = found
                else:
                    small_total[...] = found
            if s < stages:
                for copy in small_copies(s):
                    copy.start()
            for c, k in steps:
                summing.step(c, k)
        summing.settle()
        for t in range(tables):
            for d in range(1, row):
                image_copy(t, d).wait()
            image_keep(t).wait()


def block_backward(
    grad_tokens, padded, hidden, block_out, slope_one, slope_two, norm_one, norm_two,
    weight, var, scale, proj, early, smalls, dp, row, batches,
):
    tables, cells, model = grad_tokens.shape
    width = proj.shape[0]
    per = per_table(cells, width)
    once = pl.Buffered(1)
    routes = orders(dp, row)
    stages = len(routes[0])
    arrivals = sum(digit[2] - 1 for digit in routes[0])
    unit = 16 * dp * row
    rows = early.shape[0] + 10 * width
    early_units, units = early.shape[0] // unit, -(-rows // unit)
    plan = timetable(early_units, units - early_units, stages, SLOTS * tables)
    far = pl.BlockSpec(memory_space=pl.ANY)
    near = pl.BlockSpec(memory_space=pltpu.VMEM)
    sem = pltpu.SemaphoreType.DMA
    return pl.pallas_call(
        functools.partial(block_backward_kernel, plan, routes, unit, dp, row),
        grid=(tables,),
        in_specs=[per_table(cells, model)] + [per] * 7
        + [pl.BlockSpec(weight.shape, lambda t: (0, 0, 0), pipeline_mode=once)]
        + [whole(2, width)] * 2 + [whole(*proj.shape)] + [far] + [whole(*x.shape) for x in smalls],
        out_specs=[far, whole(16, model), far],
        out_shape=[
            jax.ShapeDtypeStruct((rows, model), BF),
            jax.ShapeDtypeStruct((16, model), F32),
            jax.ShapeDtypeStruct((batches, tables // batches * row, cells // row, width), BF),
        ],
        scratch_shapes=[
            pltpu.VMEM((cells + 2 * WIDE, 3 * width), BF),
            pltpu.VMEM((cells + 2 * WIDE, 3 * width), BF),
            pltpu.VMEM((cells + 80, width), F32),
            pltpu.VMEM((cells, width), F32),
            pltpu.VMEM(weight.shape, BF),
            pltpu.VMEM((2, 3, 3, width, width), F32),
            pltpu.VMEM(proj.shape, F32),
            pltpu.VMEM((4, width), F32),
            pltpu.VMEM((1, model), F32),
            pltpu.VMEM((tables, cells, width), BF),
            pltpu.VMEM((units * unit, model), BF),
            pltpu.VMEM((units * unit, model), BF),
            pltpu.VMEM((units * unit, model), BF),
            pltpu.VMEM((stages, 16, model), F32),
            pltpu.VMEM((arrivals, 16, model), F32),
            sem, sem((units, arrivals)), sem((units, arrivals)),
            sem((units, arrivals)), sem((units, arrivals)), sem((units,)),
            sem((arrivals,)), sem((arrivals,)),
            sem((tables, row - 1)), sem((tables, row - 1)), sem((tables,)),
        ],
        compiler_params=pltpu.CompilerParams(
            vmem_limit_bytes=62 * MIB, collective_id=0, has_side_effects=True
        ),
        name="block_backward",
    )(
        grad_tokens, padded, hidden, block_out, slope_one, slope_two, norm_one, norm_two,
        weight, var, scale, proj, early, *smalls,
    )


def lane_masks(rows, lanes):
    at = lax.broadcasted_iota(jnp.int32, (rows, lanes), 1) // 64
    return [at == h for h in range(GROUP)]


def by_head(value, masks):
    zero = jnp.zeros_like(value)
    return jnp.concatenate([jnp.where(m, value, zero) for m in masks], axis=0)


def own_lanes(stacked, masks):
    rows = stacked.shape[0] // GROUP
    total = stacked[0:rows]
    for h in range(1, GROUP):
        total = jnp.where(masks[h], stacked[h * rows : (h + 1) * rows], total)
    return total


def softmax_rows(scores):
    raised = jnp.exp(scores - jnp.max(scores, axis=-1, keepdims=True))
    return raised * (1.0 / jnp.sum(raised, axis=-1, keepdims=True))


def normalise(value):
    center = value - jnp.mean(value, axis=-1, keepdims=True)
    inverse = lax.rsqrt(jnp.mean(center * center, axis=-1, keepdims=True) + EPS)
    return center * inverse, inverse


def norm_back(upstream, gain, unit, inverse):
    scaled = upstream * gain
    mean = jnp.mean(scaled, axis=-1, keepdims=True)
    along = jnp.mean(scaled * unit, axis=-1, keepdims=True)
    return inverse * (scaled - mean - unit * along)


def column_sum(value):
    return jnp.sum(value, axis=0, keepdims=True)


def decoder_kernel(
    lengths, ln_gain, ln_bias, ffn_in_bias, ffn_out_bias,
    tags_far, cotangent_far, memory_far, cross_kv_far, attn_in_far, attn_out_far, ffn_in_far, ffn_out_far,
    decoded, tags_grad, grad_tokens, grads_far,
    ln_gain_grad, ln_bias_grad, ffn_in_bias_grad, ffn_out_bias_grad,
    tags, cotangent, memory, cross_kv, attn_in, attn_out, ffn_in, ffn_out,
    qkv, mix, self_shares, cross_shares, cross_q, up, grad_qkv, grad_q, grad_kv, pair_sum,
    staged, weight_sem, kv_sem, memory_sem, staged_sem,
    grads, grad_sem,
):
    tables, cells = memory_far.shape[0], memory_far.shape[1]
    slots = tags.shape[0] // tables

    def fetch_kv(t):
        return pltpu.make_async_copy(cross_kv_far.at[t], cross_kv.at[t], kv_sem.at[t])

    def fetch_memory(t):
        slot = lax.rem(t, 2)
        return pltpu.make_async_copy(memory_far.at[t], memory.at[slot], memory_sem.at[slot])

    def put_tokens(t):
        slot = lax.rem(t, 2)
        return pltpu.make_async_copy(staged.at[slot], grad_tokens.at[t], staged_sem.at[slot])

    fetches = [
        pltpu.make_async_copy(far, near, weight_sem.at[i])
        for i, (far, near) in enumerate(
            [(tags_far, tags)]
            + [(attn_in_far.at[k], attn_in.at[k]) for k in range(4)]
            + [(attn_out_far, attn_out), (cotangent_far, cotangent)]
            + [(ffn_in_far, ffn_in), (ffn_out_far, ffn_out)]
            + [(attn_in_far.at[k], attn_in.at[k]) for k in (4, 5)]
        )
    ]
    for copy in fetches[:6]:
        copy.start()
    for t in range(tables):
        fetch_kv(t).start()
    for copy in fetches[6:]:
        copy.start()
    fetch_memory(0).start()
    half = 256
    wide_f32 = lane_masks(slots, half)
    real_key = lax.rem(lax.broadcasted_iota(jnp.int32, (GROUP * slots, cells), 1), WIDE) < 28

    def allowed_of(t):
        row = lax.broadcasted_iota(jnp.int32, (slots, slots), 0)
        col = lax.broadcasted_iota(jnp.int32, (slots, slots), 1)
        once = (col <= row) & (col < lengths[t])
        return jnp.concatenate([once] * GROUP, axis=0)

    def put_grad(i, value):
        grads[i] = value.astype(BF)
        copy = pltpu.make_async_copy(grads.at[i], grads_far.at[i], grad_sem.at[i])
        copy.start()
        puts.append(copy)

    puts = []
    fetches[0].wait()
    for k in range(3):
        fetches[1 + k].wait()
        qkv[k] = dot(tags[...], attn_in[k]).astype(BF)

    def self_forward(t, carry):
        rows = pl.ds(pl.multiple_of(t * slots, slots), slots)
        allowed = allowed_of(t)
        for g in range(2):
            lanes = slice(g * half, (g + 1) * half)
            query = by_head(qkv[0, rows, lanes], wide_f32)
            scores = dot_nt(query, qkv[1, rows, lanes]) * 0.125
            shares = softmax_rows(jnp.where(allowed, scores, MASKED)).astype(BF)
            self_shares[t, g] = shares
            mix[0, rows, lanes] = own_lanes(dot(shares, qkv[2, rows, lanes]), wide_f32).astype(BF)
        return carry

    lax.fori_loop(0, tables, self_forward, 0)
    fetches[5].wait()
    first_unit, first_inv = normalise(tags[...].astype(F32) + dot(mix[0], attn_out[0]))
    first = first_unit * ln_gain[0:1] + ln_bias[0:1]
    first_low = first.astype(BF)
    fetches[4].wait()
    cross_q[...] = dot(first_low, attn_in[3]).astype(BF)

    def cross_forward(t, carry):
        fetch_kv(t).wait()
        rows = pl.ds(pl.multiple_of(t * slots, slots), slots)
        for g in range(2):
            lanes = slice(g * half, (g + 1) * half)
            query = by_head(cross_q[rows, lanes], wide_f32)
            scores = dot_nt(query, cross_kv[t, :, lanes]) * 0.125
            shares = softmax_rows(jnp.where(real_key, scores, MASKED)).astype(BF)
            cross_shares[t, g] = shares
            value = cross_kv[t, :, 512 + g * half : 512 + (g + 1) * half]
            mix[1, rows, lanes] = own_lanes(dot(shares, value), wide_f32).astype(BF)
        return carry

    lax.fori_loop(0, tables, cross_forward, 0)
    second_unit, second_inv = normalise(first + dot(mix[1], attn_out[1]))
    second = second_unit * ln_gain[1:2] + ln_bias[1:2]
    second_low = second.astype(BF)
    for copy in fetches[6:]:
        copy.wait()
    act, slope = gelu_pair(dot(second_low, ffn_in[...]) + ffn_in_bias[...])
    inner_act = act.astype(BF)
    third_unit, third_inv = normalise(second + dot(inner_act, ffn_out[...]) + ffn_out_bias[...])
    decoded[...] = (third_unit * ln_gain[2:3] + ln_bias[2:3]).astype(BF)

    up_three = cotangent[...].astype(F32)
    ln_gain_grad[2:3, :] = column_sum(up_three * third_unit)
    ln_bias_grad[2:3, :] = column_sum(up_three)
    grad_third = norm_back(up_three, ln_gain[2:3], third_unit, third_inv)
    grad_outer = grad_third.astype(BF)
    ffn_out_total = dot_tn(inner_act, grad_outer)
    for k in range(2):
        put_grad(8 + k, ffn_out_total[k * 512 : (k + 1) * 512])
    ffn_out_bias_grad[...] = column_sum(grad_outer.astype(F32))
    grad_inner = (slope * dot_nt(grad_outer, ffn_out[...])).astype(BF)
    ffn_in_total = dot_tn(second_low, grad_inner)
    for k in range(2):
        put_grad(10 + k, ffn_in_total[:, k * 512 : (k + 1) * 512])
    ffn_in_bias_grad[...] = column_sum(grad_inner.astype(F32))
    up_two = grad_third + dot_nt(grad_inner, ffn_in[...])
    ln_gain_grad[1:2, :] = column_sum(up_two * second_unit)
    ln_bias_grad[1:2, :] = column_sum(up_two)
    grad_second = norm_back(up_two, ln_gain[1:2], second_unit, second_inv)
    grad_cross_out = grad_second.astype(BF)
    put_grad(7, dot_tn(mix[1], grad_cross_out))
    up[...] = dot_nt(grad_cross_out, attn_out[1]).astype(BF)
    pair_sum[...] = jnp.zeros_like(pair_sum)

    def cross_back(t, carry):
        @pl.when(t + 1 < tables)
        def _():
            fetch_memory(t + 1).start()

        rows = pl.ds(pl.multiple_of(t * slots, slots), slots)
        for g in range(2):
            lanes = slice(g * half, (g + 1) * half)
            value_lanes = slice(512 + g * half, 512 + (g + 1) * half)
            query = by_head(cross_q[rows, lanes], wide_f32)
            upstream = by_head(up[rows, lanes], wide_f32)
            low = cross_shares[t, g]
            shares = low.astype(F32)
            grad_shares = dot_nt(upstream, cross_kv[t, :, value_lanes])
            mean = jnp.sum(grad_shares * shares, axis=-1, keepdims=True)
            grad_scores = (shares * (grad_shares - mean)).astype(BF)
            grad_q[rows, lanes] = (
                own_lanes(dot(grad_scores, cross_kv[t, :, lanes]), wide_f32) * 0.125
            ).astype(BF)
            grad_kv[:, lanes] = (dot_tn(grad_scores, query) * 0.125).astype(BF)
            grad_kv[:, value_lanes] = dot_tn(low, upstream).astype(BF)
        @pl.when(t >= 2)
        def _():
            put_tokens(t - 2).wait()

        slot = lax.rem(t, 2)
        staged[slot] = (
            dot_nt(grad_kv[:, 0:512], attn_in[4]) + dot_nt(grad_kv[:, 512:1024], attn_in[5])
        ).astype(BF)
        put_tokens(t).start()
        fetch_memory(t).wait()
        pair_sum[...] += dot_tn(memory[slot], grad_kv[...])
        return carry

    lax.fori_loop(0, tables, cross_back, 0)
    for t in range(max(tables - 2, 0), tables):
        put_tokens(t).wait()
    for k in range(2):
        put_grad(4 + k, pair_sum[:, k * 512 : (k + 1) * 512])
    put_grad(3, dot_tn(first_low, grad_q[...]))
    up_one = grad_second + dot_nt(grad_q[...], attn_in[3])
    ln_gain_grad[0:1, :] = column_sum(up_one * first_unit)
    ln_bias_grad[0:1, :] = column_sum(up_one)
    grad_first = norm_back(up_one, ln_gain[0:1], first_unit, first_inv)
    grad_self_out = grad_first.astype(BF)
    put_grad(6, dot_tn(mix[0], grad_self_out))
    up[...] = dot_nt(grad_self_out, attn_out[0]).astype(BF)

    def self_back(t, carry):
        rows = pl.ds(pl.multiple_of(t * slots, slots), slots)
        for g in range(2):
            lanes = slice(g * half, (g + 1) * half)
            query = by_head(qkv[0, rows, lanes], wide_f32)
            upstream = by_head(up[rows, lanes], wide_f32)
            low = self_shares[t, g]
            shares = low.astype(F32)
            grad_shares = dot_nt(upstream, qkv[2, rows, lanes])
            mean = jnp.sum(grad_shares * shares, axis=-1, keepdims=True)
            grad_scores = (shares * (grad_shares - mean)).astype(BF)
            grad_qkv[0, rows, lanes] = (
                own_lanes(dot(grad_scores, qkv[1, rows, lanes]), wide_f32) * 0.125
            ).astype(BF)
            grad_qkv[1, rows, lanes] = (dot_tn(grad_scores, query) * 0.125).astype(BF)
            grad_qkv[2, rows, lanes] = dot_tn(low, upstream).astype(BF)
        return carry

    lax.fori_loop(0, tables, self_back, 0)
    total = grad_first
    for k in range(3):
        put_grad(k, dot_tn(tags[...], grad_qkv[k]))
        total = total + dot_nt(grad_qkv[k], attn_in[k])
    tags_grad[...] = total
    for copy in puts:
        copy.wait()


def decoder(
    lengths, tags, cotangent, memory, cross_kv, attn_in, attn_out, ln_gain, ln_bias,
    ffn_in, ffn_in_bias, ffn_out, ffn_out_bias,
):
    tables, cells, model = memory.shape
    rows = tags.shape[0]
    slots = rows // tables
    inner = ffn_in.shape[1]
    here = pl.BlockSpec(memory_space=pltpu.VMEM)
    far = pl.BlockSpec(memory_space=pl.ANY)
    shape = jax.ShapeDtypeStruct
    stacked = GROUP * slots
    return pl.pallas_call(
        decoder_kernel,
        in_specs=[pl.BlockSpec(memory_space=pltpu.SMEM)] + [here] * 4 + [far] * 8,
        out_specs=[here] * 2 + [far] * 2 + [here] * 4,
        out_shape=[
            shape((rows, model), BF), shape((rows, model), F32), shape((tables, cells, model), BF),
            shape((12, 512, model), BF), shape((3, model), F32), shape((3, model), F32),
            shape((1, inner), F32), shape((1, model), F32),
        ],
        scratch_shapes=[
            pltpu.VMEM((rows, model), BF),
            pltpu.VMEM((rows, model), BF),
            pltpu.VMEM((2, cells, model), BF),
            pltpu.VMEM((tables, cells, 2 * model), BF),
            pltpu.VMEM(attn_in.shape, BF),
            pltpu.VMEM(attn_out.shape, BF),
            pltpu.VMEM(ffn_in.shape, BF),
            pltpu.VMEM(ffn_out.shape, BF),
            pltpu.VMEM((3, rows, model), BF),
            pltpu.VMEM((2, rows, model), BF),
            pltpu.VMEM((tables, 2, stacked, slots), BF),
            pltpu.VMEM((tables, 2, stacked, cells), BF),
            pltpu.VMEM((rows, model), BF),
            pltpu.VMEM((rows, model), BF),
            pltpu.VMEM((3, rows, model), BF),
            pltpu.VMEM((rows, model), BF),
            pltpu.VMEM((cells, 2 * model), BF),
            pltpu.VMEM((model, 2 * model), F32),
            pltpu.VMEM((2, cells, model), BF),
            pltpu.SemaphoreType.DMA((11,)),
            pltpu.SemaphoreType.DMA((tables,)),
            pltpu.SemaphoreType.DMA((2,)),
            pltpu.SemaphoreType.DMA((2,)),
            pltpu.VMEM((12, 512, model), BF),
            pltpu.SemaphoreType.DMA((12,)),
        ],
        compiler_params=pltpu.CompilerParams(vmem_limit_bytes=60 * MIB),
        name="decoder",
    )(
        lengths, ln_gain, ln_bias, ffn_in_bias, ffn_out_bias,
        tags, cotangent, memory, cross_kv, attn_in, attn_out, ffn_in, ffn_out,
    )


def widen_kernel(
    small, total, back, conv, proj, attn_in, attn_out, ffn_in, ffn_out, image_grad,
    bn_scale, bn_shift, proj_bias, gain, bias, ffn_in_bias, ffn_out_bias,
    narrow, wide, narrow_image, wide_image, in_sem, out_sem, image_in, image_out,
):
    units = in_sem.shape[0]
    batches, group = back.shape[0], back.shape[1]

    def rows(i):
        return pl.ds(i * 512, 512)

    fetches = [
        pltpu.make_async_copy(total.at[rows(i)], narrow.at[rows(i)], in_sem.at[i]) for i in range(units)
    ]
    images = [(b, g) for b in range(batches) for g in range(group)]
    image_fetches = [
        pltpu.make_async_copy(back.at[b, g], narrow_image.at[i], image_in.at[i])
        for i, (b, g) in enumerate(images)
    ]
    for copy in fetches + image_fetches:
        copy.start()
    bn_scale[...] = small[0:2, 0:256]
    bn_shift[...] = small[0:2, 256:512]
    proj_bias[...] = small[2:3, :]
    ffn_out_bias[...] = small[3:4, :]
    ffn_in_bias[:, 0:512] = small[4:5, :]
    ffn_in_bias[:, 512:1024] = small[5:6, :]
    gain[...] = small[8:11, :]
    bias[...] = small[11:14, :]
    slots = wide.shape[0]
    targets = [attn_in.at[i] for i in range(6)] + [attn_out.at[i] for i in range(2)]
    targets += [ffn_out.at[rows(i)] for i in range(2)]
    targets += [ffn_in.at[:, pl.ds(i * 512, 512)] for i in range(2)]
    pending = []

    def put(i, pairs):
        copies = [
            pltpu.make_async_copy(source, target, out_sem.at[i % slots, j])
            for j, (source, target) in enumerate(pairs)
        ]
        for copy in copies:
            copy.start()
        pending.append(copies)

    for i in range(units):
        fetches[i].wait()
        if i >= slots:
            for copy in pending[i - slots]:
                copy.wait()
        slot = wide.at[i % slots]
        slot[...] = narrow[rows(i), :].astype(F32)
        if i < 12:
            put(i, [(slot, targets[i])])
            continue
        pairs = []
        for half in range(2):
            tap = 2 * (i - 12) + half
            here = pl.ds(half * 256, 256)
            if tap < 9:
                for layer in range(2):
                    lanes = pl.ds(layer * 256, 256)
                    pairs.append((slot.at[here, lanes], conv.at[layer, tap // 3, tap % 3]))
            else:
                pairs.append((slot.at[here], proj))
        put(i, pairs)
    waits = []
    for b in range(batches):
        for g in range(group):
            image_fetches[b * group + g].wait()
            for r in range(back.shape[2] // WIDE):
                line = narrow_image[b * group + g, r * WIDE : (r + 1) * WIDE, :].astype(F32)
                for h in range(2):
                    lanes = slice(h * 128, (h + 1) * 128)
                    wide_image[b, h, pl.ds(r * 28 * group + g, 28, stride=group), :] = line[0:28, lanes]
        for h in range(2):
            waits.append(pltpu.make_async_copy(
                wide_image.at[b, h], image_grad.at[b, :, pl.ds(h * 128, 128)], image_out.at[b, h]
            ))
            waits[-1].start()
    for copies in pending[-slots:] + [waits]:
        for copy in copies:
            copy.wait()


def widen(small, total, back, image_shape, width, model, inner):
    rows = total.shape[0]
    units = rows // 512
    batches, group = back.shape[:2]
    far = pl.BlockSpec(memory_space=pl.ANY)
    near = pl.BlockSpec(memory_space=pltpu.VMEM)
    sem = pltpu.SemaphoreType.DMA
    shapes = [
        (2, 3, 3, width, width), (width, model), (6, model, model), (2, model, model),
        (model, inner), (inner, model), image_shape,
    ]
    small_shapes = [(2, width)] * 2 + [(1, model), (3, model), (3, model), (1, inner), (1, model)]
    return pl.pallas_call(
        widen_kernel,
        in_specs=[near] + [far] * 2,
        out_specs=[far] * 7 + [near] * 7,
        out_shape=[jax.ShapeDtypeStruct(s, F32) for s in shapes + small_shapes],
        scratch_shapes=[
            pltpu.VMEM((rows, model), BF),
            pltpu.VMEM((4, 512, model), F32),
            pltpu.VMEM((batches * group,) + back.shape[2:], BF),
            pltpu.VMEM((batches, 2, image_shape[1], 128), F32),
            sem((units,)), sem((4, 4)), sem((batches * group,)), sem((batches, 2)),
        ],
        compiler_params=pltpu.CompilerParams(vmem_limit_bytes=60 * MIB),
        name="widen",
    )(small, total, back)


def body(
    image, tags, tag_lengths, cotangent, conv_weight, bn_mean, bn_var, bn_scale, bn_shift,
    proj_weight, proj_bias, attn_in, attn_out, ln_gain, ln_bias,
    ffn_in, ffn_in_bias, ffn_out, ffn_out_bias,
):
    batches, owned, slots, model = tags.shape
    width = image.shape[-1]
    tables = batches * owned
    row = lax.axis_size("row")
    group, part, breadth = image.shape[1:4]
    flat_image = image.transpose(0, 2, 3, 1, 4).reshape(batches, part * breadth * group, width)
    weight = conv_weight.reshape(2, 9 * width, width)
    forward = block_forward(
        flat_image, weight, bn_mean, bn_var, bn_scale, bn_shift,
        proj_weight, proj_bias.reshape(1, -1), attn_in, row, group, part,
    )
    padded, hidden, block_out, slope_one, slope_two, norm_one, norm_two, memory, cross_kv = forward
    decoded, tags_grad, grad_tokens, decoder_g, gain_g, bias_g, ffn_in_bias_g, ffn_out_bias_g = decoder(
        tag_lengths.reshape(-1), tags.reshape(-1, model), cotangent.reshape(-1, model),
        memory, cross_kv, attn_in, attn_out, ln_gain, ln_bias,
        ffn_in, ffn_in_bias.reshape(1, -1), ffn_out, ffn_out_bias.reshape(1, -1),
    )
    total, small, back = block_backward(
        grad_tokens, padded, hidden, block_out, slope_one, slope_two, norm_one, norm_two,
        weight, bn_var, bn_scale, proj_weight, decoder_g.reshape(-1, model),
        (gain_g, bias_g, ffn_in_bias_g, ffn_out_bias_g), lax.axis_size("dp"), row, batches,
    )
    (
        conv_g, proj_g, attn_in_g, attn_out_g, ffn_in_g, ffn_out_g, image_g,
        bn_scale_g, bn_shift_g, proj_bias_g, gain_g, bias_g, ffn_in_bias_g, ffn_out_bias_g,
    ) = widen(small, total, back, flat_image.shape, width, model, ffn_in.shape[1])
    image_g = image_g.reshape(batches, part, breadth, group, width).transpose(0, 3, 1, 2, 4)
    return (
        decoded.reshape(tags.shape), image_g, tags_grad.reshape(tags.shape),
        conv_g, bn_scale_g, bn_shift_g, proj_g, proj_bias_g.reshape(-1),
        attn_in_g, attn_out_g, gain_g, bias_g,
        ffn_in_g, ffn_in_bias_g.reshape(-1), ffn_out_g, ffn_out_bias_g.reshape(-1),
    )


def solution(mesh):
    by_rows = P(None, "dp", "row", None, None)
    by_table = P(None, ("dp", "row"), None, None)
    return jax.shard_map(
        body,
        mesh=mesh,
        in_specs=(by_rows, by_table, P(None, ("dp", "row")), by_table) + (P(),) * 15,
        out_specs=(by_table, by_rows, by_table) + (P(),) * 13,
        check_vma=False,
    )
```

```python
import functools

import jax
import jax.numpy as jnp
from jax import lax
from jax.experimental import pallas as pl
from jax.experimental.pallas import tpu as pltpu
from jax.sharding import PartitionSpec as P

HEADS = 8
GROUP = 4
EPS = 1e-05
MASKED = -1e30
BF = jnp.bfloat16
F32 = jnp.float32
WIDE = 32
LEAD = 40
SLOTS = 5
PITCH = 3
SIZE = 1
EARLY = (0, 2, 1, 0, 1)
LATE = (0, 2, 1, 0, 1)
MIB = 1024 * 1024
MESH = pl.DeviceIdType.MESH
LOGICAL = pl.DeviceIdType.LOGICAL


def dot(left, right):
    return jnp.dot(left, right, preferred_element_type=F32)


def dot_nt(left, right):
    return lax.dot_general(left, right, (((1,), (1,)), ((), ())), preferred_element_type=F32)


def dot_tn(left, right):
    return lax.dot_general(left, right, (((0,), (0,)), ((), ())), preferred_element_type=F32)


def gelu_pair(value):
    cdf = 0.5 + 0.5 * lax.erf(value * 0.7071067811865476)
    density = jnp.exp(value * value * -0.5) * 0.3989422804014327
    return value * cdf, cdf + value * density


def real_columns(rows):
    at = lax.broadcasted_iota(jnp.int32, (rows, 1), 0)
    return lax.rem(at, WIDE) < 28


def spread(shifted, held, cells):
    for b in range(3):
        shifted[WIDE : WIDE + cells, b * 256 : (b + 1) * 256] = held[
            LEAD - 1 + b : LEAD - 1 + b + cells, :
        ].astype(BF)


def three_rows(shifted, start, rows):
    return jnp.concatenate(
        [shifted[start + a * WIDE : start + a * WIDE + rows, :] for a in range(3)], axis=1
    )


def clear_edges(shifted, helds, cells):
    shifted[0:WIDE, :] = jnp.zeros((WIDE, shifted.shape[1]), BF)
    shifted[WIDE + cells :, :] = jnp.zeros((WIDE, shifted.shape[1]), BF)
    for held in helds:
        held[0:LEAD, :] = jnp.zeros((LEAD, held.shape[1]), F32)
        held[LEAD + cells :, :] = jnp.zeros((held.shape[0] - LEAD - cells, held.shape[1]), F32)


def block_forward_kernel(
    row, image, lengths, tags_far, attn_in_far, attn_out_far, gain, bias,
    weight, mean, var, scale, shift, proj, proj_bias, key_value,
    padded, hidden, block_out, slope_one, slope_two, norm_one, norm_two, memory, cross_kv,
    qkv, self_shares, self_mix, first_in, cross_q,
    tags, self_in, self_out, weight_sem,
    shifted, held_in, held_mid, raw, loose, sent, landed, load_sem, send_sem, land_sem, home_sem,
):
    table = pl.program_id(0)
    cells = padded.shape[1]
    half = cells // 2
    tables, batches, rows = landed.shape[0], image.shape[0], sent.shape[2]
    owned = tables // batches
    group = owned * row
    me = lax.axis_index("row")
    factor = lax.rsqrt(var[...] + EPS)
    mine = pl.ds(pl.multiple_of(me * rows, WIDE), rows)

    def exchange(t, d):
        peer = lax.rem(me + d, row)
        return pltpu.make_async_remote_copy(
            src_ref=sent.at[t, peer], dst_ref=landed.at[t, mine],
            send_sem=send_sem.at[t, d - 1], recv_sem=land_sem.at[t, d - 1],
            device_id={"row": peer}, device_id_type=MESH,
        )

    def keep(t):
        return pltpu.make_async_copy(sent.at[t, me], landed.at[t, mine], home_sem.at[t])

    def take_apart(b):
        gap = jnp.zeros((WIDE - 28, 128), F32)
        for h in range(2):
            lanes = slice(h * 128, (h + 1) * 128)
            loose[h] = raw[b, :, lanes].astype(F32)
            for g in range(group):
                for r in range(rows // WIDE):
                    line = loose[h, pl.ds(r * 28 * group + g, 28, stride=group), :]
                    line = jnp.concatenate([line, gap], axis=0).astype(BF)
                    sent[b * owned + g % owned, g // owned, r * WIDE : (r + 1) * WIDE, lanes] = line

    @pl.when(table == 0)
    def _():
        loads = [pltpu.make_async_copy(image.at[b], raw.at[b], load_sem.at[b]) for b in range(batches)]
        fetches = [
            pltpu.make_async_copy(tags_far, tags, weight_sem.at[0]),
            pltpu.make_async_copy(attn_in_far.at[pl.ds(0, 4)], self_in, weight_sem.at[1]),
            pltpu.make_async_copy(attn_out_far.at[0], self_out, weight_sem.at[2]),
        ]
        for copy in loads + fetches:
            copy.start()
        barrier = pltpu.get_barrier_semaphore()
        for d in range(1, row):
            pl.semaphore_signal(
                barrier, inc=1, device_id={"row": lax.rem(me + d, row)}, device_id_type=MESH
            )
        for b in range(batches):
            loads[b].wait()
            take_apart(b)
            if b == 0:
                pl.semaphore_wait(barrier, row - 1)
            for t in range(b * owned, (b + 1) * owned):
                for d in range(1, row):
                    exchange(t, d).start()
                keep(t).start()
        clear_edges(shifted, (held_in, held_mid), cells)
        for copy in fetches:
            copy.wait()
        self_forward(
            lengths, tags, self_in, self_out, gain, bias, qkv, self_shares, self_mix, first_in, cross_q
        )

    for d in range(1, row):
        exchange(table, d).wait_recv()
    keep(table).wait()
    padded[0] = landed[table]
    held_in[LEAD : LEAD + cells, :] = landed[table].astype(F32)
    spread(shifted, held_in, cells)
    real = real_columns(half)
    for start in (0, half):
        pre = dot(three_rows(shifted, start, half), weight[0])
        norm = (pre - mean[0:1]) * factor[0:1]
        act, slope = gelu_pair(norm * scale[0:1] + shift[0:1])
        act = jnp.where(real, act, 0.0)
        held_mid[LEAD + start : LEAD + start + half, :] = act
        hidden[0, start : start + half, :] = act.astype(BF)
        slope_one[0, start : start + half, :] = jnp.where(real, slope, 0.0).astype(BF)
        norm_one[0, start : start + half, :] = norm.astype(BF)
    spread(shifted, held_mid, cells)
    for start in (0, half):
        pre = dot(three_rows(shifted, start, half), weight[1])
        norm = (pre - mean[1:2]) * factor[1:2]
        total = norm * scale[1:2] + shift[1:2] + held_in[LEAD + start : LEAD + start + half, :]
        act, slope = gelu_pair(total)
        block = act.astype(BF)
        block_out[0, start : start + half, :] = block
        slope_two[0, start : start + half, :] = slope.astype(BF)
        norm_two[0, start : start + half, :] = norm.astype(BF)
        tokens = (dot(block, proj[...]) + proj_bias[...]).astype(BF)
        memory[0, start : start + half, :] = tokens
        for k in range(2):
            cross_kv[0, start : start + half, k * 512 : (k + 1) * 512] = dot(
                tokens, key_value[k]
            ).astype(BF)

    @pl.when(table == tables - 1)
    def _():
        for t in range(tables):
            for d in range(1, row):
                exchange(t, d).wait_send()


def whole(*shape):
    zeros = (0,) * len(shape)
    return pl.BlockSpec(shape, lambda t: zeros)


def per_table(*shape):
    zeros = (0,) * len(shape)
    return pl.BlockSpec((1,) + shape, lambda t: (t,) + zeros)


def self_forward(lengths, tags, attn_in, attn_out, gain, bias, qkv, shares, mix, first_in, cross_q):
    tables, slots, half = shares.shape[0], shares.shape[2], 256
    masks = lane_masks(slots, half)
    for k in range(3):
        qkv[k] = dot(tags[...], attn_in[k]).astype(BF)
    key = lax.broadcasted_iota(jnp.int32, (slots, slots), 0)
    query = lax.broadcasted_iota(jnp.int32, (slots, slots), 1)

    def one(t, carry):
        rows = pl.ds(pl.multiple_of(t * slots, slots), slots)
        allowed = jnp.concatenate([(key <= query) & (key < lengths[t])] * GROUP, axis=1)
        for g in range(2):
            lanes = slice(g * half, (g + 1) * half)
            shares[t, g], mix[rows, lanes] = attend(
                by_head(qkv[0, rows, lanes], masks), qkv[1, rows, lanes], qkv[2, rows, lanes],
                lambda x: jnp.where(allowed, x, MASKED),
            )
        return carry

    lax.fori_loop(0, tables, one, 0)
    total = tags[...].astype(F32) + dot(mix[...], attn_out[...])
    first_in[...] = total
    first = normalise(total)[0] * gain[0:1] + bias[0:1]
    cross_q[...] = dot(first.astype(BF), attn_in[3]).astype(BF)


def block_forward(
    image, lengths, tags, attn_out, gain, bias,
    weight, mean, var, scale, shift, proj, proj_bias, attn_in, row, group, part,
):
    batches, width = image.shape[0], image.shape[2]
    tables, cells = batches * (group // row), part * row * WIDE
    model = proj.shape[1]
    small = jax.ShapeDtypeStruct((tables, cells, width), BF)
    stats = [whole(2, width)] * 4
    far = pl.BlockSpec(memory_space=pl.ANY)
    rows = tags.shape[0]
    tag_shapes = [
        ((3, rows, model), BF), ((tables, 2, rows // tables, GROUP * rows // tables), BF),
        ((rows, model), BF), ((rows, model), F32), ((rows, model), BF),
    ]
    return pl.pallas_call(
        functools.partial(block_forward_kernel, row),
        grid=(tables,),
        in_specs=[far, pl.BlockSpec(memory_space=pltpu.SMEM), far, far, far, whole(*gain.shape), whole(*bias.shape)]
        + [whole(*weight.shape)] + stats
        + [whole(*proj.shape), whole(1, model), pl.BlockSpec((2,) + attn_in.shape[1:], lambda t: (2, 0, 0))],
        out_specs=[per_table(cells, width)] * 7 + [per_table(cells, model), per_table(cells, 2 * model)]
        + [whole(*shape) for shape, _ in tag_shapes],
        out_shape=[small] * 7 + [
            jax.ShapeDtypeStruct((tables, cells, model), BF),
            jax.ShapeDtypeStruct((tables, cells, 2 * model), BF),
        ] + [jax.ShapeDtypeStruct(shape, dtype) for shape, dtype in tag_shapes],
        scratch_shapes=[
            pltpu.VMEM((rows, model), BF),
            pltpu.VMEM((4, model, model), BF),
            pltpu.VMEM((model, model), BF),
            pltpu.SemaphoreType.DMA((3,)),
            pltpu.VMEM((cells + 2 * WIDE, 3 * width), BF),
            pltpu.VMEM((cells + 80, width), F32),
            pltpu.VMEM((cells + 80, width), F32),
            pltpu.VMEM(image.shape, BF),
            pltpu.VMEM((2, image.shape[1], 128), F32),
            pltpu.VMEM((tables, row, part * WIDE, width), BF),
            pltpu.VMEM((tables, cells, width), BF),
            pltpu.SemaphoreType.DMA((batches,)),
            pltpu.SemaphoreType.DMA((tables, row - 1)),
            pltpu.SemaphoreType.DMA((tables, row - 1)),
            pltpu.SemaphoreType.DMA((tables,)),
        ],
        compiler_params=pltpu.CompilerParams(
            vmem_limit_bytes=56 * MIB, collective_id=1, has_side_effects=True
        ),
        name="block_forward",
    )(
        image, lengths, tags, attn_in, attn_out, gain, bias,
        weight, mean, var, scale, shift, proj, proj_bias, attn_in,
    )


def orders(dp, row):
    row_digits = [("row", 1 << i, 2) for i in range(row.bit_length() - 1)]
    far, stride = [], 2
    while stride < dp:
        radix = 2
        far.append(("dp", stride, radix))
        stride *= radix
    pair, others, near = row_digits[:1], row_digits[1:], [("dp", 1, 2)]
    return [pair + near + others + far, pair + others + near + far, pair + far + near + others]


def places(dp, row, route):
    at = {"dp": lax.axis_index("dp"), "row": lax.axis_index("row")}
    weight = {"dp": row, "row": 1}
    here = at["dp"] * row + at["row"]
    peers = [lax.rem(at["row"] + d, row) for d in range(row)]
    peer_ids = [here - at["row"] + peer for peer in peers]
    own, partners = {}, {}
    for digit in route:
        axis, stride, radix = digit
        own[digit] = [lax.rem(at[axis] // stride + d, radix) for d in range(radix)]
        partners[digit] = [
            here + (other - own[digit][0]) * (stride * weight[axis]) for other in own[digit]
        ]
    return peers, peer_ids, own, partners


def timetable(early, late, stages, slots):
    table, chunks, at_unit = {}, [], 0
    for first, count, pitch, size, turns in ((0, early, PITCH, SIZE, EARLY), (slots, late, 1, 1, LATE)):
        seen, last, i = {}, at_unit + count, 0
        while at_unit < last:
            stream = turns[i % len(turns)]
            lag = seen.get(stream, 0)
            seen[stream] = lag + 1
            units = min(size, last - at_unit)
            chunks.append((stream, at_unit, units))
            at_unit, i = at_unit + units, i + 1
            for k in range(2 * stages + 1):
                at = first + pitch * (lag + k)
                if pitch > 1 and at >= slots:
                    at = slots + (at - slots) // pitch
                table.setdefault(at, []).append((len(chunks) - 1, k))
    return {at: steps[::-1] for at, steps in sorted(table.items())}, chunks


class Summing:
    def __init__(self, chunks, routes, own, partners, unit, held, landed, done, total, rows_all, sems):
        self.chunks, self.routes, self.unit, self.partners = chunks, routes, unit, partners
        self.held, self.landed, self.done, self.total, self.rows_all = held, landed, done, total, rows_all
        self.send_sem, self.land_sem, self.back_sem, self.home_sem, self.out_sem = sems
        self.stages = len(routes[0])
        self.plans = {}
        for stream, units in sorted({(stream, units) for stream, _, units in chunks}):
            start, rows, slot, plan = 0, unit * units, 0, []
            for digit in routes[stream]:
                radix = digit[2]
                part = rows // radix
                targets = [start + other * part for other in own[digit]]
                plan.append((targets, part, unit * units - rows, slot, partners[digit]))
                start, rows, slot = targets[0], part, slot + radix - 1
            self.plans[stream, units] = plan

    def plan(self, c, s):
        stream, _, units = self.chunks[c]
        return self.plans[stream, units][s]

    def base(self, c):
        return self.chunks[c][1] * self.unit

    def rows_at(self, c, offset, rows):
        return pl.ds(pl.multiple_of(self.base(c) + offset, 16), rows)

    def out(self, c, s):
        targets, part, landing, slot, partners = self.plan(c, s)
        return [
            pltpu.make_async_remote_copy(
                src_ref=self.held.at[self.rows_at(c, targets[d], part), :],
                dst_ref=self.landed.at[pl.ds(self.base(c) + landing + (d - 1) * part, part), :],
                send_sem=self.send_sem.at[c, slot + d - 1], recv_sem=self.land_sem.at[c, slot + d - 1],
                device_id=partners[d], device_id_type=LOGICAL,
            )
            for d in range(1, len(partners))
        ]

    def back(self, c, s):
        targets, part, _, slot, partners = self.plan(c, s)
        here = self.done.at[self.rows_at(c, targets[0], part), :]
        return [
            pltpu.make_async_remote_copy(
                src_ref=here, dst_ref=here,
                send_sem=self.back_sem.at[c, slot + d - 1], recv_sem=self.home_sem.at[c, slot + d - 1],
                device_id=partners[d], device_id_type=LOGICAL,
            )
            for d in range(1, len(partners))
        ]

    def collect(self, c, s, target):
        targets, part, landing, _, partners = self.plan(c, s)
        for copy in self.out(c, s):
            copy.wait_recv()
        step = min(part, 256)
        for i in range(0, part, step):
            here = self.rows_at(c, targets[0] + i, step)
            found = self.held[here, :].astype(F32)
            for d in range(len(partners) - 1):
                found += self.landed[pl.ds(self.base(c) + landing + d * part + i, step), :].astype(F32)
            target[here, :] = found.astype(BF)

    def finish(self, c):
        rows = pl.ds(self.base(c), min(self.unit * self.chunks[c][2], self.rows_all - self.base(c)))
        return pltpu.make_async_copy(self.done.at[rows, :], self.total.at[rows, :], self.out_sem.at[c])

    def step(self, c, k):
        last = self.stages
        if 0 < k < last:
            self.collect(c, k - 1, self.held)
        elif k == last:
            self.collect(c, k - 1, self.done)
        elif k > last:
            for copy in self.back(c, 2 * last - k):
                copy.wait_recv()
        if k < last:
            copies = self.out(c, k)
        elif k < 2 * last:
            copies = self.back(c, 2 * last - 1 - k)
        else:
            copies = [self.finish(c)]
        for copy in copies:
            copy.start()

    def settle(self):
        for c in range(len(self.chunks)):
            for s in range(self.stages):
                for copy in self.out(c, s) + self.back(c, s):
                    copy.wait_send()
            self.finish(c).wait()


def block_backward_kernel(
    plan, routes, unit, dp, row,
    grad_tokens, padded, hidden, block_out, slope_one, slope_two, norm_one, norm_two,
    weight, var, scale, proj, early, line_gain, line_bias, line_ffn_in, line_ffn_out,
    total, small_total, image_back,
    shifted_two, shifted_one, held, kept, weight_back, conv_sum, proj_sum, bn_sum, bias_sum, image_grad,
    parts, landed, done, small_held, small_landed,
    load_sem, send_sem, land_sem, back_sem, home_sem, out_sem,
    small_send, small_land, image_send, image_land, image_sem,
):
    step = pl.program_id(0)
    tables, cells = image_grad.shape[0], padded.shape[1]
    half = cells // 2
    owned, rows = image_back.shape[1] // row, image_back.shape[2]
    gain = lax.rsqrt(var[...] + EPS) * scale[...]
    peers, peer_ids, own, partners = places(dp, row, routes[0])
    me = peers[0]
    turns, chunks = plan
    stages = len(routes[0])
    early_rows = early.shape[0]
    summing = Summing(
        chunks, routes, own, partners, unit, parts, landed, done, total, total.shape[0],
        (send_sem, land_sem, back_sem, home_sem, out_sem),
    )
    load = pltpu.make_async_copy(early, parts.at[pl.ds(0, early_rows), :], load_sem)

    def image_copy(t, d):
        return pltpu.make_async_remote_copy(
            src_ref=image_grad.at[t, pl.ds(pl.multiple_of(peers[d] * rows, WIDE), rows)],
            dst_ref=image_back.at[t // owned, me * owned + lax.rem(t, owned)],
            send_sem=image_send.at[t, d - 1], recv_sem=image_land.at[t, d - 1],
            device_id=peer_ids[d], device_id_type=LOGICAL,
        )

    def image_keep(t):
        return pltpu.make_async_copy(
            image_grad.at[t, pl.ds(pl.multiple_of(me * rows, WIDE), rows)],
            image_back.at[t // owned, me * owned + lax.rem(t, owned)], image_sem.at[t],
        )

    def slot(phase):
        for t in range(tables):
            steps = turns.get(t * SLOTS + phase)
            if steps:
                @pl.when(step == t)
                def _():
                    for c, k in steps:
                        summing.step(c, k)

    @pl.when(step == 0)
    def _():
        load.start()
        barrier = pltpu.get_barrier_semaphore()
        greeted = peer_ids[1:]
        for digit in routes[0]:
            if digit[0] == "dp":
                greeted = greeted + partners[digit][1:]
        for device in greeted:
            pl.semaphore_signal(barrier, inc=1, device_id=device, device_id_type=LOGICAL)
        clear_edges(shifted_two, (held,), cells)
        clear_edges(shifted_one, (), cells)
        conv_sum[...] = jnp.zeros_like(conv_sum)
        proj_sum[...] = jnp.zeros_like(proj_sum)
        bn_sum[...] = jnp.zeros_like(bn_sum)
        bias_sum[...] = jnp.zeros_like(bias_sum)
        pl.semaphore_wait(barrier, len(greeted))
        load.wait()

    slot(0)

    @pl.when(step == 0)
    def _():
        for layer in range(2):
            for tap in range(9):
                turned = weight[layer, tap * 256 : (tap + 1) * 256, :].T
                weight_back[layer, (8 - tap) * 256 : (9 - tap) * 256, :] = turned

    def add_stats(layer, grad, norm):
        bn_sum[layer : layer + 1, :] += jnp.sum(grad * norm.astype(F32), axis=0, keepdims=True)
        bn_sum[2 + layer : 3 + layer, :] += jnp.sum(grad, axis=0, keepdims=True)

    def add_conv(layer, inputs, shifted):
        turned = inputs.T
        for a in range(3):
            start = (2 - a) * WIDE
            found = dot(turned, shifted[start : start + cells, :])
            for b in range(3):
                conv_sum[layer, a, b] += found[:, (2 - b) * 256 : (3 - b) * 256]

    proj_sum[...] += dot_tn(block_out[0], grad_tokens[0])
    bias_sum[...] += jnp.sum(grad_tokens[0].astype(F32), axis=0, keepdims=True)
    for start in (0, half):
        part = slice(start, start + half)
        grad = slope_two[0, part, :].astype(F32) * dot_nt(grad_tokens[0, part, :], proj[...])
        kept[part, :] = grad
        add_stats(1, grad, norm_two[0, part, :])
        held[LEAD + start : LEAD + start + half, :] = grad * gain[1:2]
    slot(1)
    spread(shifted_two, held, cells)
    for start in (0, half):
        part = slice(start, start + half)
        back = dot(three_rows(shifted_two, start, half), weight_back[1])
        grad = slope_one[0, part, :].astype(F32) * back
        add_stats(0, grad, norm_one[0, part, :])
        held[LEAD + start : LEAD + start + half, :] = grad * gain[0:1]
    slot(2)
    spread(shifted_one, held, cells)
    for start in (0, half):
        back = dot(three_rows(shifted_one, start, half), weight_back[0]) + kept[start : start + half, :]
        image_grad[step, start : start + half, :] = back.astype(BF)
    for d in range(1, row):
        image_copy(step, d).start()
    image_keep(step).start()
    slot(3)
    add_conv(1, hidden[0], shifted_two)
    slot(4)
    add_conv(0, padded[0], shifted_one)

    @pl.when(step == tables - 1)
    def _():
        for a in range(3):
            for b in range(3):
                at = early_rows + (3 * a + b) * 256
                for layer in range(2):
                    lanes = slice(layer * 256, (layer + 1) * 256)
                    parts[at : at + 256, lanes] = conv_sum[layer, a, b].astype(BF)
        at = early_rows + 9 * 256
        parts[at : at + 256, :] = proj_sum[...].astype(BF)
        small_held[0] = jnp.concatenate([
            jnp.concatenate([bn_sum[0:2, :], bn_sum[2:4, :]], axis=1), bias_sum[...], line_ffn_out[...],
            line_ffn_in[:, 0:512], line_ffn_in[:, 512:1024], jnp.zeros((2, 512), F32),
            line_gain[...], line_bias[...], jnp.zeros((2, 512), F32),
        ], axis=0)

        slots = [sum(digit[2] - 1 for digit in routes[0][:s]) for s in range(stages)]

        def small_copies(s):
            return [
                pltpu.make_async_remote_copy(
                    src_ref=small_held.at[s], dst_ref=small_landed.at[slots[s] + d - 1],
                    send_sem=small_send.at[slots[s] + d - 1], recv_sem=small_land.at[slots[s] + d - 1],
                    device_id=partners[routes[0][s]][d], device_id_type=LOGICAL,
                )
                for d in range(1, routes[0][s][2])
            ]

        for at, steps in turns.items():
            if at < tables * SLOTS:
                continue
            s = at - tables * SLOTS
            if 0 < s <= stages:
                found = small_held[s - 1]
                for d, copy in enumerate(small_copies(s - 1)):
                    copy.wait()
                    found += small_landed[slots[s - 1] + d]
                if s < stages:
                    small_held[s] = found
                else:
                    small_total[...] = found
            if s < stages:
                for copy in small_copies(s):
                    copy.start()
            for c, k in steps:
                summing.step(c, k)
        summing.settle()
        for t in range(tables):
            for d in range(1, row):
                image_copy(t, d).wait()
            image_keep(t).wait()


def block_backward(
    grad_tokens, padded, hidden, block_out, slope_one, slope_two, norm_one, norm_two,
    weight, var, scale, proj, early, smalls, dp, row, batches,
):
    tables, cells, model = grad_tokens.shape
    width = proj.shape[0]
    per = per_table(cells, width)
    once = pl.Buffered(1)
    routes = orders(dp, row)
    stages = len(routes[0])
    arrivals = sum(digit[2] - 1 for digit in routes[0])
    unit = 16 * dp * row
    rows = early.shape[0] + 10 * width
    early_units, units = early.shape[0] // unit, -(-rows // unit)
    plan = timetable(early_units, units - early_units, stages, SLOTS * tables)
    far = pl.BlockSpec(memory_space=pl.ANY)
    near = pl.BlockSpec(memory_space=pltpu.VMEM)
    sem = pltpu.SemaphoreType.DMA
    return pl.pallas_call(
        functools.partial(block_backward_kernel, plan, routes, unit, dp, row),
        grid=(tables,),
        in_specs=[per_table(cells, model)] + [per] * 7
        + [pl.BlockSpec(weight.shape, lambda t: (0, 0, 0), pipeline_mode=once)]
        + [whole(2, width)] * 2 + [whole(*proj.shape)] + [far] + [whole(*x.shape) for x in smalls],
        out_specs=[far, whole(16, model), far],
        out_shape=[
            jax.ShapeDtypeStruct((rows, model), BF),
            jax.ShapeDtypeStruct((16, model), F32),
            jax.ShapeDtypeStruct((batches, tables // batches * row, cells // row, width), BF),
        ],
        scratch_shapes=[
            pltpu.VMEM((cells + 2 * WIDE, 3 * width), BF),
            pltpu.VMEM((cells + 2 * WIDE, 3 * width), BF),
            pltpu.VMEM((cells + 80, width), F32),
            pltpu.VMEM((cells, width), F32),
            pltpu.VMEM(weight.shape, BF),
            pltpu.VMEM((2, 3, 3, width, width), F32),
            pltpu.VMEM(proj.shape, F32),
            pltpu.VMEM((4, width), F32),
            pltpu.VMEM((1, model), F32),
            pltpu.VMEM((tables, cells, width), BF),
            pltpu.VMEM((units * unit, model), BF),
            pltpu.VMEM((units * unit, model), BF),
            pltpu.VMEM((units * unit, model), BF),
            pltpu.VMEM((stages, 16, model), F32),
            pltpu.VMEM((arrivals, 16, model), F32),
            sem, sem((units, arrivals)), sem((units, arrivals)),
            sem((units, arrivals)), sem((units, arrivals)), sem((units,)),
            sem((arrivals,)), sem((arrivals,)),
            sem((tables, row - 1)), sem((tables, row - 1)), sem((tables,)),
        ],
        compiler_params=pltpu.CompilerParams(
            vmem_limit_bytes=62 * MIB, collective_id=0, has_side_effects=True
        ),
        name="block_backward",
    )(
        grad_tokens, padded, hidden, block_out, slope_one, slope_two, norm_one, norm_two,
        weight, var, scale, proj, early, *smalls,
    )


def lane_masks(rows, lanes):
    at = lax.broadcasted_iota(jnp.int32, (rows, lanes), 1) // 64
    return [at == h for h in range(GROUP)]


def by_head(value, masks):
    zero = jnp.zeros_like(value)
    return jnp.concatenate([jnp.where(m, value, zero) for m in masks], axis=0)


def own_block(turned):
    depth, slots = turned.shape[0] // GROUP, turned.shape[1] // GROUP
    parts = [
        turned[h * depth : (h + 1) * depth, h * slots : (h + 1) * slots] for h in range(GROUP)
    ]
    return jnp.concatenate(parts, axis=0).T


def softmax_keys(scores):
    raised = jnp.exp(scores - jnp.max(scores, axis=0, keepdims=True))
    return raised * (1.0 / jnp.sum(raised, axis=0, keepdims=True))


def attend(query, key, value, hidden):
    shares = softmax_keys(hidden(dot_nt(key, query) * 0.125)).astype(BF)
    return shares, own_block(dot_tn(value, shares)).astype(BF)


def attend_back(query, key, value, low, upstream):
    shares = low.astype(F32)
    grad_shares = dot_nt(value, upstream)
    mean = jnp.sum(grad_shares * shares, axis=0, keepdims=True)
    grad_scores = (shares * (grad_shares - mean)).astype(BF)
    grad_query = (own_block(dot_tn(key, grad_scores)) * 0.125).astype(BF)
    grad_key = (dot(grad_scores, query) * 0.125).astype(BF)
    return grad_query, grad_key, dot(low, upstream).astype(BF)


def normalise(value):
    center = value - jnp.mean(value, axis=-1, keepdims=True)
    inverse = lax.rsqrt(jnp.mean(center * center, axis=-1, keepdims=True) + EPS)
    return center * inverse, inverse


def norm_back(upstream, gain, unit, inverse):
    scaled = upstream * gain
    mean = jnp.mean(scaled, axis=-1, keepdims=True)
    along = jnp.mean(scaled * unit, axis=-1, keepdims=True)
    return inverse * (scaled - mean - unit * along)


def column_sum(value):
    return jnp.sum(value, axis=0, keepdims=True)


def decoder_kernel(
    ln_gain, ln_bias, ffn_in_bias, ffn_out_bias,
    qkv_far, shares_far, mix_far, first_far, cross_q_far, tags_far, cotangent_far, memory_far, cross_kv_far, attn_in_far, attn_out_far, ffn_in_far, ffn_out_far,
    decoded, tags_grad, grad_tokens, grads_far,
    ln_gain_grad, ln_bias_grad, ffn_in_bias_grad, ffn_out_bias_grad,
    tags, cotangent, memory, cross_kv, attn_in, attn_out, ffn_in, ffn_out,
    qkv, mix, self_shares, first_in, cross_shares, cross_q, up, grad_qkv, grad_q, grad_kv, pair_sum,
    staged, weight_sem, kv_sem, memory_sem, staged_sem,
    grads, grad_sem,
):
    tables, cells = memory_far.shape[0], memory_far.shape[1]
    slots = tags.shape[0] // tables

    def fetch_kv(t):
        return pltpu.make_async_copy(cross_kv_far.at[t], cross_kv.at[t], kv_sem.at[t])

    def fetch_memory(t):
        slot = lax.rem(t, 2)
        return pltpu.make_async_copy(memory_far.at[t], memory.at[slot], memory_sem.at[slot])

    def put_tokens(t):
        slot = lax.rem(t, 2)
        return pltpu.make_async_copy(staged.at[slot], grad_tokens.at[t], staged_sem.at[slot])

    fetches = [
        pltpu.make_async_copy(far, near, weight_sem.at[i])
        for i, (far, near) in enumerate(
            [(first_far, first_in), (cross_q_far, cross_q), (attn_out_far, attn_out)]
            + [(cotangent_far, cotangent), (ffn_in_far, ffn_in), (ffn_out_far, ffn_out)]
            + [(attn_in_far, attn_in), (qkv_far, qkv), (shares_far, self_shares)]
            + [(mix_far, mix.at[0]), (tags_far, tags)]
        )
    ]
    for copy in fetches[:2]:
        copy.start()
    for t in range(tables):
        fetch_kv(t).start()
    for copy in fetches[2:]:
        copy.start()
    fetch_memory(0).start()
    half = 256
    wide_f32 = lane_masks(slots, half)
    real_key = real_columns(cells)

    def put_grad(i, value):
        grads[i] = value.astype(BF)
        copy = pltpu.make_async_copy(grads.at[i], grads_far.at[i], grad_sem.at[i])
        copy.start()
        puts.append(copy)

    puts = []
    for copy in fetches[:2]:
        copy.wait()
    first_unit, first_inv = normalise(first_in[...])
    first = first_unit * ln_gain[0:1] + ln_bias[0:1]
    first_low = first.astype(BF)

    def cross_forward(t, carry):
        fetch_kv(t).wait()
        rows = pl.ds(pl.multiple_of(t * slots, slots), slots)
        for g in range(2):
            lanes = slice(g * half, (g + 1) * half)
            query = by_head(cross_q[rows, lanes], wide_f32)
            value = cross_kv[t, :, 512 + g * half : 512 + (g + 1) * half]
            cross_shares[t, g], mix[1, rows, lanes] = attend(
                query, cross_kv[t, :, lanes], value, lambda x: jnp.where(real_key, x, MASKED)
            )
        return carry

    lax.fori_loop(0, tables, cross_forward, 0)
    fetches[2].wait()
    second_unit, second_inv = normalise(first + dot(mix[1], attn_out[1]))
    second = second_unit * ln_gain[1:2] + ln_bias[1:2]
    second_low = second.astype(BF)
    for copy in fetches[3:6]:
        copy.wait()
    act, slope = gelu_pair(dot(second_low, ffn_in[...]) + ffn_in_bias[...])
    inner_act = act.astype(BF)
    third_unit, third_inv = normalise(second + dot(inner_act, ffn_out[...]) + ffn_out_bias[...])
    decoded[...] = (third_unit * ln_gain[2:3] + ln_bias[2:3]).astype(BF)

    up_three = cotangent[...].astype(F32)
    ln_gain_grad[2:3, :] = column_sum(up_three * third_unit)
    ln_bias_grad[2:3, :] = column_sum(up_three)
    grad_third = norm_back(up_three, ln_gain[2:3], third_unit, third_inv)
    grad_outer = grad_third.astype(BF)
    ffn_out_total = dot_tn(inner_act, grad_outer)
    for k in range(2):
        put_grad(8 + k, ffn_out_total[k * 512 : (k + 1) * 512])
    ffn_out_bias_grad[...] = column_sum(grad_outer.astype(F32))
    grad_inner = (slope * dot_nt(grad_outer, ffn_out[...])).astype(BF)
    ffn_in_total = dot_tn(second_low, grad_inner)
    for k in range(2):
        put_grad(10 + k, ffn_in_total[:, k * 512 : (k + 1) * 512])
    ffn_in_bias_grad[...] = column_sum(grad_inner.astype(F32))
    up_two = grad_third + dot_nt(grad_inner, ffn_in[...])
    ln_gain_grad[1:2, :] = column_sum(up_two * second_unit)
    ln_bias_grad[1:2, :] = column_sum(up_two)
    grad_second = norm_back(up_two, ln_gain[1:2], second_unit, second_inv)
    grad_cross_out = grad_second.astype(BF)
    put_grad(7, dot_tn(mix[1], grad_cross_out))
    up[...] = dot_nt(grad_cross_out, attn_out[1]).astype(BF)
    pair_sum[...] = jnp.zeros_like(pair_sum)
    for copy in fetches[6:]:
        copy.wait()

    def cross_back(t, carry):
        @pl.when(t + 1 < tables)
        def _():
            fetch_memory(t + 1).start()

        rows = pl.ds(pl.multiple_of(t * slots, slots), slots)
        for g in range(2):
            lanes = slice(g * half, (g + 1) * half)
            value_lanes = slice(512 + g * half, 512 + (g + 1) * half)
            query = by_head(cross_q[rows, lanes], wide_f32)
            upstream = by_head(up[rows, lanes], wide_f32)
            grad_q[rows, lanes], grad_kv[:, lanes], grad_kv[:, value_lanes] = attend_back(
                query, cross_kv[t, :, lanes], cross_kv[t, :, value_lanes], cross_shares[t, g], upstream
            )
        @pl.when(t >= 2)
        def _():
            put_tokens(t - 2).wait()

        slot = lax.rem(t, 2)
        staged[slot] = (
            dot_nt(grad_kv[:, 0:512], attn_in[4]) + dot_nt(grad_kv[:, 512:1024], attn_in[5])
        ).astype(BF)
        put_tokens(t).start()
        fetch_memory(t).wait()
        pair_sum[...] += dot_tn(memory[slot], grad_kv[...])
        return carry

    lax.fori_loop(0, tables, cross_back, 0)
    for t in range(max(tables - 2, 0), tables):
        put_tokens(t).wait()
    for k in range(2):
        put_grad(4 + k, pair_sum[:, k * 512 : (k + 1) * 512])
    put_grad(3, dot_tn(first_low, grad_q[...]))
    up_one = grad_second + dot_nt(grad_q[...], attn_in[3])
    ln_gain_grad[0:1, :] = column_sum(up_one * first_unit)
    ln_bias_grad[0:1, :] = column_sum(up_one)
    grad_first = norm_back(up_one, ln_gain[0:1], first_unit, first_inv)
    grad_self_out = grad_first.astype(BF)
    put_grad(6, dot_tn(mix[0], grad_self_out))
    up[...] = dot_nt(grad_self_out, attn_out[0]).astype(BF)

    def self_back(t, carry):
        rows = pl.ds(pl.multiple_of(t * slots, slots), slots)
        for g in range(2):
            lanes = slice(g * half, (g + 1) * half)
            query = by_head(qkv[0, rows, lanes], wide_f32)
            upstream = by_head(up[rows, lanes], wide_f32)
            grad_qkv[0, rows, lanes], grad_qkv[1, rows, lanes], grad_qkv[2, rows, lanes] = attend_back(
                query, qkv[1, rows, lanes], qkv[2, rows, lanes], self_shares[t, g], upstream
            )
        return carry

    lax.fori_loop(0, tables, self_back, 0)
    total = grad_first
    for k in range(3):
        put_grad(k, dot_tn(tags[...], grad_qkv[k]))
        total = total + dot_nt(grad_qkv[k], attn_in[k])
    tags_grad[...] = total
    for copy in puts:
        copy.wait()


def decoder(
    kept, tags, cotangent, memory, cross_kv, attn_in, attn_out, ln_gain, ln_bias,
    ffn_in, ffn_in_bias, ffn_out, ffn_out_bias,
):
    tables, cells, model = memory.shape
    rows = tags.shape[0]
    slots = rows // tables
    inner = ffn_in.shape[1]
    here = pl.BlockSpec(memory_space=pltpu.VMEM)
    far = pl.BlockSpec(memory_space=pl.ANY)
    shape = jax.ShapeDtypeStruct
    stacked = GROUP * slots
    return pl.pallas_call(
        decoder_kernel,
        in_specs=[here] * 4 + [far] * 13,
        out_specs=[here] * 2 + [far] * 2 + [here] * 4,
        out_shape=[
            shape((rows, model), BF), shape((rows, model), F32), shape((tables, cells, model), BF),
            shape((12, 512, model), BF), shape((3, model), F32), shape((3, model), F32),
            shape((1, inner), F32), shape((1, model), F32),
        ],
        scratch_shapes=[
            pltpu.VMEM((rows, model), BF),
            pltpu.VMEM((rows, model), BF),
            pltpu.VMEM((2, cells, model), BF),
            pltpu.VMEM((tables, cells, 2 * model), BF),
            pltpu.VMEM(attn_in.shape, BF),
            pltpu.VMEM(attn_out.shape, BF),
            pltpu.VMEM(ffn_in.shape, BF),
            pltpu.VMEM(ffn_out.shape, BF),
            pltpu.VMEM((3, rows, model), BF),
            pltpu.VMEM((2, rows, model), BF),
            pltpu.VMEM((tables, 2, slots, stacked), BF),
            pltpu.VMEM((rows, model), F32),
            pltpu.VMEM((tables, 2, cells, stacked), BF),
            pltpu.VMEM((rows, model), BF),
            pltpu.VMEM((rows, model), BF),
            pltpu.VMEM((3, rows, model), BF),
            pltpu.VMEM((rows, model), BF),
            pltpu.VMEM((cells, 2 * model), BF),
            pltpu.VMEM((model, 2 * model), F32),
            pltpu.VMEM((2, cells, model), BF),
            pltpu.SemaphoreType.DMA((11,)),
            pltpu.SemaphoreType.DMA((tables,)),
            pltpu.SemaphoreType.DMA((2,)),
            pltpu.SemaphoreType.DMA((2,)),
            pltpu.VMEM((12, 512, model), BF),
            pltpu.SemaphoreType.DMA((12,)),
        ],
        compiler_params=pltpu.CompilerParams(vmem_limit_bytes=60 * MIB),
        name="decoder",
    )(
        ln_gain, ln_bias, ffn_in_bias, ffn_out_bias, *kept,
        tags, cotangent, memory, cross_kv, attn_in, attn_out, ffn_in, ffn_out,
    )


def widen_kernel(
    small, total, back, conv, proj, attn_in, attn_out, ffn_in, ffn_out, image_grad,
    bn_scale, bn_shift, proj_bias, gain, bias, ffn_in_bias, ffn_out_bias,
    narrow, wide, narrow_image, wide_image, in_sem, out_sem, image_in, image_out,
):
    units = in_sem.shape[0]
    batches, group = back.shape[0], back.shape[1]

    def rows(i):
        return pl.ds(i * 512, 512)

    fetches = [
        pltpu.make_async_copy(total.at[rows(i)], narrow.at[rows(i)], in_sem.at[i]) for i in range(units)
    ]
    images = [(b, g) for b in range(batches) for g in range(group)]
    image_fetches = [
        pltpu.make_async_copy(back.at[b, g], narrow_image.at[i], image_in.at[i])
        for i, (b, g) in enumerate(images)
    ]
    for copy in fetches + image_fetches:
        copy.start()
    bn_scale[...] = small[0:2, 0:256]
    bn_shift[...] = small[0:2, 256:512]
    proj_bias[...] = small[2:3, :]
    ffn_out_bias[...] = small[3:4, :]
    ffn_in_bias[:, 0:512] = small[4:5, :]
    ffn_in_bias[:, 512:1024] = small[5:6, :]
    gain[...] = small[8:11, :]
    bias[...] = small[11:14, :]
    slots = wide.shape[0]
    targets = [attn_in.at[i] for i in range(6)] + [attn_out.at[i] for i in range(2)]
    targets += [ffn_out.at[rows(i)] for i in range(2)]
    targets += [ffn_in.at[:, pl.ds(i * 512, 512)] for i in range(2)]
    pending = []

    def put(i, pairs):
        copies = [
            pltpu.make_async_copy(source, target, out_sem.at[i % slots, j])
            for j, (source, target) in enumerate(pairs)
        ]
        for copy in copies:
            copy.start()
        pending.append(copies)

    for i in range(units):
        fetches[i].wait()
        if i >= slots:
            for copy in pending[i - slots]:
                copy.wait()
        slot = wide.at[i % slots]
        slot[...] = narrow[rows(i), :].astype(F32)
        if i < 12:
            put(i, [(slot, targets[i])])
            continue
        pairs = []
        for half in range(2):
            tap = 2 * (i - 12) + half
            here = pl.ds(half * 256, 256)
            if tap < 9:
                for layer in range(2):
                    lanes = pl.ds(layer * 256, 256)
                    pairs.append((slot.at[here, lanes], conv.at[layer, tap // 3, tap % 3]))
            else:
                pairs.append((slot.at[here], proj))
        put(i, pairs)
    waits = []
    for b in range(batches):
        for g in range(group):
            image_fetches[b * group + g].wait()
            for r in range(back.shape[2] // WIDE):
                line = narrow_image[b * group + g, r * WIDE : (r + 1) * WIDE, :].astype(F32)
                for h in range(2):
                    lanes = slice(h * 128, (h + 1) * 128)
                    wide_image[b, h, pl.ds(r * 28 * group + g, 28, stride=group), :] = line[0:28, lanes]
        for h in range(2):
            waits.append(pltpu.make_async_copy(
                wide_image.at[b, h], image_grad.at[b, :, pl.ds(h * 128, 128)], image_out.at[b, h]
            ))
            waits[-1].start()
    for copies in pending[-slots:] + [waits]:
        for copy in copies:
            copy.wait()


def widen(small, total, back, image_shape, width, model, inner):
    rows = total.shape[0]
    units = rows // 512
    batches, group = back.shape[:2]
    far = pl.BlockSpec(memory_space=pl.ANY)
    near = pl.BlockSpec(memory_space=pltpu.VMEM)
    sem = pltpu.SemaphoreType.DMA
    shapes = [
        (2, 3, 3, width, width), (width, model), (6, model, model), (2, model, model),
        (model, inner), (inner, model), image_shape,
    ]
    small_shapes = [(2, width)] * 2 + [(1, model), (3, model), (3, model), (1, inner), (1, model)]
    return pl.pallas_call(
        widen_kernel,
        in_specs=[near] + [far] * 2,
        out_specs=[far] * 7 + [near] * 7,
        out_shape=[jax.ShapeDtypeStruct(s, F32) for s in shapes + small_shapes],
        scratch_shapes=[
            pltpu.VMEM((rows, model), BF),
            pltpu.VMEM((4, 512, model), F32),
            pltpu.VMEM((batches * group,) + back.shape[2:], BF),
            pltpu.VMEM((batches, 2, image_shape[1], 128), F32),
            sem((units,)), sem((4, 4)), sem((batches * group,)), sem((batches, 2)),
        ],
        compiler_params=pltpu.CompilerParams(vmem_limit_bytes=60 * MIB),
        name="widen",
    )(small, total, back)


def body(
    image, tags, tag_lengths, cotangent, conv_weight, bn_mean, bn_var, bn_scale, bn_shift,
    proj_weight, proj_bias, attn_in, attn_out, ln_gain, ln_bias,
    ffn_in, ffn_in_bias, ffn_out, ffn_out_bias,
):
    batches, owned, slots, model = tags.shape
    width = image.shape[-1]
    tables = batches * owned
    row = lax.axis_size("row")
    group, part, breadth = image.shape[1:4]
    flat_image = image.transpose(0, 2, 3, 1, 4).reshape(batches, part * breadth * group, width)
    weight = conv_weight.reshape(2, 9 * width, width)
    forward = block_forward(
        flat_image, tag_lengths.reshape(-1), tags.reshape(-1, model), attn_out, ln_gain, ln_bias,
        weight, bn_mean, bn_var, bn_scale, bn_shift,
        proj_weight, proj_bias.reshape(1, -1), attn_in, row, group, part,
    )
    padded, hidden, block_out, slope_one, slope_two, norm_one, norm_two, memory, cross_kv = forward[:9]
    decoded, tags_grad, grad_tokens, decoder_g, gain_g, bias_g, ffn_in_bias_g, ffn_out_bias_g = decoder(
        forward[9:], tags.reshape(-1, model), cotangent.reshape(-1, model),
        memory, cross_kv, attn_in, attn_out, ln_gain, ln_bias,
        ffn_in, ffn_in_bias.reshape(1, -1), ffn_out, ffn_out_bias.reshape(1, -1),
    )
    total, small, back = block_backward(
        grad_tokens, padded, hidden, block_out, slope_one, slope_two, norm_one, norm_two,
        weight, bn_var, bn_scale, proj_weight, decoder_g.reshape(-1, model),
        (gain_g, bias_g, ffn_in_bias_g, ffn_out_bias_g), lax.axis_size("dp"), row, batches,
    )
    (
        conv_g, proj_g, attn_in_g, attn_out_g, ffn_in_g, ffn_out_g, image_g,
        bn_scale_g, bn_shift_g, proj_bias_g, gain_g, bias_g, ffn_in_bias_g, ffn_out_bias_g,
    ) = widen(small, total, back, flat_image.shape, width, model, ffn_in.shape[1])
    image_g = image_g.reshape(batches, part, breadth, group, width).transpose(0, 3, 1, 2, 4)
    return (
        decoded.reshape(tags.shape), image_g, tags_grad.reshape(tags.shape),
        conv_g, bn_scale_g, bn_shift_g, proj_g, proj_bias_g.reshape(-1),
        attn_in_g, attn_out_g, gain_g, bias_g,
        ffn_in_g, ffn_in_bias_g.reshape(-1), ffn_out_g, ffn_out_bias_g.reshape(-1),
    )


def solution(mesh):
    by_rows = P(None, "dp", "row", None, None)
    by_table = P(None, ("dp", "row"), None, None)
    return jax.shard_map(
        body,
        mesh=mesh,
        in_specs=(by_rows, by_table, P(None, ("dp", "row")), by_table) + (P(),) * 15,
        out_specs=(by_table, by_rows, by_table) + (P(),) * 13,
        check_vma=False,
    )
```

```python
import functools

import jax
import jax.numpy as jnp
from jax import lax
from jax.experimental import pallas as pl
from jax.experimental.pallas import tpu as pltpu
from jax.sharding import PartitionSpec as P

HEADS = 8
GROUP = 4
EPS = 1e-05
MASKED = -1e30
BF = jnp.bfloat16
F32 = jnp.float32
WIDE = 32
LEAD = 40
SLOTS = 5
PITCH = 3
SIZE = 1
EARLY = (0, 2, 1, 0, 1)
LATE = (0, 2, 1, 0, 1)
MIB = 1024 * 1024
MESH = pl.DeviceIdType.MESH
LOGICAL = pl.DeviceIdType.LOGICAL


def dot(left, right):
    return jnp.dot(left, right, preferred_element_type=F32)


def dot_nt(left, right):
    return lax.dot_general(left, right, (((1,), (1,)), ((), ())), preferred_element_type=F32)


def dot_tn(left, right):
    return lax.dot_general(left, right, (((0,), (0,)), ((), ())), preferred_element_type=F32)


def gelu_pair(value):
    cdf = 0.5 + 0.5 * lax.erf(value * 0.7071067811865476)
    density = jnp.exp(value * value * -0.5) * 0.3989422804014327
    return value * cdf, cdf + value * density


def real_columns(rows):
    at = lax.broadcasted_iota(jnp.int32, (rows, 1), 0)
    return lax.rem(at, WIDE) < 28


def spread(shifted, held, cells):
    for b in range(3):
        shifted[WIDE : WIDE + cells, b * 256 : (b + 1) * 256] = held[
            LEAD - 1 + b : LEAD - 1 + b + cells, :
        ].astype(BF)


def three_rows(shifted, start, rows):
    return jnp.concatenate(
        [shifted[start + a * WIDE : start + a * WIDE + rows, :] for a in range(3)], axis=1
    )


def clear_edges(shifted, helds, cells):
    shifted[0:WIDE, :] = jnp.zeros((WIDE, shifted.shape[1]), BF)
    shifted[WIDE + cells :, :] = jnp.zeros((WIDE, shifted.shape[1]), BF)
    for held in helds:
        held[0:LEAD, :] = jnp.zeros((LEAD, held.shape[1]), F32)
        held[LEAD + cells :, :] = jnp.zeros((held.shape[0] - LEAD - cells, held.shape[1]), F32)


def block_forward_kernel(
    row, image, lengths, tags_far, attn_in_far, attn_out_far, gain, bias,
    weight_far, mean, var, scale, shift, proj, proj_bias,
    padded, hidden, block_out, slope_one, slope_two, norm_one, norm_two, memory, cross_kv,
    qkv, self_shares, self_mix, first_in, cross_q,
    tags, self_in, self_out, weight, key_value, weight_sem,
    shifted, held_in, held_mid, raw, loose, sent, landed, load_sem, send_sem, land_sem, home_sem,
):
    table = pl.program_id(0)
    cells = padded.shape[1]
    half = cells // 2
    tables, batches, rows = landed.shape[0], image.shape[0], sent.shape[2]
    owned = tables // batches
    group = owned * row
    me = lax.axis_index("row")
    factor = lax.rsqrt(var[...] + EPS)
    mine = pl.ds(pl.multiple_of(me * rows, WIDE), rows)

    def exchange(t, d):
        peer = lax.rem(me + d, row)
        return pltpu.make_async_remote_copy(
            src_ref=sent.at[t, peer], dst_ref=landed.at[t, mine],
            send_sem=send_sem.at[t, d - 1], recv_sem=land_sem.at[t, d - 1],
            device_id={"row": peer}, device_id_type=MESH,
        )

    def keep(t):
        return pltpu.make_async_copy(sent.at[t, me], landed.at[t, mine], home_sem.at[t])

    def take_apart(b):
        gap = jnp.zeros((WIDE - 28, 128), F32)
        for h in range(2):
            lanes = slice(h * 128, (h + 1) * 128)
            loose[h, 0 : raw.shape[1]] = raw[b, :, lanes].astype(F32)
            for g in range(group):
                for r in range(rows // WIDE):
                    line = loose[h, pl.ds(r * 28 * group + g, 28, stride=group), :]
                    line = jnp.concatenate([line, gap], axis=0).astype(BF)
                    sent[b * owned + g % owned, g // owned, r * WIDE : (r + 1) * WIDE, lanes] = line

    @pl.when(table == 0)
    def _():
        loads = [pltpu.make_async_copy(image.at[b], raw.at[b], load_sem.at[b]) for b in range(batches)]
        fetches = [
            pltpu.make_async_copy(tags_far, tags, weight_sem.at[0]),
            pltpu.make_async_copy(attn_in_far.at[pl.ds(0, 4)], self_in, weight_sem.at[1]),
            pltpu.make_async_copy(attn_out_far.at[0], self_out, weight_sem.at[2]),
            pltpu.make_async_copy(weight_far, weight, weight_sem.at[3]),
            pltpu.make_async_copy(attn_in_far.at[pl.ds(4, 2)], key_value, weight_sem.at[4]),
        ]
        for copy in loads + fetches:
            copy.start()
        barrier = pltpu.get_barrier_semaphore()
        for d in range(1, row):
            pl.semaphore_signal(
                barrier, inc=1, device_id={"row": lax.rem(me + d, row)}, device_id_type=MESH
            )
        for b in range(batches):
            loads[b].wait()
            take_apart(b)
            if b == 0:
                pl.semaphore_wait(barrier, row - 1)
            for t in range(b * owned, (b + 1) * owned):
                for d in range(1, row):
                    exchange(t, d).start()
                keep(t).start()
        clear_edges(shifted, (held_in, held_mid), cells)
        for copy in fetches:
            copy.wait()
        self_forward(
            lengths, tags, self_in, self_out, gain, bias, qkv, self_shares, self_mix, first_in, cross_q
        )

    for d in range(1, row):
        exchange(table, d).wait_recv()
    keep(table).wait()
    padded[0] = landed[table]
    held_in[LEAD : LEAD + cells, :] = landed[table].astype(F32)
    spread(shifted, held_in, cells)
    real = real_columns(half)
    for start in (0, half):
        pre = dot(three_rows(shifted, start, half), weight[0])
        norm = (pre - mean[0:1]) * factor[0:1]
        act, slope = gelu_pair(norm * scale[0:1] + shift[0:1])
        act = jnp.where(real, act, 0.0)
        held_mid[LEAD + start : LEAD + start + half, :] = act
        hidden[0, start : start + half, :] = act.astype(BF)
        slope_one[0, start : start + half, :] = jnp.where(real, slope, 0.0).astype(BF)
        norm_one[0, start : start + half, :] = norm.astype(BF)
    spread(shifted, held_mid, cells)
    for start in (0, half):
        pre = dot(three_rows(shifted, start, half), weight[1])
        norm = (pre - mean[1:2]) * factor[1:2]
        total = norm * scale[1:2] + shift[1:2] + held_in[LEAD + start : LEAD + start + half, :]
        act, slope = gelu_pair(total)
        block = act.astype(BF)
        block_out[0, start : start + half, :] = block
        slope_two[0, start : start + half, :] = slope.astype(BF)
        norm_two[0, start : start + half, :] = norm.astype(BF)
        tokens = (dot(block, proj[...]) + proj_bias[...]).astype(BF)
        memory[0, start : start + half, :] = tokens
        for k in range(2):
            cross_kv[0, start : start + half, k * 512 : (k + 1) * 512] = dot(
                tokens, key_value[k]
            ).astype(BF)

    @pl.when(table == tables - 1)
    def _():
        for t in range(tables):
            for d in range(1, row):
                exchange(t, d).wait_send()


def whole(*shape):
    zeros = (0,) * len(shape)
    return pl.BlockSpec(shape, lambda t: zeros)


def per_table(*shape):
    zeros = (0,) * len(shape)
    return pl.BlockSpec((1,) + shape, lambda t: (t,) + zeros)


def self_forward(lengths, tags, attn_in, attn_out, gain, bias, qkv, shares, mix, first_in, cross_q):
    tables, slots, half, owned = shares.shape[0], shares.shape[2], 256, lengths.shape[1]
    masks = lane_masks(slots, half)
    for k in range(3):
        qkv[k] = dot(tags[...], attn_in[k]).astype(BF)
    key = lax.broadcasted_iota(jnp.int32, (slots, slots), 0)
    query = lax.broadcasted_iota(jnp.int32, (slots, slots), 1)

    def one(t, carry):
        rows = pl.ds(pl.multiple_of(t * slots, slots), slots)
        length = lengths[t // owned, lax.rem(t, owned)]
        allowed = jnp.concatenate([(key <= query) & (key < length)] * GROUP, axis=1)
        for g in range(2):
            lanes = slice(g * half, (g + 1) * half)
            shares[t, g], mix[rows, lanes] = attend(
                by_head(qkv[0, rows, lanes], masks), qkv[1, rows, lanes], qkv[2, rows, lanes],
                lambda x: jnp.where(allowed, x, MASKED),
            )
        return carry

    lax.fori_loop(0, tables, one, 0)
    total = tags[...].astype(F32) + dot(mix[...], attn_out[...])
    first_in[...] = total
    first = normalise(total)[0] * gain[0:1] + bias[0:1]
    cross_q[...] = dot(first.astype(BF), attn_in[3]).astype(BF)


def block_forward(
    image, lengths, tags, attn_out, gain, bias,
    weight, mean, var, scale, shift, proj, proj_bias, attn_in, row, group, part,
):
    batches, width = image.shape[0], image.shape[2]
    tables, cells = batches * (group // row), part * row * WIDE
    model = proj.shape[1]
    small = jax.ShapeDtypeStruct((tables, cells, width), BF)
    stats = [whole(2, width)] * 4
    far = pl.BlockSpec(memory_space=pl.ANY)
    rows = tags.shape[0]
    tag_shapes = [
        ((3, rows, model), BF), ((tables, 2, rows // tables, GROUP * rows // tables), BF),
        ((rows, model), BF), ((rows, model), F32), ((rows, model), BF),
    ]
    return pl.pallas_call(
        functools.partial(block_forward_kernel, row),
        grid=(tables,),
        in_specs=[far, pl.BlockSpec(memory_space=pltpu.SMEM), far, far, far, whole(*gain.shape), whole(*bias.shape)]
        + [far] + stats
        + [whole(*proj.shape), whole(1, model)],
        out_specs=[per_table(cells, width)] * 7 + [per_table(cells, model), per_table(cells, 2 * model)]
        + [whole(*shape) for shape, _ in tag_shapes],
        out_shape=[small] * 7 + [
            jax.ShapeDtypeStruct((tables, cells, model), BF),
            jax.ShapeDtypeStruct((tables, cells, 2 * model), BF),
        ] + [jax.ShapeDtypeStruct(shape, dtype) for shape, dtype in tag_shapes],
        scratch_shapes=[
            pltpu.VMEM((rows, model), BF),
            pltpu.VMEM((4, model, model), BF),
            pltpu.VMEM((model, model), BF),
            pltpu.VMEM(weight.shape, BF),
            pltpu.VMEM((2, model, model), BF),
            pltpu.SemaphoreType.DMA((5,)),
            pltpu.VMEM((cells + 2 * WIDE, 3 * width), BF),
            pltpu.VMEM((cells + 80, width), F32),
            pltpu.VMEM((cells + 80, width), F32),
            pltpu.VMEM(image.shape, BF),
            pltpu.VMEM((2, image.shape[1] + 8 * group, 128), F32),
            pltpu.VMEM((tables, row, part * WIDE, width), BF),
            pltpu.VMEM((tables, cells, width), BF),
            pltpu.SemaphoreType.DMA((batches,)),
            pltpu.SemaphoreType.DMA((tables, row - 1)),
            pltpu.SemaphoreType.DMA((tables, row - 1)),
            pltpu.SemaphoreType.DMA((tables,)),
        ],
        compiler_params=pltpu.CompilerParams(
            vmem_limit_bytes=56 * MIB, collective_id=1, has_side_effects=True
        ),
        name="block_forward",
    )(
        image, lengths, tags, attn_in, attn_out, gain, bias,
        weight, mean, var, scale, shift, proj, proj_bias,
    )


def orders(dp, row):
    row_digits = [("row", 1 << i, 2) for i in range(row.bit_length() - 1)]
    far, stride = [], 2
    while stride < dp:
        radix = 2
        far.append(("dp", stride, radix))
        stride *= radix
    pair, others, near = row_digits[:1], row_digits[1:], [("dp", 1, 2)]
    return [pair + near + others + far, pair + others + near + far, pair + far + near + others]


def places(dp, row, route):
    at = {"dp": lax.axis_index("dp"), "row": lax.axis_index("row")}
    weight = {"dp": row, "row": 1}
    here = at["dp"] * row + at["row"]
    peers = [lax.rem(at["row"] + d, row) for d in range(row)]
    peer_ids = [here - at["row"] + peer for peer in peers]
    own, partners = {}, {}
    for digit in route:
        axis, stride, radix = digit
        own[digit] = [lax.rem(at[axis] // stride + d, radix) for d in range(radix)]
        partners[digit] = [
            here + (other - own[digit][0]) * (stride * weight[axis]) for other in own[digit]
        ]
    return peers, peer_ids, own, partners


def timetable(early, late, stages, slots):
    table, chunks, at_unit = {}, [], 0
    for first, count, pitch, size, turns in ((0, early, PITCH, SIZE, EARLY), (slots, late, 1, 1, LATE)):
        seen, last, i = {}, at_unit + count, 0
        while at_unit < last:
            stream = turns[i % len(turns)]
            lag = seen.get(stream, 0)
            seen[stream] = lag + 1
            units = min(size, last - at_unit)
            chunks.append((stream, at_unit, units))
            at_unit, i = at_unit + units, i + 1
            for k in range(2 * stages + 1):
                at = first + pitch * (lag + k)
                if pitch > 1 and at >= slots:
                    at = slots + (at - slots) // pitch
                table.setdefault(at, []).append((len(chunks) - 1, k))
    return {at: steps[::-1] for at, steps in sorted(table.items())}, chunks


class Summing:
    def __init__(self, chunks, routes, own, partners, unit, held, landed, done, total, rows_all, sems):
        self.chunks, self.routes, self.unit, self.partners = chunks, routes, unit, partners
        self.held, self.landed, self.done, self.total, self.rows_all = held, landed, done, total, rows_all
        self.send_sem, self.land_sem, self.back_sem, self.home_sem, self.out_sem = sems
        self.stages = len(routes[0])
        self.plans = {}
        for stream, units in sorted({(stream, units) for stream, _, units in chunks}):
            start, rows, slot, plan = 0, unit * units, 0, []
            for digit in routes[stream]:
                radix = digit[2]
                part = rows // radix
                targets = [start + other * part for other in own[digit]]
                plan.append((targets, part, unit * units - rows, slot, partners[digit]))
                start, rows, slot = targets[0], part, slot + radix - 1
            self.plans[stream, units] = plan

    def plan(self, c, s):
        stream, _, units = self.chunks[c]
        return self.plans[stream, units][s]

    def base(self, c):
        return self.chunks[c][1] * self.unit

    def rows_at(self, c, offset, rows):
        return pl.ds(pl.multiple_of(self.base(c) + offset, 16), rows)

    def out(self, c, s):
        targets, part, landing, slot, partners = self.plan(c, s)
        return [
            pltpu.make_async_remote_copy(
                src_ref=self.held.at[self.rows_at(c, targets[d], part), :],
                dst_ref=self.landed.at[pl.ds(self.base(c) + landing + (d - 1) * part, part), :],
                send_sem=self.send_sem.at[c, slot + d - 1], recv_sem=self.land_sem.at[c, slot + d - 1],
                device_id=partners[d], device_id_type=LOGICAL,
            )
            for d in range(1, len(partners))
        ]

    def back(self, c, s):
        targets, part, _, slot, partners = self.plan(c, s)
        here = self.done.at[self.rows_at(c, targets[0], part), :]
        return [
            pltpu.make_async_remote_copy(
                src_ref=here, dst_ref=here,
                send_sem=self.back_sem.at[c, slot + d - 1], recv_sem=self.home_sem.at[c, slot + d - 1],
                device_id=partners[d], device_id_type=LOGICAL,
            )
            for d in range(1, len(partners))
        ]

    def collect(self, c, s, target):
        targets, part, landing, _, partners = self.plan(c, s)
        for copy in self.out(c, s):
            copy.wait_recv()
        step = min(part, 256)
        for i in range(0, part, step):
            here = self.rows_at(c, targets[0] + i, step)
            found = self.held[here, :].astype(F32)
            for d in range(len(partners) - 1):
                found += self.landed[pl.ds(self.base(c) + landing + d * part + i, step), :].astype(F32)
            target[here, :] = found.astype(BF)

    def finish(self, c):
        rows = pl.ds(self.base(c), min(self.unit * self.chunks[c][2], self.rows_all - self.base(c)))
        return pltpu.make_async_copy(self.done.at[rows, :], self.total.at[rows, :], self.out_sem.at[c])

    def step(self, c, k):
        last = self.stages
        if 0 < k < last:
            self.collect(c, k - 1, self.held)
        elif k == last:
            self.collect(c, k - 1, self.done)
        elif k > last:
            for copy in self.back(c, 2 * last - k):
                copy.wait_recv()
        if k < last:
            copies = self.out(c, k)
        elif k < 2 * last:
            copies = self.back(c, 2 * last - 1 - k)
        else:
            copies = [self.finish(c)]
        for copy in copies:
            copy.start()

    def settle(self):
        for c in range(len(self.chunks)):
            for s in range(self.stages):
                for copy in self.out(c, s) + self.back(c, s):
                    copy.wait_send()
            self.finish(c).wait()


def block_backward_kernel(
    plan, routes, unit, dp, row,
    grad_tokens, padded, hidden, block_out, slope_one, slope_two, norm_one, norm_two,
    weight_far, var, scale, proj, early, line_gain, line_bias, line_ffn_in, line_ffn_out,
    total, small_total, image_back,
    shifted_two, shifted_one, held, kept, weight, weight_back, conv_sum, proj_sum, bn_sum, bias_sum, image_grad,
    parts, landed, done, small_held, small_landed,
    load_sem, turn_sem, send_sem, land_sem, back_sem, home_sem, out_sem,
    small_send, small_land, image_send, image_land, image_sem,
):
    step = pl.program_id(0)
    tables, cells = image_grad.shape[0], padded.shape[1]
    half = cells // 2
    owned, rows = image_back.shape[1] // row, image_back.shape[2]
    gain = lax.rsqrt(var[...] + EPS) * scale[...]
    peers, peer_ids, own, partners = places(dp, row, routes[0])
    me = peers[0]
    turns, chunks = plan
    stages = len(routes[0])
    early_rows = early.shape[0]
    summing = Summing(
        chunks, routes, own, partners, unit, parts, landed, done, total, total.shape[0],
        (send_sem, land_sem, back_sem, home_sem, out_sem),
    )
    early_units = early_rows // unit

    def load(c):
        here = pl.ds(c * unit, unit)
        return pltpu.make_async_copy(early.at[here, :], parts.at[here, :], load_sem.at[c])

    def advance(c, k):
        if k == 0 and c < early_units:
            load(c).wait()
        summing.step(c, k)

    turn = pltpu.make_async_copy(weight_far, weight, turn_sem)

    def image_copy(t, d):
        return pltpu.make_async_remote_copy(
            src_ref=image_grad.at[t, pl.ds(pl.multiple_of(peers[d] * rows, WIDE), rows)],
            dst_ref=image_back.at[t // owned, me * owned + lax.rem(t, owned)],
            send_sem=image_send.at[t, d - 1], recv_sem=image_land.at[t, d - 1],
            device_id=peer_ids[d], device_id_type=LOGICAL,
        )

    def image_keep(t):
        return pltpu.make_async_copy(
            image_grad.at[t, pl.ds(pl.multiple_of(me * rows, WIDE), rows)],
            image_back.at[t // owned, me * owned + lax.rem(t, owned)], image_sem.at[t],
        )

    def slot(phase):
        for t in range(tables):
            steps = turns.get(t * SLOTS + phase)
            if steps:
                @pl.when(step == t)
                def _():
                    for c, k in steps:
                        advance(c, k)

    @pl.when(step == 0)
    def _():
        for c in range(early_units):
            load(c).start()
        turn.start()
        barrier = pltpu.get_barrier_semaphore()
        greeted = peer_ids[1:]
        for digit in routes[0]:
            if digit[0] == "dp":
                greeted = greeted + partners[digit][1:]
        for device in greeted:
            pl.semaphore_signal(barrier, inc=1, device_id=device, device_id_type=LOGICAL)
        clear_edges(shifted_two, (held,), cells)
        clear_edges(shifted_one, (), cells)
        conv_sum[...] = jnp.zeros_like(conv_sum)
        proj_sum[...] = jnp.zeros_like(proj_sum)
        bn_sum[...] = jnp.zeros_like(bn_sum)
        bias_sum[...] = jnp.zeros_like(bias_sum)
        pl.semaphore_wait(barrier, len(greeted))

    slot(0)

    @pl.when(step == 0)
    def _():
        turn.wait()
        for layer in range(2):
            for tap in range(9):
                turned = weight[layer, tap * 256 : (tap + 1) * 256, :].T
                weight_back[layer, (8 - tap) * 256 : (9 - tap) * 256, :] = turned

    def add_stats(layer, grad, norm):
        bn_sum[layer : layer + 1, :] += jnp.sum(grad * norm.astype(F32), axis=0, keepdims=True)
        bn_sum[2 + layer : 3 + layer, :] += jnp.sum(grad, axis=0, keepdims=True)

    def add_conv(layer, inputs, shifted):
        turned = inputs.T
        for a in range(3):
            start = (2 - a) * WIDE
            found = dot(turned, shifted[start : start + cells, :])
            for b in range(3):
                conv_sum[layer, a, b] += found[:, (2 - b) * 256 : (3 - b) * 256]

    proj_sum[...] += dot_tn(block_out[0], grad_tokens[0])
    bias_sum[...] += jnp.sum(grad_tokens[0].astype(F32), axis=0, keepdims=True)
    for start in (0, half):
        part = slice(start, start + half)
        grad = slope_two[0, part, :].astype(F32) * dot_nt(grad_tokens[0, part, :], proj[...])
        kept[part, :] = grad
        add_stats(1, grad, norm_two[0, part, :])
        held[LEAD + start : LEAD + start + half, :] = grad * gain[1:2]
    slot(1)
    spread(shifted_two, held, cells)
    for start in (0, half):
        part = slice(start, start + half)
        back = dot(three_rows(shifted_two, start, half), weight_back[1])
        grad = slope_one[0, part, :].astype(F32) * back
        add_stats(0, grad, norm_one[0, part, :])
        held[LEAD + start : LEAD + start + half, :] = grad * gain[0:1]
    slot(2)
    spread(shifted_one, held, cells)
    for start in (0, half):
        back = dot(three_rows(shifted_one, start, half), weight_back[0]) + kept[start : start + half, :]
        image_grad[step, start : start + half, :] = back.astype(BF)
    for d in range(1, row):
        image_copy(step, d).start()
    image_keep(step).start()
    slot(3)
    add_conv(1, hidden[0], shifted_two)
    slot(4)
    add_conv(0, padded[0], shifted_one)

    @pl.when(step == tables - 1)
    def _():
        for a in range(3):
            for b in range(3):
                at = early_rows + (3 * a + b) * 256
                for layer in range(2):
                    lanes = slice(layer * 256, (layer + 1) * 256)
                    parts[at : at + 256, lanes] = conv_sum[layer, a, b].astype(BF)
        at = early_rows + 9 * 256
        parts[at : at + 256, :] = proj_sum[...].astype(BF)
        small_held[0] = jnp.concatenate([
            jnp.concatenate([bn_sum[0:2, :], bn_sum[2:4, :]], axis=1), bias_sum[...], line_ffn_out[...],
            line_ffn_in[:, 0:512], line_ffn_in[:, 512:1024], jnp.zeros((2, 512), F32),
            line_gain[...], line_bias[...], jnp.zeros((2, 512), F32),
        ], axis=0)

        slots = [sum(digit[2] - 1 for digit in routes[0][:s]) for s in range(stages)]

        def small_copies(s):
            return [
                pltpu.make_async_remote_copy(
                    src_ref=small_held.at[s], dst_ref=small_landed.at[slots[s] + d - 1],
                    send_sem=small_send.at[slots[s] + d - 1], recv_sem=small_land.at[slots[s] + d - 1],
                    device_id=partners[routes[0][s]][d], device_id_type=LOGICAL,
                )
                for d in range(1, routes[0][s][2])
            ]

        for at, steps in turns.items():
            if at < tables * SLOTS:
                continue
            s = at - tables * SLOTS
            if 0 < s <= stages:
                found = small_held[s - 1]
                for d, copy in enumerate(small_copies(s - 1)):
                    copy.wait()
                    found += small_landed[slots[s - 1] + d]
                if s < stages:
                    small_held[s] = found
                else:
                    small_total[...] = found
            if s < stages:
                for copy in small_copies(s):
                    copy.start()
            for c, k in steps:
                advance(c, k)
        summing.settle()
        for t in range(tables):
            for d in range(1, row):
                image_copy(t, d).wait()
            image_keep(t).wait()


def block_backward(
    grad_tokens, padded, hidden, block_out, slope_one, slope_two, norm_one, norm_two,
    weight, var, scale, proj, early, smalls, dp, row, batches,
):
    tables, cells, model = grad_tokens.shape
    width = proj.shape[0]
    per = per_table(cells, width)
    routes = orders(dp, row)
    stages = len(routes[0])
    arrivals = sum(digit[2] - 1 for digit in routes[0])
    unit = 16 * dp * row
    rows = early.shape[0] + 10 * width
    early_units, units = early.shape[0] // unit, -(-rows // unit)
    plan = timetable(early_units, units - early_units, stages, SLOTS * tables)
    far = pl.BlockSpec(memory_space=pl.ANY)
    near = pl.BlockSpec(memory_space=pltpu.VMEM)
    sem = pltpu.SemaphoreType.DMA
    return pl.pallas_call(
        functools.partial(block_backward_kernel, plan, routes, unit, dp, row),
        grid=(tables,),
        in_specs=[per_table(cells, model)] + [per] * 7
        + [far] + [whole(2, width)] * 2 + [whole(*proj.shape)] + [far] + [whole(*x.shape) for x in smalls],
        out_specs=[far, whole(16, model), far],
        out_shape=[
            jax.ShapeDtypeStruct((rows, model), BF),
            jax.ShapeDtypeStruct((16, model), F32),
            jax.ShapeDtypeStruct((batches, tables // batches * row, cells // row, width), BF),
        ],
        scratch_shapes=[
            pltpu.VMEM((cells + 2 * WIDE, 3 * width), BF),
            pltpu.VMEM((cells + 2 * WIDE, 3 * width), BF),
            pltpu.VMEM((cells + 80, width), F32),
            pltpu.VMEM((cells, width), F32),
            pltpu.VMEM(weight.shape, BF),
            pltpu.VMEM(weight.shape, BF),
            pltpu.VMEM((2, 3, 3, width, width), F32),
            pltpu.VMEM(proj.shape, F32),
            pltpu.VMEM((4, width), F32),
            pltpu.VMEM((1, model), F32),
            pltpu.VMEM((tables, cells, width), BF),
            pltpu.VMEM((units * unit, model), BF),
            pltpu.VMEM((units * unit, model), BF),
            pltpu.VMEM((units * unit, model), BF),
            pltpu.VMEM((stages, 16, model), F32),
            pltpu.VMEM((arrivals, 16, model), F32),
            sem((early_units,)), sem, sem((units, arrivals)), sem((units, arrivals)),
            sem((units, arrivals)), sem((units, arrivals)), sem((units,)),
            sem((arrivals,)), sem((arrivals,)),
            sem((tables, row - 1)), sem((tables, row - 1)), sem((tables,)),
        ],
        compiler_params=pltpu.CompilerParams(
            vmem_limit_bytes=62 * MIB, collective_id=0, has_side_effects=True
        ),
        name="block_backward",
    )(
        grad_tokens, padded, hidden, block_out, slope_one, slope_two, norm_one, norm_two,
        weight, var, scale, proj, early, *smalls,
    )


def lane_masks(rows, lanes):
    at = lax.broadcasted_iota(jnp.int32, (rows, lanes), 1) // 64
    return [at == h for h in range(GROUP)]


def by_head(value, masks):
    zero = jnp.zeros_like(value)
    return jnp.concatenate([jnp.where(m, value, zero) for m in masks], axis=0)


def own_block(turned):
    depth, slots = turned.shape[0] // GROUP, turned.shape[1] // GROUP
    parts = [
        turned[h * depth : (h + 1) * depth, h * slots : (h + 1) * slots] for h in range(GROUP)
    ]
    return jnp.concatenate(parts, axis=0).T


def softmax_keys(scores):
    raised = jnp.exp(scores - jnp.max(scores, axis=0, keepdims=True))
    return raised * (1.0 / jnp.sum(raised, axis=0, keepdims=True))


def attend(query, key, value, hidden):
    shares = softmax_keys(hidden(dot_nt(key, query) * 0.125)).astype(BF)
    return shares, own_block(dot_tn(value, shares)).astype(BF)


def attend_back(query, key, value, low, upstream):
    shares = low.astype(F32)
    grad_shares = dot_nt(value, upstream)
    mean = jnp.sum(grad_shares * shares, axis=0, keepdims=True)
    grad_scores = (shares * (grad_shares - mean)).astype(BF)
    grad_query = (own_block(dot_tn(key, grad_scores)) * 0.125).astype(BF)
    grad_key = (dot(grad_scores, query) * 0.125).astype(BF)
    return grad_query, grad_key, dot(low, upstream).astype(BF)


def normalise(value):
    center = value - jnp.mean(value, axis=-1, keepdims=True)
    inverse = lax.rsqrt(jnp.mean(center * center, axis=-1, keepdims=True) + EPS)
    return center * inverse, inverse


def norm_back(upstream, gain, unit, inverse):
    scaled = upstream * gain
    mean = jnp.mean(scaled, axis=-1, keepdims=True)
    along = jnp.mean(scaled * unit, axis=-1, keepdims=True)
    return inverse * (scaled - mean - unit * along)


def column_sum(value):
    return jnp.sum(value, axis=0, keepdims=True)


def decoder_kernel(
    ln_gain, ln_bias, ffn_in_bias, ffn_out_bias,
    qkv_far, shares_far, mix_far, first_far, cross_q_far, tags_far, cotangent_far, memory_far, cross_kv_far, attn_in_far, attn_out_far, ffn_in_far, ffn_out_far,
    decoded, tags_grad, grad_tokens, grads_far,
    ln_gain_grad, ln_bias_grad, ffn_in_bias_grad, ffn_out_bias_grad,
    tags, cotangent, memory, cross_kv, attn_in, attn_out, ffn_in, ffn_out,
    qkv, mix, self_shares, first_in, cross_shares, cross_q, up, grad_qkv, grad_q, grad_kv, pair_sum,
    staged, weight_sem, kv_sem, memory_sem, staged_sem,
    grads, grad_sem,
):
    tables, cells = memory_far.shape[0], memory_far.shape[1]
    slots = tags.shape[0] // tables

    def fetch_kv(t):
        return pltpu.make_async_copy(cross_kv_far.at[t], cross_kv.at[t], kv_sem.at[t])

    def fetch_memory(t):
        slot = lax.rem(t, 2)
        return pltpu.make_async_copy(memory_far.at[t], memory.at[slot], memory_sem.at[slot])

    def put_tokens(t):
        slot = lax.rem(t, 2)
        return pltpu.make_async_copy(staged.at[slot], grad_tokens.at[t], staged_sem.at[slot])

    fetches = [
        pltpu.make_async_copy(far, near, weight_sem.at[i])
        for i, (far, near) in enumerate(
            [(first_far, first_in), (cross_q_far, cross_q), (attn_out_far, attn_out)]
            + [(cotangent_far, cotangent), (ffn_in_far, ffn_in), (ffn_out_far, ffn_out)]
            + [(attn_in_far, attn_in), (qkv_far, qkv), (shares_far, self_shares)]
            + [(mix_far, mix.at[0]), (tags_far, tags)]
        )
    ]
    for copy in fetches[:2]:
        copy.start()
    for t in range(tables):
        fetch_kv(t).start()
    for copy in fetches[2:]:
        copy.start()
    fetch_memory(0).start()
    half = 256
    wide_f32 = lane_masks(slots, half)
    real_key = real_columns(cells)

    def put_grad(i, value):
        grads[i] = value.astype(BF)
        copy = pltpu.make_async_copy(grads.at[i], grads_far.at[i], grad_sem.at[i])
        copy.start()
        puts.append(copy)

    puts = []
    for copy in fetches[:2]:
        copy.wait()
    first_unit, first_inv = normalise(first_in[...])
    first = first_unit * ln_gain[0:1] + ln_bias[0:1]
    first_low = first.astype(BF)

    def cross_forward(t, carry):
        fetch_kv(t).wait()
        rows = pl.ds(pl.multiple_of(t * slots, slots), slots)
        for g in range(2):
            lanes = slice(g * half, (g + 1) * half)
            query = by_head(cross_q[rows, lanes], wide_f32)
            value = cross_kv[t, :, 512 + g * half : 512 + (g + 1) * half]
            cross_shares[t, g], mix[1, rows, lanes] = attend(
                query, cross_kv[t, :, lanes], value, lambda x: jnp.where(real_key, x, MASKED)
            )
        return carry

    lax.fori_loop(0, tables, cross_forward, 0)
    fetches[2].wait()
    second_unit, second_inv = normalise(first + dot(mix[1], attn_out[1]))
    second = second_unit * ln_gain[1:2] + ln_bias[1:2]
    second_low = second.astype(BF)
    for copy in fetches[3:6]:
        copy.wait()
    act, slope = gelu_pair(dot(second_low, ffn_in[...]) + ffn_in_bias[...])
    inner_act = act.astype(BF)
    third_unit, third_inv = normalise(second + dot(inner_act, ffn_out[...]) + ffn_out_bias[...])
    decoded[...] = (third_unit * ln_gain[2:3] + ln_bias[2:3]).astype(BF)

    up_three = cotangent[...].astype(F32)
    ln_gain_grad[2:3, :] = column_sum(up_three * third_unit)
    ln_bias_grad[2:3, :] = column_sum(up_three)
    grad_third = norm_back(up_three, ln_gain[2:3], third_unit, third_inv)
    grad_outer = grad_third.astype(BF)
    ffn_out_total = dot_tn(inner_act, grad_outer)
    for k in range(2):
        put_grad(8 + k, ffn_out_total[k * 512 : (k + 1) * 512])
    ffn_out_bias_grad[...] = column_sum(grad_outer.astype(F32))
    grad_inner = (slope * dot_nt(grad_outer, ffn_out[...])).astype(BF)
    ffn_in_total = dot_tn(second_low, grad_inner)
    for k in range(2):
        put_grad(10 + k, ffn_in_total[:, k * 512 : (k + 1) * 512])
    ffn_in_bias_grad[...] = column_sum(grad_inner.astype(F32))
    up_two = grad_third + dot_nt(grad_inner, ffn_in[...])
    ln_gain_grad[1:2, :] = column_sum(up_two * second_unit)
    ln_bias_grad[1:2, :] = column_sum(up_two)
    grad_second = norm_back(up_two, ln_gain[1:2], second_unit, second_inv)
    grad_cross_out = grad_second.astype(BF)
    put_grad(7, dot_tn(mix[1], grad_cross_out))
    up[...] = dot_nt(grad_cross_out, attn_out[1]).astype(BF)
    pair_sum[...] = jnp.zeros_like(pair_sum)
    for copy in fetches[6:]:
        copy.wait()

    def cross_back(t, carry):
        @pl.when(t + 1 < tables)
        def _():
            fetch_memory(t + 1).start()

        rows = pl.ds(pl.multiple_of(t * slots, slots), slots)
        for g in range(2):
            lanes = slice(g * half, (g + 1) * half)
            value_lanes = slice(512 + g * half, 512 + (g + 1) * half)
            query = by_head(cross_q[rows, lanes], wide_f32)
            upstream = by_head(up[rows, lanes], wide_f32)
            grad_q[rows, lanes], grad_kv[:, lanes], grad_kv[:, value_lanes] = attend_back(
                query, cross_kv[t, :, lanes], cross_kv[t, :, value_lanes], cross_shares[t, g], upstream
            )
        @pl.when(t >= 2)
        def _():
            put_tokens(t - 2).wait()

        slot = lax.rem(t, 2)
        staged[slot] = (
            dot_nt(grad_kv[:, 0:512], attn_in[4]) + dot_nt(grad_kv[:, 512:1024], attn_in[5])
        ).astype(BF)
        put_tokens(t).start()
        fetch_memory(t).wait()
        pair_sum[...] += dot_tn(memory[slot], grad_kv[...])
        return carry

    lax.fori_loop(0, tables, cross_back, 0)
    for t in range(max(tables - 2, 0), tables):
        put_tokens(t).wait()
    for k in range(2):
        put_grad(4 + k, pair_sum[:, k * 512 : (k + 1) * 512])
    put_grad(3, dot_tn(first_low, grad_q[...]))
    up_one = grad_second + dot_nt(grad_q[...], attn_in[3])
    ln_gain_grad[0:1, :] = column_sum(up_one * first_unit)
    ln_bias_grad[0:1, :] = column_sum(up_one)
    grad_first = norm_back(up_one, ln_gain[0:1], first_unit, first_inv)
    grad_self_out = grad_first.astype(BF)
    put_grad(6, dot_tn(mix[0], grad_self_out))
    up[...] = dot_nt(grad_self_out, attn_out[0]).astype(BF)

    def self_back(t, carry):
        rows = pl.ds(pl.multiple_of(t * slots, slots), slots)
        for g in range(2):
            lanes = slice(g * half, (g + 1) * half)
            query = by_head(qkv[0, rows, lanes], wide_f32)
            upstream = by_head(up[rows, lanes], wide_f32)
            grad_qkv[0, rows, lanes], grad_qkv[1, rows, lanes], grad_qkv[2, rows, lanes] = attend_back(
                query, qkv[1, rows, lanes], qkv[2, rows, lanes], self_shares[t, g], upstream
            )
        return carry

    lax.fori_loop(0, tables, self_back, 0)
    total = grad_first
    for k in range(3):
        put_grad(k, dot_tn(tags[...], grad_qkv[k]))
        total = total + dot_nt(grad_qkv[k], attn_in[k])
    tags_grad[...] = total
    for copy in puts:
        copy.wait()


def decoder(
    kept, tags, cotangent, memory, cross_kv, attn_in, attn_out, ln_gain, ln_bias,
    ffn_in, ffn_in_bias, ffn_out, ffn_out_bias,
):
    tables, cells, model = memory.shape
    rows = tags.shape[0]
    slots = rows // tables
    inner = ffn_in.shape[1]
    here = pl.BlockSpec(memory_space=pltpu.VMEM)
    far = pl.BlockSpec(memory_space=pl.ANY)
    shape = jax.ShapeDtypeStruct
    stacked = GROUP * slots
    return pl.pallas_call(
        decoder_kernel,
        in_specs=[here] * 4 + [far] * 13,
        out_specs=[here] * 2 + [far] * 2 + [here] * 4,
        out_shape=[
            shape((rows, model), BF), shape((rows, model), F32), shape((tables, cells, model), BF),
            shape((12, 512, model), BF), shape((3, model), F32), shape((3, model), F32),
            shape((1, inner), F32), shape((1, model), F32),
        ],
        scratch_shapes=[
            pltpu.VMEM((rows, model), BF),
            pltpu.VMEM((rows, model), BF),
            pltpu.VMEM((2, cells, model), BF),
            pltpu.VMEM((tables, cells, 2 * model), BF),
            pltpu.VMEM(attn_in.shape, BF),
            pltpu.VMEM(attn_out.shape, BF),
            pltpu.VMEM(ffn_in.shape, BF),
            pltpu.VMEM(ffn_out.shape, BF),
            pltpu.VMEM((3, rows, model), BF),
            pltpu.VMEM((2, rows, model), BF),
            pltpu.VMEM((tables, 2, slots, stacked), BF),
            pltpu.VMEM((rows, model), F32),
            pltpu.VMEM((tables, 2, cells, stacked), BF),
            pltpu.VMEM((rows, model), BF),
            pltpu.VMEM((rows, model), BF),
            pltpu.VMEM((3, rows, model), BF),
            pltpu.VMEM((rows, model), BF),
            pltpu.VMEM((cells, 2 * model), BF),
            pltpu.VMEM((model, 2 * model), F32),
            pltpu.VMEM((2, cells, model), BF),
            pltpu.SemaphoreType.DMA((11,)),
            pltpu.SemaphoreType.DMA((tables,)),
            pltpu.SemaphoreType.DMA((2,)),
            pltpu.SemaphoreType.DMA((2,)),
            pltpu.VMEM((12, 512, model), BF),
            pltpu.SemaphoreType.DMA((12,)),
        ],
        compiler_params=pltpu.CompilerParams(vmem_limit_bytes=60 * MIB),
        name="decoder",
    )(
        ln_gain, ln_bias, ffn_in_bias, ffn_out_bias, *kept,
        tags, cotangent, memory, cross_kv, attn_in, attn_out, ffn_in, ffn_out,
    )


def widen_kernel(
    small, total, back, conv, proj, attn_in, attn_out, ffn_in, ffn_out, image_grad,
    bn_scale, bn_shift, proj_bias, gain, bias, ffn_in_bias, ffn_out_bias,
    narrow, wide, narrow_image, wide_image, in_sem, out_sem, image_in, image_out,
):
    units = in_sem.shape[0]
    batches, group = back.shape[0], back.shape[1]

    def rows(i):
        return pl.ds(i * 512, 512)

    fetches = [
        pltpu.make_async_copy(total.at[rows(i)], narrow.at[rows(i)], in_sem.at[i]) for i in range(units)
    ]
    images = [(b, g) for b in range(batches) for g in range(group)]
    image_fetches = [
        pltpu.make_async_copy(back.at[b, g], narrow_image.at[i], image_in.at[i])
        for i, (b, g) in enumerate(images)
    ]
    for copy in fetches + image_fetches:
        copy.start()
    bn_scale[...] = small[0:2, 0:256]
    bn_shift[...] = small[0:2, 256:512]
    proj_bias[...] = small[2:3, :]
    ffn_out_bias[...] = small[3:4, :]
    ffn_in_bias[:, 0:512] = small[4:5, :]
    ffn_in_bias[:, 512:1024] = small[5:6, :]
    gain[...] = small[8:11, :]
    bias[...] = small[11:14, :]
    slots = wide.shape[0]
    targets = [attn_in.at[i] for i in range(6)] + [attn_out.at[i] for i in range(2)]
    targets += [ffn_out.at[rows(i)] for i in range(2)]
    targets += [ffn_in.at[:, pl.ds(i * 512, 512)] for i in range(2)]
    pending = []

    def put(i, pairs):
        copies = [
            pltpu.make_async_copy(source, target, out_sem.at[i % slots, j])
            for j, (source, target) in enumerate(pairs)
        ]
        for copy in copies:
            copy.start()
        pending.append(copies)

    for i in range(units):
        fetches[i].wait()
        if i >= slots:
            for copy in pending[i - slots]:
                copy.wait()
        slot = wide.at[i % slots]
        slot[...] = narrow[rows(i), :].astype(F32)
        if i < 12:
            put(i, [(slot, targets[i])])
            continue
        pairs = []
        for half in range(2):
            tap = 2 * (i - 12) + half
            here = pl.ds(half * 256, 256)
            if tap < 9:
                for layer in range(2):
                    lanes = pl.ds(layer * 256, 256)
                    pairs.append((slot.at[here, lanes], conv.at[layer, tap // 3, tap % 3]))
            else:
                pairs.append((slot.at[here], proj))
        put(i, pairs)
    waits = []
    for b in range(batches):
        for g in range(group):
            image_fetches[b * group + g].wait()
            for r in range(back.shape[2] // WIDE):
                line = narrow_image[b * group + g, r * WIDE : (r + 1) * WIDE, :].astype(F32)
                for h in range(2):
                    lanes = slice(h * 128, (h + 1) * 128)
                    wide_image[b, h, pl.ds(r * 28 * group + g, 28, stride=group), :] = line[0:28, lanes]
        for h in range(2):
            waits.append(pltpu.make_async_copy(
                wide_image.at[b, h, pl.ds(0, image_grad.shape[1])],
                image_grad.at[b, :, pl.ds(h * 128, 128)], image_out.at[b, h],
            ))
            waits[-1].start()
    for copies in pending[-slots:] + [waits]:
        for copy in copies:
            copy.wait()


def widen(small, total, back, image_shape, width, model, inner):
    rows = total.shape[0]
    units = rows // 512
    batches, group = back.shape[:2]
    far = pl.BlockSpec(memory_space=pl.ANY)
    near = pl.BlockSpec(memory_space=pltpu.VMEM)
    sem = pltpu.SemaphoreType.DMA
    shapes = [
        (2, 3, 3, width, width), (width, model), (6, model, model), (2, model, model),
        (model, inner), (inner, model), image_shape,
    ]
    small_shapes = [(2, width)] * 2 + [(1, model), (3, model), (3, model), (1, inner), (1, model)]
    return pl.pallas_call(
        widen_kernel,
        in_specs=[near] + [far] * 2,
        out_specs=[far] * 7 + [near] * 7,
        out_shape=[jax.ShapeDtypeStruct(s, F32) for s in shapes + small_shapes],
        scratch_shapes=[
            pltpu.VMEM((rows, model), BF),
            pltpu.VMEM((4, 512, model), F32),
            pltpu.VMEM((batches * group,) + back.shape[2:], BF),
            pltpu.VMEM((batches, 2, image_shape[1] + 8 * group, 128), F32),
            sem((units,)), sem((4, 4)), sem((batches * group,)), sem((batches, 2)),
        ],
        compiler_params=pltpu.CompilerParams(vmem_limit_bytes=60 * MIB),
        name="widen",
    )(small, total, back)


def body(
    image, tags, tag_lengths, cotangent, conv_weight, bn_mean, bn_var, bn_scale, bn_shift,
    proj_weight, proj_bias, attn_in, attn_out, ln_gain, ln_bias,
    ffn_in, ffn_in_bias, ffn_out, ffn_out_bias,
):
    batches, owned, slots, model = tags.shape
    width = image.shape[-1]
    tables = batches * owned
    row = lax.axis_size("row")
    group, part, breadth = image.shape[1:4]
    flat_image = image.transpose(0, 2, 3, 1, 4).reshape(batches, part * breadth * group, width)
    weight = conv_weight.reshape(2, 9 * width, width)
    forward = block_forward(
        flat_image, tag_lengths, tags.reshape(-1, model), attn_out, ln_gain, ln_bias,
        weight, bn_mean, bn_var, bn_scale, bn_shift,
        proj_weight, proj_bias.reshape(1, -1), attn_in, row, group, part,
    )
    padded, hidden, block_out, slope_one, slope_two, norm_one, norm_two, memory, cross_kv = forward[:9]
    decoded, tags_grad, grad_tokens, decoder_g, gain_g, bias_g, ffn_in_bias_g, ffn_out_bias_g = decoder(
        forward[9:], tags.reshape(-1, model), cotangent.reshape(-1, model),
        memory, cross_kv, attn_in, attn_out, ln_gain, ln_bias,
        ffn_in, ffn_in_bias.reshape(1, -1), ffn_out, ffn_out_bias.reshape(1, -1),
    )
    total, small, back = block_backward(
        grad_tokens, padded, hidden, block_out, slope_one, slope_two, norm_one, norm_two,
        weight, bn_var, bn_scale, proj_weight, decoder_g.reshape(-1, model),
        (gain_g, bias_g, ffn_in_bias_g, ffn_out_bias_g), lax.axis_size("dp"), row, batches,
    )
    (
        conv_g, proj_g, attn_in_g, attn_out_g, ffn_in_g, ffn_out_g, image_g,
        bn_scale_g, bn_shift_g, proj_bias_g, gain_g, bias_g, ffn_in_bias_g, ffn_out_bias_g,
    ) = widen(small, total, back, flat_image.shape, width, model, ffn_in.shape[1])
    image_g = image_g.reshape(batches, part, breadth, group, width).transpose(0, 3, 1, 2, 4)
    return (
        decoded.reshape(tags.shape), image_g, tags_grad.reshape(tags.shape),
        conv_g, bn_scale_g, bn_shift_g, proj_g, proj_bias_g.reshape(-1),
        attn_in_g, attn_out_g, gain_g, bias_g,
        ffn_in_g, ffn_in_bias_g.reshape(-1), ffn_out_g, ffn_out_bias_g.reshape(-1),
    )


def solution(mesh):
    by_rows = P(None, "dp", "row", None, None)
    by_table = P(None, ("dp", "row"), None, None)
    return jax.shard_map(
        body,
        mesh=mesh,
        in_specs=(by_rows, by_table, P(None, ("dp", "row")), by_table) + (P(),) * 15,
        out_specs=(by_table, by_rows, by_table) + (P(),) * 13,
        check_vma=False,
    )
```

```python
import functools

import jax
import jax.numpy as jnp
from jax import lax
from jax.experimental import pallas as pl
from jax.experimental.pallas import tpu as pltpu
from jax.sharding import PartitionSpec as P

HEADS = 8
GROUP = 4
EPS = 1e-05
MASKED = -1e30
BF = jnp.bfloat16
F32 = jnp.float32
WIDE = 32
LEAD = 40
SLOTS = 5
PITCH = 3
SIZE = 1
EARLY = (0, 2, 1, 0, 1)
LATE = (0, 2, 1, 0, 1)
MIB = 1024 * 1024
MESH = pl.DeviceIdType.MESH
LOGICAL = pl.DeviceIdType.LOGICAL


def dot(left, right):
    return jnp.dot(left, right, preferred_element_type=F32)


def dot_nt(left, right):
    return lax.dot_general(left, right, (((1,), (1,)), ((), ())), preferred_element_type=F32)


def dot_tn(left, right):
    return lax.dot_general(left, right, (((0,), (0,)), ((), ())), preferred_element_type=F32)


def gelu_pair(value):
    cdf = 0.5 + 0.5 * lax.erf(value * 0.7071067811865476)
    density = jnp.exp(value * value * -0.5) * 0.3989422804014327
    return value * cdf, cdf + value * density


def real_columns(rows):
    at = lax.broadcasted_iota(jnp.int32, (rows, 1), 0)
    return lax.rem(at, WIDE) < 28


def spread(shifted, held, cells):
    for b in range(3):
        shifted[WIDE : WIDE + cells, b * 256 : (b + 1) * 256] = held[
            LEAD - 1 + b : LEAD - 1 + b + cells, :
        ].astype(BF)


def three_rows(shifted, start, rows):
    return jnp.concatenate(
        [shifted[start + a * WIDE : start + a * WIDE + rows, :] for a in range(3)], axis=1
    )


def clear_edges(shifted, helds, cells):
    shifted[0:WIDE, :] = jnp.zeros((WIDE, shifted.shape[1]), BF)
    shifted[WIDE + cells :, :] = jnp.zeros((WIDE, shifted.shape[1]), BF)
    for held in helds:
        held[0:LEAD, :] = jnp.zeros((LEAD, held.shape[1]), F32)
        held[LEAD + cells :, :] = jnp.zeros((held.shape[0] - LEAD - cells, held.shape[1]), F32)


def block_forward_kernel(
    row, image, lengths, tags_far, attn_in_far, attn_out_far, gain, bias,
    weight_far, mean, var, scale, shift, proj, proj_bias,
    padded, hidden, block_out, slope_one, slope_two, norm_one, norm_two, memory, cross_kv,
    qkv, self_shares, self_mix, first_in, cross_q,
    tags, self_in, self_out, weight, key_value, weight_sem,
    shifted, held_in, held_mid, raw, loose, sent, landed, load_sem, send_sem, land_sem, home_sem,
):
    table = pl.program_id(0)
    cells = padded.shape[1]
    half = cells // 2
    tables, batches, rows = landed.shape[0], image.shape[0], sent.shape[2]
    owned = tables // batches
    group = owned * row
    me = lax.axis_index("row")
    factor = lax.rsqrt(var[...] + EPS)
    mine = pl.ds(pl.multiple_of(me * rows, WIDE), rows)

    def exchange(t, d):
        peer = lax.rem(me + d, row)
        return pltpu.make_async_remote_copy(
            src_ref=sent.at[t, peer], dst_ref=landed.at[t, mine],
            send_sem=send_sem.at[t, d - 1], recv_sem=land_sem.at[t, d - 1],
            device_id={"row": peer}, device_id_type=MESH,
        )

    def keep(t):
        return pltpu.make_async_copy(sent.at[t, me], landed.at[t, mine], home_sem.at[t])

    def take_apart(b):
        gap = jnp.zeros((WIDE - 28, 128), F32)
        for h in range(2):
            lanes = slice(h * 128, (h + 1) * 128)
            loose[h, 0 : raw.shape[1]] = raw[b, :, lanes].astype(F32)
            for g in range(group):
                for r in range(rows // WIDE):
                    line = loose[h, pl.ds(r * 28 * group + g, 28, stride=group), :]
                    line = jnp.concatenate([line, gap], axis=0).astype(BF)
                    sent[b * owned + g % owned, g // owned, r * WIDE : (r + 1) * WIDE, lanes] = line

    @pl.when(table == 0)
    def _():
        loads = [pltpu.make_async_copy(image.at[b], raw.at[b], load_sem.at[b]) for b in range(batches)]
        fetches = [
            pltpu.make_async_copy(tags_far, tags, weight_sem.at[0]),
            pltpu.make_async_copy(attn_in_far.at[pl.ds(0, 4)], self_in, weight_sem.at[1]),
            pltpu.make_async_copy(attn_out_far.at[0], self_out, weight_sem.at[2]),
            pltpu.make_async_copy(weight_far, weight, weight_sem.at[3]),
            pltpu.make_async_copy(attn_in_far.at[pl.ds(4, 2)], key_value, weight_sem.at[4]),
        ]
        for copy in loads + fetches:
            copy.start()
        barrier = pltpu.get_barrier_semaphore()
        for d in range(1, row):
            pl.semaphore_signal(
                barrier, inc=1, device_id={"row": lax.rem(me + d, row)}, device_id_type=MESH
            )
        for b in range(batches):
            loads[b].wait()
            take_apart(b)
            if b == 0:
                pl.semaphore_wait(barrier, row - 1)
            for t in range(b * owned, (b + 1) * owned):
                for d in range(1, row):
                    exchange(t, d).start()
                keep(t).start()
        clear_edges(shifted, (held_in, held_mid), cells)
        for copy in fetches:
            copy.wait()
        self_forward(
            lengths, tags, self_in, self_out, gain, bias, qkv, self_shares, self_mix, first_in, cross_q
        )

    for d in range(1, row):
        exchange(table, d).wait_recv()
    keep(table).wait()
    padded[0] = landed[table]
    held_in[LEAD : LEAD + cells, :] = landed[table].astype(F32)
    spread(shifted, held_in, cells)
    real = real_columns(half)
    for start in (0, half):
        pre = dot(three_rows(shifted, start, half), weight[0])
        norm = (pre - mean[0:1]) * factor[0:1]
        act, slope = gelu_pair(norm * scale[0:1] + shift[0:1])
        act = jnp.where(real, act, 0.0)
        held_mid[LEAD + start : LEAD + start + half, :] = act
        hidden[0, start : start + half, :] = act.astype(BF)
        slope_one[0, start : start + half, :] = jnp.where(real, slope, 0.0).astype(BF)
        norm_one[0, start : start + half, :] = norm.astype(BF)
    spread(shifted, held_mid, cells)
    for start in (0, half):
        pre = dot(three_rows(shifted, start, half), weight[1])
        norm = (pre - mean[1:2]) * factor[1:2]
        total = norm * scale[1:2] + shift[1:2] + held_in[LEAD + start : LEAD + start + half, :]
        act, slope = gelu_pair(total)
        block = act.astype(BF)
        block_out[0, start : start + half, :] = block
        slope_two[0, start : start + half, :] = slope.astype(BF)
        norm_two[0, start : start + half, :] = norm.astype(BF)
        tokens = (dot(block, proj[...]) + proj_bias[...]).astype(BF)
        memory[0, start : start + half, :] = tokens
        for k in range(2):
            cross_kv[0, start : start + half, k * 512 : (k + 1) * 512] = dot(
                tokens, key_value[k]
            ).astype(BF)

    @pl.when(table == tables - 1)
    def _():
        for t in range(tables):
            for d in range(1, row):
                exchange(t, d).wait_send()


def whole(*shape):
    zeros = (0,) * len(shape)
    return pl.BlockSpec(shape, lambda t: zeros)


def per_table(*shape):
    zeros = (0,) * len(shape)
    return pl.BlockSpec((1,) + shape, lambda t: (t,) + zeros)


def self_forward(lengths, tags, attn_in, attn_out, gain, bias, qkv, shares, mix, first_in, cross_q):
    tables, slots, half, owned = shares.shape[0], shares.shape[2], 256, lengths.shape[1]
    masks = lane_masks(slots, half)
    for k in range(3):
        qkv[k] = dot(tags[...], attn_in[k]).astype(BF)
    key = lax.broadcasted_iota(jnp.int32, (slots, slots), 0)
    query = lax.broadcasted_iota(jnp.int32, (slots, slots), 1)

    def one(t, carry):
        rows = pl.ds(pl.multiple_of(t * slots, slots), slots)
        length = lengths[t // owned, lax.rem(t, owned)]
        allowed = jnp.concatenate([(key <= query) & (key < length)] * GROUP, axis=1)
        for g in range(2):
            lanes = slice(g * half, (g + 1) * half)
            shares[t, g], mix[rows, lanes] = attend(
                by_head(qkv[0, rows, lanes], masks), qkv[1, rows, lanes], qkv[2, rows, lanes],
                lambda x: jnp.where(allowed, x, MASKED),
            )
        return carry

    lax.fori_loop(0, tables, one, 0)
    total = tags[...].astype(F32) + dot(mix[...], attn_out[...])
    first_in[...] = total
    first = normalise(total)[0] * gain[0:1] + bias[0:1]
    cross_q[...] = dot(first.astype(BF), attn_in[3]).astype(BF)


def block_forward(
    image, lengths, tags, attn_out, gain, bias,
    weight, mean, var, scale, shift, proj, proj_bias, attn_in, row, group, part,
):
    batches, width = image.shape[0], image.shape[2]
    tables, cells = batches * (group // row), part * row * WIDE
    model = proj.shape[1]
    small = jax.ShapeDtypeStruct((tables, cells, width), BF)
    stats = [whole(2, width)] * 4
    far = pl.BlockSpec(memory_space=pl.ANY)
    rows = tags.shape[0]
    tag_shapes = [
        ((3, rows, model), BF), ((tables, 2, rows // tables, GROUP * rows // tables), BF),
        ((rows, model), BF), ((rows, model), F32), ((rows, model), BF),
    ]
    return pl.pallas_call(
        functools.partial(block_forward_kernel, row),
        grid=(tables,),
        in_specs=[far, pl.BlockSpec(memory_space=pltpu.SMEM), far, far, far, whole(*gain.shape), whole(*bias.shape)]
        + [far] + stats
        + [whole(*proj.shape), whole(1, model)],
        out_specs=[per_table(cells, width)] * 7 + [per_table(cells, model), per_table(cells, 2 * model)]
        + [whole(*shape) for shape, _ in tag_shapes],
        out_shape=[small] * 7 + [
            jax.ShapeDtypeStruct((tables, cells, model), BF),
            jax.ShapeDtypeStruct((tables, cells, 2 * model), BF),
        ] + [jax.ShapeDtypeStruct(shape, dtype) for shape, dtype in tag_shapes],
        scratch_shapes=[
            pltpu.VMEM((rows, model), BF),
            pltpu.VMEM((4, model, model), BF),
            pltpu.VMEM((model, model), BF),
            pltpu.VMEM(weight.shape, BF),
            pltpu.VMEM((2, model, model), BF),
            pltpu.SemaphoreType.DMA((5,)),
            pltpu.VMEM((cells + 2 * WIDE, 3 * width), BF),
            pltpu.VMEM((cells + 80, width), F32),
            pltpu.VMEM((cells + 80, width), F32),
            pltpu.VMEM(image.shape, BF),
            pltpu.VMEM((2, image.shape[1] + 8 * group, 128), F32),
            pltpu.VMEM((tables, row, part * WIDE, width), BF),
            pltpu.VMEM((tables, cells, width), BF),
            pltpu.SemaphoreType.DMA((batches,)),
            pltpu.SemaphoreType.DMA((tables, row - 1)),
            pltpu.SemaphoreType.DMA((tables, row - 1)),
            pltpu.SemaphoreType.DMA((tables,)),
        ],
        compiler_params=pltpu.CompilerParams(
            vmem_limit_bytes=56 * MIB, collective_id=1, has_side_effects=True
        ),
        name="block_forward",
    )(
        image, lengths, tags, attn_in, attn_out, gain, bias,
        weight, mean, var, scale, shift, proj, proj_bias,
    )


def orders(dp, row):
    row_digits = [("row", 1 << i, 2) for i in range(row.bit_length() - 1)]
    far, stride = [], 2
    while stride < dp:
        radix = 2
        far.append(("dp", stride, radix))
        stride *= radix
    pair, others, near = row_digits[:1], row_digits[1:], [("dp", 1, 2)]
    return [pair + near + others + far, pair + others + near + far, pair + far + near + others]


def places(dp, row, route):
    at = {"dp": lax.axis_index("dp"), "row": lax.axis_index("row")}
    weight = {"dp": row, "row": 1}
    here = at["dp"] * row + at["row"]
    peers = [lax.rem(at["row"] + d, row) for d in range(row)]
    peer_ids = [here - at["row"] + peer for peer in peers]
    own, partners = {}, {}
    for digit in route:
        axis, stride, radix = digit
        own[digit] = [lax.rem(at[axis] // stride + d, radix) for d in range(radix)]
        partners[digit] = [
            here + (other - own[digit][0]) * (stride * weight[axis]) for other in own[digit]
        ]
    return peers, peer_ids, own, partners


def timetable(early, late, stages, slots):
    table, chunks, at_unit = {}, [], 0
    for first, count, pitch, size, turns in ((0, early, PITCH, SIZE, EARLY), (slots, late, 1, 1, LATE)):
        seen, last, i = {}, at_unit + count, 0
        while at_unit < last:
            stream = turns[i % len(turns)]
            lag = seen.get(stream, 0)
            seen[stream] = lag + 1
            units = min(size, last - at_unit)
            chunks.append((stream, at_unit, units))
            at_unit, i = at_unit + units, i + 1
            for k in range(2 * stages + 1):
                at = first + pitch * (lag + k)
                if pitch > 1 and at >= slots:
                    at = slots + (at - slots) // pitch
                table.setdefault(at, []).append((len(chunks) - 1, k))
    return {at: sorted(steps, key=lambda step: step[1]) for at, steps in sorted(table.items())}, chunks


class Summing:
    def __init__(self, chunks, routes, own, partners, unit, held, landed, done, total, rows_all, sems):
        self.chunks, self.routes, self.unit, self.partners = chunks, routes, unit, partners
        self.held, self.landed, self.done, self.total, self.rows_all = held, landed, done, total, rows_all
        self.send_sem, self.land_sem, self.back_sem, self.home_sem, self.out_sem = sems
        self.stages = len(routes[0])
        self.plans = {}
        for stream, units in sorted({(stream, units) for stream, _, units in chunks}):
            start, rows, slot, plan = 0, unit * units, 0, []
            for digit in routes[stream]:
                radix = digit[2]
                part = rows // radix
                targets = [start + other * part for other in own[digit]]
                plan.append((targets, part, unit * units - rows, slot, partners[digit]))
                start, rows, slot = targets[0], part, slot + radix - 1
            self.plans[stream, units] = plan

    def plan(self, c, s):
        stream, _, units = self.chunks[c]
        return self.plans[stream, units][s]

    def base(self, c):
        return self.chunks[c][1] * self.unit

    def rows_at(self, c, offset, rows):
        return pl.ds(pl.multiple_of(self.base(c) + offset, 16), rows)

    def out(self, c, s):
        targets, part, landing, slot, partners = self.plan(c, s)
        return [
            pltpu.make_async_remote_copy(
                src_ref=self.held.at[self.rows_at(c, targets[d], part), :],
                dst_ref=self.landed.at[pl.ds(self.base(c) + landing + (d - 1) * part, part), :],
                send_sem=self.send_sem.at[c, slot + d - 1], recv_sem=self.land_sem.at[c, slot + d - 1],
                device_id=partners[d], device_id_type=LOGICAL,
            )
            for d in range(1, len(partners))
        ]

    def back(self, c, s):
        targets, part, _, slot, partners = self.plan(c, s)
        here = self.done.at[self.rows_at(c, targets[0], part), :]
        return [
            pltpu.make_async_remote_copy(
                src_ref=here, dst_ref=here,
                send_sem=self.back_sem.at[c, slot + d - 1], recv_sem=self.home_sem.at[c, slot + d - 1],
                device_id=partners[d], device_id_type=LOGICAL,
            )
            for d in range(1, len(partners))
        ]

    def collect(self, c, s, target):
        targets, part, landing, _, partners = self.plan(c, s)
        for copy in self.out(c, s):
            copy.wait_recv()
        step = min(part, 256)
        for i in range(0, part, step):
            here = self.rows_at(c, targets[0] + i, step)
            found = self.held[here, :].astype(F32)
            for d in range(len(partners) - 1):
                found += self.landed[pl.ds(self.base(c) + landing + d * part + i, step), :].astype(F32)
            target[here, :] = found.astype(BF)

    def finish(self, c):
        rows = pl.ds(self.base(c), min(self.unit * self.chunks[c][2], self.rows_all - self.base(c)))
        return pltpu.make_async_copy(self.done.at[rows, :], self.total.at[rows, :], self.out_sem.at[c])

    def step(self, c, k):
        last = self.stages
        if 0 < k < last:
            self.collect(c, k - 1, self.held)
        elif k == last:
            self.collect(c, k - 1, self.done)
        elif k > last:
            for copy in self.back(c, 2 * last - k):
                copy.wait_recv()
        if k < last:
            copies = self.out(c, k)
        elif k < 2 * last:
            copies = self.back(c, 2 * last - 1 - k)
        else:
            copies = [self.finish(c)]
        for copy in copies:
            copy.start()

    def settle(self):
        for c in range(len(self.chunks)):
            for s in range(self.stages):
                for copy in self.out(c, s) + self.back(c, s):
                    copy.wait_send()
            self.finish(c).wait()


def block_backward_kernel(
    plan, routes, unit, dp, row,
    grad_tokens, padded, hidden, block_out, slope_one, slope_two, norm_one, norm_two,
    weight_far, var, scale, proj, early, line_gain, line_bias, line_ffn_in, line_ffn_out,
    total, small_total, image_back,
    shifted_two, shifted_one, held, kept, weight, weight_back, conv_sum, proj_sum, bn_sum, bias_sum, image_grad,
    parts, landed, done, small_held, small_landed,
    load_sem, turn_sem, send_sem, land_sem, back_sem, home_sem, out_sem,
    small_send, small_land, image_send, image_land, image_sem,
):
    step = pl.program_id(0)
    tables, cells = image_grad.shape[0], padded.shape[1]
    half = cells // 2
    owned, rows = image_back.shape[1] // row, image_back.shape[2]
    gain = lax.rsqrt(var[...] + EPS) * scale[...]
    peers, peer_ids, own, partners = places(dp, row, routes[0])
    me = peers[0]
    turns, chunks = plan
    stages = len(routes[0])
    early_rows = early.shape[0]
    summing = Summing(
        chunks, routes, own, partners, unit, parts, landed, done, total, total.shape[0],
        (send_sem, land_sem, back_sem, home_sem, out_sem),
    )
    early_units = early_rows // unit

    def load(c):
        here = pl.ds(c * unit, unit)
        return pltpu.make_async_copy(early.at[here, :], parts.at[here, :], load_sem.at[c])

    def advance(c, k):
        if k == 0 and c < early_units:
            load(c).wait()
        summing.step(c, k)

    turn = pltpu.make_async_copy(weight_far, weight, turn_sem)

    def image_copy(t, d):
        return pltpu.make_async_remote_copy(
            src_ref=image_grad.at[t, pl.ds(pl.multiple_of(peers[d] * rows, WIDE), rows)],
            dst_ref=image_back.at[t // owned, me * owned + lax.rem(t, owned)],
            send_sem=image_send.at[t, d - 1], recv_sem=image_land.at[t, d - 1],
            device_id=peer_ids[d], device_id_type=LOGICAL,
        )

    def image_keep(t):
        return pltpu.make_async_copy(
            image_grad.at[t, pl.ds(pl.multiple_of(me * rows, WIDE), rows)],
            image_back.at[t // owned, me * owned + lax.rem(t, owned)], image_sem.at[t],
        )

    def slot(phase):
        for t in range(tables):
            steps = turns.get(t * SLOTS + phase)
            if steps:
                @pl.when(step == t)
                def _():
                    for c, k in steps:
                        advance(c, k)

    @pl.when(step == 0)
    def _():
        for c in range(early_units):
            load(c).start()
        turn.start()
        barrier = pltpu.get_barrier_semaphore()
        greeted = peer_ids[1:]
        for digit in routes[0]:
            if digit[0] == "dp":
                greeted = greeted + partners[digit][1:]
        for device in greeted:
            pl.semaphore_signal(barrier, inc=1, device_id=device, device_id_type=LOGICAL)
        clear_edges(shifted_two, (held,), cells)
        clear_edges(shifted_one, (), cells)
        conv_sum[...] = jnp.zeros_like(conv_sum)
        proj_sum[...] = jnp.zeros_like(proj_sum)
        bn_sum[...] = jnp.zeros_like(bn_sum)
        bias_sum[...] = jnp.zeros_like(bias_sum)
        pl.semaphore_wait(barrier, len(greeted))

    slot(0)

    @pl.when(step == 0)
    def _():
        turn.wait()
        for layer in range(2):
            for tap in range(9):
                turned = weight[layer, tap * 256 : (tap + 1) * 256, :].T
                weight_back[layer, (8 - tap) * 256 : (9 - tap) * 256, :] = turned

    def add_stats(layer, grad, norm):
        bn_sum[layer : layer + 1, :] += jnp.sum(grad * norm.astype(F32), axis=0, keepdims=True)
        bn_sum[2 + layer : 3 + layer, :] += jnp.sum(grad, axis=0, keepdims=True)

    def add_conv(layer, inputs, shifted):
        turned = inputs.T
        for a in range(3):
            start = (2 - a) * WIDE
            found = dot(turned, shifted[start : start + cells, :])
            for b in range(3):
                conv_sum[layer, a, b] += found[:, (2 - b) * 256 : (3 - b) * 256]

    proj_sum[...] += dot_tn(block_out[0], grad_tokens[0])
    bias_sum[...] += jnp.sum(grad_tokens[0].astype(F32), axis=0, keepdims=True)
    for start in (0, half):
        part = slice(start, start + half)
        grad = slope_two[0, part, :].astype(F32) * dot_nt(grad_tokens[0, part, :], proj[...])
        kept[part, :] = grad
        add_stats(1, grad, norm_two[0, part, :])
        held[LEAD + start : LEAD + start + half, :] = grad * gain[1:2]
    slot(1)
    spread(shifted_two, held, cells)
    for start in (0, half):
        part = slice(start, start + half)
        back = dot(three_rows(shifted_two, start, half), weight_back[1])
        grad = slope_one[0, part, :].astype(F32) * back
        add_stats(0, grad, norm_one[0, part, :])
        held[LEAD + start : LEAD + start + half, :] = grad * gain[0:1]
    slot(2)
    spread(shifted_one, held, cells)
    for start in (0, half):
        back = dot(three_rows(shifted_one, start, half), weight_back[0]) + kept[start : start + half, :]
        image_grad[step, start : start + half, :] = back.astype(BF)
    for d in range(1, row):
        image_copy(step, d).start()
    image_keep(step).start()
    slot(3)
    add_conv(1, hidden[0], shifted_two)
    slot(4)
    add_conv(0, padded[0], shifted_one)

    @pl.when(step == tables - 1)
    def _():
        for a in range(3):
            for b in range(3):
                at = early_rows + (3 * a + b) * 256
                for layer in range(2):
                    lanes = slice(layer * 256, (layer + 1) * 256)
                    parts[at : at + 256, lanes] = conv_sum[layer, a, b].astype(BF)
        at = early_rows + 9 * 256
        parts[at : at + 256, :] = proj_sum[...].astype(BF)
        small_held[0] = jnp.concatenate([
            jnp.concatenate([bn_sum[0:2, :], bn_sum[2:4, :]], axis=1), bias_sum[...], line_ffn_out[...],
            line_ffn_in[:, 0:512], line_ffn_in[:, 512:1024], jnp.zeros((2, 512), F32),
            line_gain[...], line_bias[...], jnp.zeros((2, 512), F32),
        ], axis=0)

        slots = [sum(digit[2] - 1 for digit in routes[0][:s]) for s in range(stages)]

        def small_copies(s):
            return [
                pltpu.make_async_remote_copy(
                    src_ref=small_held.at[s], dst_ref=small_landed.at[slots[s] + d - 1],
                    send_sem=small_send.at[slots[s] + d - 1], recv_sem=small_land.at[slots[s] + d - 1],
                    device_id=partners[routes[0][s]][d], device_id_type=LOGICAL,
                )
                for d in range(1, routes[0][s][2])
            ]

        for at, steps in turns.items():
            if at < tables * SLOTS:
                continue
            s = at - tables * SLOTS
            if 0 < s <= stages:
                found = small_held[s - 1]
                for d, copy in enumerate(small_copies(s - 1)):
                    copy.wait()
                    found += small_landed[slots[s - 1] + d]
                if s < stages:
                    small_held[s] = found
                else:
                    small_total[...] = found
            if s < stages:
                for copy in small_copies(s):
                    copy.start()
            for c, k in steps:
                advance(c, k)
        summing.settle()
        for t in range(tables):
            for d in range(1, row):
                image_copy(t, d).wait()
            image_keep(t).wait()


def block_backward(
    grad_tokens, padded, hidden, block_out, slope_one, slope_two, norm_one, norm_two,
    weight, var, scale, proj, early, smalls, dp, row, batches,
):
    tables, cells, model = grad_tokens.shape
    width = proj.shape[0]
    per = per_table(cells, width)
    routes = orders(dp, row)
    stages = len(routes[0])
    arrivals = sum(digit[2] - 1 for digit in routes[0])
    unit = 16 * dp * row
    rows = early.shape[0] + 10 * width
    early_units, units = early.shape[0] // unit, -(-rows // unit)
    plan = timetable(early_units, units - early_units, stages, SLOTS * tables)
    far = pl.BlockSpec(memory_space=pl.ANY)
    near = pl.BlockSpec(memory_space=pltpu.VMEM)
    sem = pltpu.SemaphoreType.DMA
    return pl.pallas_call(
        functools.partial(block_backward_kernel, plan, routes, unit, dp, row),
        grid=(tables,),
        in_specs=[per_table(cells, model)] + [per] * 7
        + [far] + [whole(2, width)] * 2 + [whole(*proj.shape)] + [far] + [whole(*x.shape) for x in smalls],
        out_specs=[far, whole(16, model), far],
        out_shape=[
            jax.ShapeDtypeStruct((rows, model), BF),
            jax.ShapeDtypeStruct((16, model), F32),
            jax.ShapeDtypeStruct((batches, tables // batches * row, cells // row, width), BF),
        ],
        scratch_shapes=[
            pltpu.VMEM((cells + 2 * WIDE, 3 * width), BF),
            pltpu.VMEM((cells + 2 * WIDE, 3 * width), BF),
            pltpu.VMEM((cells + 80, width), F32),
            pltpu.VMEM((cells, width), F32),
            pltpu.VMEM(weight.shape, BF),
            pltpu.VMEM(weight.shape, BF),
            pltpu.VMEM((2, 3, 3, width, width), F32),
            pltpu.VMEM(proj.shape, F32),
            pltpu.VMEM((4, width), F32),
            pltpu.VMEM((1, model), F32),
            pltpu.VMEM((tables, cells, width), BF),
            pltpu.VMEM((units * unit, model), BF),
            pltpu.VMEM((units * unit, model), BF),
            pltpu.VMEM((units * unit, model), BF),
            pltpu.VMEM((stages, 16, model), F32),
            pltpu.VMEM((arrivals, 16, model), F32),
            sem((early_units,)), sem, sem((units, arrivals)), sem((units, arrivals)),
            sem((units, arrivals)), sem((units, arrivals)), sem((units,)),
            sem((arrivals,)), sem((arrivals,)),
            sem((tables, row - 1)), sem((tables, row - 1)), sem((tables,)),
        ],
        compiler_params=pltpu.CompilerParams(
            vmem_limit_bytes=62 * MIB, collective_id=0, has_side_effects=True
        ),
        name="block_backward",
    )(
        grad_tokens, padded, hidden, block_out, slope_one, slope_two, norm_one, norm_two,
        weight, var, scale, proj, early, *smalls,
    )


def lane_masks(rows, lanes):
    at = lax.broadcasted_iota(jnp.int32, (rows, lanes), 1) // 64
    return [at == h for h in range(GROUP)]


def by_head(value, masks):
    zero = jnp.zeros_like(value)
    return jnp.concatenate([jnp.where(m, value, zero) for m in masks], axis=0)


def own_block(turned):
    depth, slots = turned.shape[0] // GROUP, turned.shape[1] // GROUP
    parts = [
        turned[h * depth : (h + 1) * depth, h * slots : (h + 1) * slots] for h in range(GROUP)
    ]
    return jnp.concatenate(parts, axis=0).T


def softmax_keys(scores):
    raised = jnp.exp(scores - jnp.max(scores, axis=0, keepdims=True))
    return raised * (1.0 / jnp.sum(raised, axis=0, keepdims=True))


def attend(query, key, value, hidden):
    shares = softmax_keys(hidden(dot_nt(key, query * 0.125))).astype(BF)
    return shares, own_block(dot_tn(value, shares)).astype(BF)


def attend_back(query, key, value, low, upstream):
    shares = low.astype(F32)
    grad_shares = dot_nt(value, upstream)
    mean = jnp.sum(grad_shares * shares, axis=0, keepdims=True)
    grad_scores = (shares * (grad_shares - mean)).astype(BF)
    grad_query = (own_block(dot_tn(key, grad_scores)) * 0.125).astype(BF)
    grad_key = dot(grad_scores, query * 0.125).astype(BF)
    return grad_query, grad_key, dot(low, upstream).astype(BF)


def normalise(value):
    center = value - jnp.mean(value, axis=-1, keepdims=True)
    inverse = lax.rsqrt(jnp.mean(center * center, axis=-1, keepdims=True) + EPS)
    return center * inverse, inverse


def norm_back(upstream, gain, unit, inverse):
    scaled = upstream * gain
    mean = jnp.mean(scaled, axis=-1, keepdims=True)
    along = jnp.mean(scaled * unit, axis=-1, keepdims=True)
    return inverse * (scaled - mean - unit * along)


def column_sum(value):
    return jnp.sum(value, axis=0, keepdims=True)


def decoder_kernel(
    ln_gain, ln_bias, ffn_in_bias, ffn_out_bias,
    qkv_far, shares_far, mix_far, first_far, cross_q_far, tags_far, cotangent_far, memory_far, cross_kv_far, attn_in_far, attn_out_far, ffn_in_far, ffn_out_far,
    decoded, tags_grad, grad_tokens, grads_far,
    ln_gain_grad, ln_bias_grad, ffn_in_bias_grad, ffn_out_bias_grad,
    tags, cotangent, memory, cross_kv, attn_in, attn_out, ffn_in, ffn_out,
    qkv, mix, self_shares, first_in, cross_shares, cross_q, up, grad_qkv, grad_q, grad_kv, pair_sum,
    staged, weight_sem, kv_sem, memory_sem, staged_sem,
    grads, grad_sem,
):
    tables, cells = memory_far.shape[0], memory_far.shape[1]
    slots = tags.shape[0] // tables

    def fetch_kv(t):
        return pltpu.make_async_copy(cross_kv_far.at[t], cross_kv.at[t], kv_sem.at[t])

    def fetch_memory(t):
        slot = lax.rem(t, 2)
        return pltpu.make_async_copy(memory_far.at[t], memory.at[slot], memory_sem.at[slot])

    def put_tokens(t):
        slot = lax.rem(t, 2)
        return pltpu.make_async_copy(staged.at[slot], grad_tokens.at[t], staged_sem.at[slot])

    fetches = [
        pltpu.make_async_copy(far, near, weight_sem.at[i])
        for i, (far, near) in enumerate(
            [(first_far, first_in), (cross_q_far, cross_q), (attn_out_far, attn_out)]
            + [(cotangent_far, cotangent), (ffn_in_far, ffn_in), (ffn_out_far, ffn_out)]
            + [(attn_in_far, attn_in), (qkv_far, qkv), (shares_far, self_shares)]
            + [(mix_far, mix.at[0]), (tags_far, tags)]
        )
    ]
    for copy in fetches[:2]:
        copy.start()
    for t in range(tables):
        fetch_kv(t).start()
    for copy in fetches[2:]:
        copy.start()
    fetch_memory(0).start()
    half = 256
    wide_f32 = lane_masks(slots, half)
    real_key = real_columns(cells)

    def put_grad(i, value):
        grads[i] = value.astype(BF)
        copy = pltpu.make_async_copy(grads.at[i], grads_far.at[i], grad_sem.at[i])
        copy.start()
        puts.append(copy)

    puts = []
    for copy in fetches[:2]:
        copy.wait()
    first_unit, first_inv = normalise(first_in[...])
    first = first_unit * ln_gain[0:1] + ln_bias[0:1]
    first_low = first.astype(BF)

    def cross_forward(t, carry):
        fetch_kv(t).wait()
        rows = pl.ds(pl.multiple_of(t * slots, slots), slots)
        for g in range(2):
            lanes = slice(g * half, (g + 1) * half)
            query = by_head(cross_q[rows, lanes], wide_f32)
            value = cross_kv[t, :, 512 + g * half : 512 + (g + 1) * half]
            cross_shares[t, g], mix[1, rows, lanes] = attend(
                query, cross_kv[t, :, lanes], value, lambda x: jnp.where(real_key, x, MASKED)
            )
        return carry

    lax.fori_loop(0, tables, cross_forward, 0)
    fetches[2].wait()
    second_unit, second_inv = normalise(first + dot(mix[1], attn_out[1]))
    second = second_unit * ln_gain[1:2] + ln_bias[1:2]
    second_low = second.astype(BF)
    for copy in fetches[3:6]:
        copy.wait()
    act, slope = gelu_pair(dot(second_low, ffn_in[...]) + ffn_in_bias[...])
    inner_act = act.astype(BF)
    third_unit, third_inv = normalise(second + dot(inner_act, ffn_out[...]) + ffn_out_bias[...])
    decoded[...] = (third_unit * ln_gain[2:3] + ln_bias[2:3]).astype(BF)

    up_three = cotangent[...].astype(F32)
    ln_gain_grad[2:3, :] = column_sum(up_three * third_unit)
    ln_bias_grad[2:3, :] = column_sum(up_three)
    grad_third = norm_back(up_three, ln_gain[2:3], third_unit, third_inv)
    grad_outer = grad_third.astype(BF)
    ffn_out_total = dot_tn(inner_act, grad_outer)
    for k in range(2):
        put_grad(8 + k, ffn_out_total[k * 512 : (k + 1) * 512])
    ffn_out_bias_grad[...] = column_sum(grad_outer.astype(F32))
    grad_inner = (slope * dot_nt(grad_outer, ffn_out[...])).astype(BF)
    ffn_in_total = dot_tn(second_low, grad_inner)
    for k in range(2):
        put_grad(10 + k, ffn_in_total[:, k * 512 : (k + 1) * 512])
    ffn_in_bias_grad[...] = column_sum(grad_inner.astype(F32))
    up_two = grad_third + dot_nt(grad_inner, ffn_in[...])
    ln_gain_grad[1:2, :] = column_sum(up_two * second_unit)
    ln_bias_grad[1:2, :] = column_sum(up_two)
    grad_second = norm_back(up_two, ln_gain[1:2], second_unit, second_inv)
    grad_cross_out = grad_second.astype(BF)
    put_grad(7, dot_tn(mix[1], grad_cross_out))
    up[...] = dot_nt(grad_cross_out, attn_out[1]).astype(BF)
    pair_sum[...] = jnp.zeros_like(pair_sum)
    for copy in fetches[6:]:
        copy.wait()

    def cross_back(t, carry):
        @pl.when(t + 1 < tables)
        def _():
            fetch_memory(t + 1).start()

        rows = pl.ds(pl.multiple_of(t * slots, slots), slots)
        for g in range(2):
            lanes = slice(g * half, (g + 1) * half)
            value_lanes = slice(512 + g * half, 512 + (g + 1) * half)
            query = by_head(cross_q[rows, lanes], wide_f32)
            upstream = by_head(up[rows, lanes], wide_f32)
            grad_q[rows, lanes], grad_kv[:, lanes], grad_kv[:, value_lanes] = attend_back(
                query, cross_kv[t, :, lanes], cross_kv[t, :, value_lanes], cross_shares[t, g], upstream
            )
        @pl.when(t >= 2)
        def _():
            put_tokens(t - 2).wait()

        slot = lax.rem(t, 2)
        staged[slot] = (
            dot_nt(grad_kv[:, 0:512], attn_in[4]) + dot_nt(grad_kv[:, 512:1024], attn_in[5])
        ).astype(BF)
        put_tokens(t).start()
        fetch_memory(t).wait()
        pair_sum[...] += dot_tn(memory[slot], grad_kv[...])
        return carry

    lax.fori_loop(0, tables, cross_back, 0)
    for t in range(max(tables - 2, 0), tables):
        put_tokens(t).wait()
    for k in range(2):
        put_grad(4 + k, pair_sum[:, k * 512 : (k + 1) * 512])
    put_grad(3, dot_tn(first_low, grad_q[...]))
    up_one = grad_second + dot_nt(grad_q[...], attn_in[3])
    ln_gain_grad[0:1, :] = column_sum(up_one * first_unit)
    ln_bias_grad[0:1, :] = column_sum(up_one)
    grad_first = norm_back(up_one, ln_gain[0:1], first_unit, first_inv)
    grad_self_out = grad_first.astype(BF)
    put_grad(6, dot_tn(mix[0], grad_self_out))
    up[...] = dot_nt(grad_self_out, attn_out[0]).astype(BF)

    def self_back(t, carry):
        rows = pl.ds(pl.multiple_of(t * slots, slots), slots)
        for g in range(2):
            lanes = slice(g * half, (g + 1) * half)
            query = by_head(qkv[0, rows, lanes], wide_f32)
            upstream = by_head(up[rows, lanes], wide_f32)
            grad_qkv[0, rows, lanes], grad_qkv[1, rows, lanes], grad_qkv[2, rows, lanes] = attend_back(
                query, qkv[1, rows, lanes], qkv[2, rows, lanes], self_shares[t, g], upstream
            )
        return carry

    lax.fori_loop(0, tables, self_back, 0)
    total = grad_first
    for k in range(3):
        put_grad(k, dot_tn(tags[...], grad_qkv[k]))
        total = total + dot_nt(grad_qkv[k], attn_in[k])
    tags_grad[...] = total
    for copy in puts:
        copy.wait()


def decoder(
    kept, tags, cotangent, memory, cross_kv, attn_in, attn_out, ln_gain, ln_bias,
    ffn_in, ffn_in_bias, ffn_out, ffn_out_bias,
):
    tables, cells, model = memory.shape
    rows = tags.shape[0]
    slots = rows // tables
    inner = ffn_in.shape[1]
    here = pl.BlockSpec(memory_space=pltpu.VMEM)
    far = pl.BlockSpec(memory_space=pl.ANY)
    shape = jax.ShapeDtypeStruct
    stacked = GROUP * slots
    return pl.pallas_call(
        decoder_kernel,
        in_specs=[here] * 4 + [far] * 13,
        out_specs=[here] * 2 + [far] * 2 + [here] * 4,
        out_shape=[
            shape((rows, model), BF), shape((rows, model), F32), shape((tables, cells, model), BF),
            shape((12, 512, model), BF), shape((3, model), F32), shape((3, model), F32),
            shape((1, inner), F32), shape((1, model), F32),
        ],
        scratch_shapes=[
            pltpu.VMEM((rows, model), BF),
            pltpu.VMEM((rows, model), BF),
            pltpu.VMEM((2, cells, model), BF),
            pltpu.VMEM((tables, cells, 2 * model), BF),
            pltpu.VMEM(attn_in.shape, BF),
            pltpu.VMEM(attn_out.shape, BF),
            pltpu.VMEM(ffn_in.shape, BF),
            pltpu.VMEM(ffn_out.shape, BF),
            pltpu.VMEM((3, rows, model), BF),
            pltpu.VMEM((2, rows, model), BF),
            pltpu.VMEM((tables, 2, slots, stacked), BF),
            pltpu.VMEM((rows, model), F32),
            pltpu.VMEM((tables, 2, cells, stacked), BF),
            pltpu.VMEM((rows, model), BF),
            pltpu.VMEM((rows, model), BF),
            pltpu.VMEM((3, rows, model), BF),
            pltpu.VMEM((rows, model), BF),
            pltpu.VMEM((cells, 2 * model), BF),
            pltpu.VMEM((model, 2 * model), F32),
            pltpu.VMEM((2, cells, model), BF),
            pltpu.SemaphoreType.DMA((11,)),
            pltpu.SemaphoreType.DMA((tables,)),
            pltpu.SemaphoreType.DMA((2,)),
            pltpu.SemaphoreType.DMA((2,)),
            pltpu.VMEM((12, 512, model), BF),
            pltpu.SemaphoreType.DMA((12,)),
        ],
        compiler_params=pltpu.CompilerParams(vmem_limit_bytes=60 * MIB),
        name="decoder",
    )(
        ln_gain, ln_bias, ffn_in_bias, ffn_out_bias, *kept,
        tags, cotangent, memory, cross_kv, attn_in, attn_out, ffn_in, ffn_out,
    )


def widen_kernel(
    small, total, back, conv, proj, attn_in, attn_out, ffn_in, ffn_out, image_grad,
    bn_scale, bn_shift, proj_bias, gain, bias, ffn_in_bias, ffn_out_bias,
    narrow, wide, narrow_image, wide_image, in_sem, out_sem, image_in, image_out,
):
    units = in_sem.shape[0]
    batches, group = back.shape[0], back.shape[1]

    def rows(i):
        return pl.ds(i * 512, 512)

    fetches = [
        pltpu.make_async_copy(total.at[rows(i)], narrow.at[rows(i)], in_sem.at[i]) for i in range(units)
    ]
    images = [(b, g) for b in range(batches) for g in range(group)]
    image_fetches = [
        pltpu.make_async_copy(back.at[b, g], narrow_image.at[i], image_in.at[i])
        for i, (b, g) in enumerate(images)
    ]
    for copy in fetches + image_fetches:
        copy.start()
    bn_scale[...] = small[0:2, 0:256]
    bn_shift[...] = small[0:2, 256:512]
    proj_bias[...] = small[2:3, :]
    ffn_out_bias[...] = small[3:4, :]
    ffn_in_bias[:, 0:512] = small[4:5, :]
    ffn_in_bias[:, 512:1024] = small[5:6, :]
    gain[...] = small[8:11, :]
    bias[...] = small[11:14, :]
    slots = wide.shape[0]
    targets = [attn_in.at[i] for i in range(6)] + [attn_out.at[i] for i in range(2)]
    targets += [ffn_out.at[rows(i)] for i in range(2)]
    targets += [ffn_in.at[:, pl.ds(i * 512, 512)] for i in range(2)]
    pending = []

    def put(i, pairs):
        copies = [
            pltpu.make_async_copy(source, target, out_sem.at[i % slots, j])
            for j, (source, target) in enumerate(pairs)
        ]
        for copy in copies:
            copy.start()
        pending.append(copies)

    for i in range(units):
        fetches[i].wait()
        if i >= slots:
            for copy in pending[i - slots]:
                copy.wait()
        slot = wide.at[i % slots]
        slot[...] = narrow[rows(i), :].astype(F32)
        if i < 12:
            put(i, [(slot, targets[i])])
            continue
        pairs = []
        for half in range(2):
            tap = 2 * (i - 12) + half
            here = pl.ds(half * 256, 256)
            if tap < 9:
                for layer in range(2):
                    lanes = pl.ds(layer * 256, 256)
                    pairs.append((slot.at[here, lanes], conv.at[layer, tap // 3, tap % 3]))
            else:
                pairs.append((slot.at[here], proj))
        put(i, pairs)
    waits = []
    for b in range(batches):
        for g in range(group):
            image_fetches[b * group + g].wait()
            for r in range(back.shape[2] // WIDE):
                line = narrow_image[b * group + g, r * WIDE : (r + 1) * WIDE, :].astype(F32)
                for h in range(2):
                    lanes = slice(h * 128, (h + 1) * 128)
                    wide_image[b, h, pl.ds(r * 28 * group + g, 28, stride=group), :] = line[0:28, lanes]
        for h in range(2):
            waits.append(pltpu.make_async_copy(
                wide_image.at[b, h, pl.ds(0, image_grad.shape[1])],
                image_grad.at[b, :, pl.ds(h * 128, 128)], image_out.at[b, h],
            ))
            waits[-1].start()
    for copies in pending[-slots:] + [waits]:
        for copy in copies:
            copy.wait()


def widen(small, total, back, image_shape, width, model, inner):
    rows = total.shape[0]
    units = rows // 512
    batches, group = back.shape[:2]
    far = pl.BlockSpec(memory_space=pl.ANY)
    near = pl.BlockSpec(memory_space=pltpu.VMEM)
    sem = pltpu.SemaphoreType.DMA
    shapes = [
        (2, 3, 3, width, width), (width, model), (6, model, model), (2, model, model),
        (model, inner), (inner, model), image_shape,
    ]
    small_shapes = [(2, width)] * 2 + [(1, model), (3, model), (3, model), (1, inner), (1, model)]
    return pl.pallas_call(
        widen_kernel,
        in_specs=[near] + [far] * 2,
        out_specs=[far] * 7 + [near] * 7,
        out_shape=[jax.ShapeDtypeStruct(s, F32) for s in shapes + small_shapes],
        scratch_shapes=[
            pltpu.VMEM((rows, model), BF),
            pltpu.VMEM((4, 512, model), F32),
            pltpu.VMEM((batches * group,) + back.shape[2:], BF),
            pltpu.VMEM((batches, 2, image_shape[1] + 8 * group, 128), F32),
            sem((units,)), sem((4, 4)), sem((batches * group,)), sem((batches, 2)),
        ],
        compiler_params=pltpu.CompilerParams(vmem_limit_bytes=60 * MIB),
        name="widen",
    )(small, total, back)


def body(
    image, tags, tag_lengths, cotangent, conv_weight, bn_mean, bn_var, bn_scale, bn_shift,
    proj_weight, proj_bias, attn_in, attn_out, ln_gain, ln_bias,
    ffn_in, ffn_in_bias, ffn_out, ffn_out_bias,
):
    batches, owned, slots, model = tags.shape
    width = image.shape[-1]
    tables = batches * owned
    row = lax.axis_size("row")
    group, part, breadth = image.shape[1:4]
    flat_image = image.transpose(0, 2, 3, 1, 4).reshape(batches, part * breadth * group, width)
    weight = conv_weight.reshape(2, 9 * width, width)
    forward = block_forward(
        flat_image, tag_lengths, tags.reshape(-1, model), attn_out, ln_gain, ln_bias,
        weight, bn_mean, bn_var, bn_scale, bn_shift,
        proj_weight, proj_bias.reshape(1, -1), attn_in, row, group, part,
    )
    padded, hidden, block_out, slope_one, slope_two, norm_one, norm_two, memory, cross_kv = forward[:9]
    decoded, tags_grad, grad_tokens, decoder_g, gain_g, bias_g, ffn_in_bias_g, ffn_out_bias_g = decoder(
        forward[9:], tags.reshape(-1, model), cotangent.reshape(-1, model),
        memory, cross_kv, attn_in, attn_out, ln_gain, ln_bias,
        ffn_in, ffn_in_bias.reshape(1, -1), ffn_out, ffn_out_bias.reshape(1, -1),
    )
    total, small, back = block_backward(
        grad_tokens, padded, hidden, block_out, slope_one, slope_two, norm_one, norm_two,
        weight, bn_var, bn_scale, proj_weight, decoder_g.reshape(-1, model),
        (gain_g, bias_g, ffn_in_bias_g, ffn_out_bias_g), lax.axis_size("dp"), row, batches,
    )
    (
        conv_g, proj_g, attn_in_g, attn_out_g, ffn_in_g, ffn_out_g, image_g,
        bn_scale_g, bn_shift_g, proj_bias_g, gain_g, bias_g, ffn_in_bias_g, ffn_out_bias_g,
    ) = widen(small, total, back, flat_image.shape, width, model, ffn_in.shape[1])
    image_g = image_g.reshape(batches, part, breadth, group, width).transpose(0, 3, 1, 2, 4)
    return (
        decoded.reshape(tags.shape), image_g, tags_grad.reshape(tags.shape),
        conv_g, bn_scale_g, bn_shift_g, proj_g, proj_bias_g.reshape(-1),
        attn_in_g, attn_out_g, gain_g, bias_g,
        ffn_in_g, ffn_in_bias_g.reshape(-1), ffn_out_g, ffn_out_bias_g.reshape(-1),
    )


def solution(mesh):
    by_rows = P(None, "dp", "row", None, None)
    by_table = P(None, ("dp", "row"), None, None)
    return jax.shard_map(
        body,
        mesh=mesh,
        in_specs=(by_rows, by_table, P(None, ("dp", "row")), by_table) + (P(),) * 15,
        out_specs=(by_table, by_rows, by_table) + (P(),) * 13,
        check_vma=False,
    )
```
